32 devices in a mesh: lat: 4 (over z), lon: 8 (over y, x, core).
Axes of the slice: x: 2, y: 2, z: 4, core: 2. Of those that a mesh axis runs over, the one named last changes fastest.
Arguments:
- satellite_blocks: bfloat16 [4096, 16, 128], P(('lat', 'lon')), may hold values from -6 to 6
- slot_source: int32 [32, 32, 4], P(('lat', 'lon')), may hold values from 0 to 127
- slot_weight: bfloat16 [32, 32, 4, 8, 128], P(('lat', 'lon')), may hold values from -2 to 2
- slot_target: int32 [32, 32, 4], P(('lat', 'lon')), may hold values from 0 to 63
- tile_counts: int32 [32, 32], P(('lat', 'lon')), may hold values from 0 to 4, as said below
- gate_input_weight: bfloat16 [128, 144], replicated, may hold values from -0.5 to 0.5
- gate_state_weight: bfloat16 [128, 288], replicated, may hold values from -0.375 to 0.375
- gate_bias: float32 [128], replicated, may hold values from -4 to 4
- hidden_init: bfloat16 [32, 128, 2048], P(None, 'lat', 'lon'), may hold values from -1 to 1
- cell_init: bfloat16 [32, 128, 2048], P(None, 'lat', 'lon'), may hold values from -6 to 6
Outputs:
- hidden_out: bfloat16 [32, 128, 2048], P(None, 'lat', 'lon')
- cell_out: bfloat16 [32, 128, 2048], P(None, 'lat', 'lon')
The draws below stay inside these ranges and needn't reach their ends.
Inputs may be any that keep to these rules, and one draw needn't show every extreme that they name: slot_source[p, q, s] names one of the 128 blocks held by source device p. slot_target[q, p, s] is the cell block of tile q fed by slot s from device p. Only slots s < tile_counts[q, p] carry data from device p to tile q; at least one tile receives 4 blocks from every source device.
All inputs are finite; a program needn't handle non-finite values.
Results may differ from the reference program's by a relative error of at most 0.0069.
Values may be sent and summed in bfloat16 or wider, within the bound.
No kernel may reach another device: no remote copies, remote signals or barrier semaphores. Data moves between devices by JAX's collectives and lax.ppermute only.
A program may use at most 128 MiB of HBM per device.

```python
import jax
import jax.numpy as jnp
from jax import lax

CH = 16
HID = 32
GATES = 128
BLOCK = 128
BAND = 8
CAP = 4
STEPS = 3
TLAT = 32
TLON = 256
SB_DEV = 128
DB_DEV = 64
NLAT = 128
NLON = 2048
SRC = 4096
N_LAT = 4
N_LON = 8
DEVICES = 32


def draw_tile_counts(key, part):
    key_first, key_second, key_third = jax.random.split(key, 3)
    first = jax.random.randint(key_first, (DEVICES, DEVICES), 0, CAP + 1)
    second = jax.random.randint(key_second, (DEVICES, DEVICES), 0, CAP + 1)
    hottest = jax.random.randint(key_third, (), 0, DEVICES)
    tiles = jnp.arange(DEVICES, dtype=jnp.int32)[:, None]
    base = jnp.minimum(first, second)
    return jnp.where(tiles == hottest, CAP, base).astype(jnp.int32)


def with_ends(drawn, rng, low, high):
    shape = drawn.shape
    spot = [jax.random.randint(jax.random.fold_in(rng, axis), (), 0, shape[axis]) for axis in range(len(shape))]
    drawn = drawn.at[tuple(spot)].set(low)
    longest = shape.index(max(shape))
    spot[longest] = (spot[longest] + 1) % shape[longest]
    return drawn.at[tuple(spot)].set(high)


def levels(rng, extent, cuts, least, top_value):
    def one(dim, shards_of):
        heights = jax.random.uniform(jax.random.fold_in(jax.random.fold_in(rng, 6), dim), (shards_of,), jnp.float32, least / len(cuts), top_value / len(cuts))
        return jnp.repeat(jnp.exp(heights), extent[dim] // shards_of).reshape((-1,) + (1,) * (len(extent) - dim - 1))

    level = one(*cuts[0])
    for cut in cuts[1:]:
        level = level * one(*cut)
    return level


def noise(stream_key, dims, spread, most, cuts=(), kind=jnp.bfloat16):
    loudness = levels(stream_key, dims, cuts, -0.22, 0.18) if cuts else 1.0
    values = jax.random.normal(stream_key, dims, jnp.float32) * spread * loudness
    return jnp.minimum(jnp.maximum(values, -most), most).astype(kind)


def setup_inputs(seed: int = 0) -> dict:
    seeds = jax.random.split(jax.random.key(seed), 11)
    return {
        "satellite_blocks": noise(seeds[0], (SRC, CH, BLOCK), 1.0, 6.0, ((0, 32),)),
        "slot_source": with_ends(jax.random.randint(seeds[1], (DEVICES, DEVICES, CAP), 0, SB_DEV), jax.random.fold_in(seeds[1], 1), 0, SB_DEV - 1).astype(jnp.int32),
        "slot_weight": noise(seeds[2], (DEVICES, DEVICES, CAP, BAND, BLOCK), BAND ** -0.5, 2.0, ((0, 32),)),
        "slot_target": with_ends(jax.random.randint(seeds[3], (DEVICES, DEVICES, CAP), 0, DB_DEV), jax.random.fold_in(seeds[3], 1), 0, DB_DEV - 1).astype(jnp.int32),
        "tile_counts": draw_tile_counts(jax.random.fold_in(seeds[10], 71), 0),
        "gate_input_weight": noise(seeds[5], (GATES, 9 * CH), (9 * CH) ** -0.5, 0.5),
        "gate_state_weight": noise(seeds[6], (GATES, 9 * HID), (9 * HID) ** -0.5, 0.375),
        "gate_bias": noise(seeds[7], (GATES,), 1.0, 4.0, (), jnp.float32),
        "hidden_init": jnp.clip(jax.random.uniform(seeds[8], (HID, NLAT, NLON), jnp.float32, -1.0, 1.0) * levels(seeds[8], (HID, NLAT, NLON), ((1, 4), (2, 8)), -0.4, 0.0), -1.0, 1.0).astype(jnp.bfloat16),
        "cell_init": noise(seeds[9], (HID, NLAT, NLON), 1.0, 6.0, ((1, 4), (2, 8))),
    }


def band_apply(picked, weights):
    band_size = weights.shape[-2]
    margin_left = band_size // 2
    values = picked.astype(jnp.float32)
    padded = jnp.pad(values, ((0, 0), (0, 0), (0, 0), (margin_left, band_size - 1 - margin_left)))
    summed = jnp.zeros(values.shape, jnp.float32)
    for offset in range(band_size):
        factor = weights[:, :, offset, :].astype(jnp.float32)[:, :, None, :]
        summed = summed + factor * padded[..., offset:offset + values.shape[-1]]
    return summed.astype(jnp.bfloat16)


def convolve(padded, weights, row_count, column_count):
    shifted_list = [padded[:, row_shift:row_shift + row_count, column_shift:column_shift + column_count]
                    for row_shift in range(3) for column_shift in range(3)]
    stacked = jnp.concatenate(shifted_list, axis=0)
    flattened = stacked.reshape(stacked.shape[0], row_count * column_count)
    result = jnp.dot(weights, flattened, preferred_element_type=jnp.float32)
    return result.reshape(weights.shape[0], row_count, column_count)


def cell_update(gates, memory):
    hidden_units = gates.shape[0] // 4
    ingate = jax.nn.sigmoid(gates[:hidden_units])
    forget = jax.nn.sigmoid(gates[hidden_units:2 * hidden_units])
    outgate = jax.nn.sigmoid(gates[2 * hidden_units:3 * hidden_units])
    candidate = jnp.tanh(gates[3 * hidden_units:])
    memory = forget * memory + ingate * candidate
    hidden = (outgate * jnp.tanh(memory)).astype(jnp.bfloat16)
    return hidden, memory


def wrap_pad(field):
    widened = jnp.pad(field, ((0, 0), (0, 0), (1, 1)), mode="wrap")
    return jnp.pad(widened, ((0, 0), (1, 1), (0, 0)))


def reference(satellite_blocks, slot_source, slot_weight, slot_target, tile_counts,
              gate_input_weight, gate_state_weight, gate_bias, hidden_init, cell_init):
    def one_source(totals, source_index):
        blocks = lax.dynamic_slice_in_dim(satellite_blocks, source_index * SB_DEV, SB_DEV, 0)
        picked = jnp.take(blocks, slot_source[source_index], axis=0)
        contribution = band_apply(picked, slot_weight[source_index]).astype(jnp.float32)
        live_slot = jnp.arange(CAP, dtype=jnp.int32)[None, :] < tile_counts[:, source_index][:, None]
        contribution = jnp.where(live_slot[:, :, None, None], contribution, jnp.zeros_like(contribution))
        tiles = jnp.broadcast_to(jnp.arange(DEVICES, dtype=jnp.int32)[:, None], (DEVICES, CAP))
        totals = totals.at[tiles, slot_target[:, source_index, :]].add(contribution)
        return totals, None

    start_totals = jnp.zeros((DEVICES, DB_DEV, CH, BLOCK), jnp.float32)
    totals, _ = lax.scan(one_source, start_totals, jnp.arange(DEVICES, dtype=jnp.int32))
    forcing_blocks = totals.astype(jnp.bfloat16)
    forcing = forcing_blocks.transpose(0, 2, 1, 3).reshape(N_LAT, N_LON, CH, TLAT, TLON)
    forcing = forcing.transpose(2, 0, 3, 1, 4).reshape(CH, NLAT, NLON)

    forcing_padded = wrap_pad(forcing)
    hidden = hidden_init
    memory = cell_init.astype(jnp.float32)
    for update_index in range(STEPS):
        hidden_padded = wrap_pad(hidden)

        def one_band(band_index):
            start = band_index * TLAT
            forcing_slab = lax.dynamic_slice_in_dim(forcing_padded, start, TLAT + 2, 1)
            hidden_slab = lax.dynamic_slice_in_dim(hidden_padded, start, TLAT + 2, 1)
            memory_slab = lax.dynamic_slice_in_dim(memory, start, TLAT, 1)
            forcing_gates = convolve(forcing_slab, gate_input_weight, TLAT, NLON) + gate_bias[:, None, None]
            gates = forcing_gates + convolve(hidden_slab, gate_state_weight, TLAT, NLON)
            return cell_update(gates, memory_slab)

        band_hidden, band_memory = lax.map(one_band, jnp.arange(N_LAT, dtype=jnp.int32))
        hidden = band_hidden.transpose(1, 0, 2, 3).reshape(HID, NLAT, NLON)
        memory = band_memory.transpose(1, 0, 2, 3).reshape(HID, NLAT, NLON)
    return hidden, memory.astype(jnp.bfloat16)
```

```python
import functools

import jax
import jax.numpy as jnp
from jax import lax
from jax.experimental import pallas as pl
from jax.experimental.pallas import tpu as pltpu
from jax.sharding import PartitionSpec as P

STEPS = 3
PAD = 4
LANES = 128
STRIP = 3 * LANES
BF = jnp.bfloat16
F32 = jnp.float32


def lane_of(shape):
    return lax.broadcasted_iota(jnp.int32, shape, len(shape) - 1)


def whole(count):
    return [pl.BlockSpec(memory_space=pltpu.VMEM)] * count


def scalars(count):
    return [pl.BlockSpec(memory_space=pltpu.SMEM)] * count


def call(kernel, outs, ins, scalar_count, scratch, name, flops, args):
    nbytes = sum(a.size * a.dtype.itemsize for a in list(args) + list(outs))
    return pl.pallas_call(
        kernel,
        out_shape=tuple(outs),
        in_specs=scalars(scalar_count) + whole(ins),
        out_specs=tuple(whole(len(outs))),
        scratch_shapes=scratch,
        compiler_params=pltpu.CompilerParams(vmem_limit_bytes=40 * 2**20),
        cost_estimate=pl.CostEstimate(flops=flops, bytes_accessed=nbytes, transcendentals=0),
        name=name,
    )(*args)


def edge_tiles(row_of, row_count, channels):
    lane = lane_of((channels, LANES))
    tiles = [jnp.zeros((channels, LANES), BF) for _ in range(STRIP // LANES)]
    for y in range(row_count):
        row = row_of(y)
        both = jnp.where(lane < 64, row[:, :LANES], row[:, -LANES:])
        r = y + PAD
        place = r % 16
        turned = pltpu.roll(both, (8 * place + 4) % LANES, axis=1)
        tiles[r // 16] = jnp.where(lane // 8 == place, turned, tiles[r // 16])
    return tiles


def gather_kernel(source_ref, blocks_ref, weight_ref, out_ref):
    slots, band, width = weight_ref.shape
    channels = blocks_ref.shape[1]
    offset = lax.broadcasted_iota(jnp.int32, (band, width), 0) - band // 2
    spot = lane_of((band, width)) + offset
    inside = (spot >= 0) & (spot < width)

    def one(slot, carry):
        block = blocks_ref[source_ref[slot]]
        factor = jnp.where(inside, weight_ref[slot].astype(F32), 0.0)
        total = jnp.zeros((channels, width), F32)
        for k in range(band):
            moved = block if k == band // 2 else pltpu.roll(block, (band // 2 - k) % width, axis=1)
            total = total + factor[k : k + 1, :] * moved.astype(F32)
        out_ref[slot] = total.astype(BF)
        return carry

    lax.fori_loop(0, slots, one, 0, unroll=8)


def prepare_kernel(hidden_ref, cell_ref, rows_ref, edge_ref):
    units = hidden_ref.shape[0]
    row_count = hidden_ref.shape[1]
    rows_ref[:, :units, :] = jnp.swapaxes(hidden_ref[...], 0, 1)
    rows_ref[:, units:, :] = jnp.swapaxes(cell_ref[...], 0, 1)
    tiles = edge_tiles(lambda y: rows_ref[y], row_count, 2 * units)
    for t, tile in enumerate(tiles):
        edge_ref[:, t * LANES : (t + 1) * LANES] = tile


def strips_kernel(rows_ref, edge_ref, left_ref, right_ref, strip_ref, up_ref, down_ref):
    channels = edge_ref.shape[0]
    near = lane_of((channels, STRIP)) % 8 < 4
    left = jnp.where(near, left_ref[...], edge_ref[...])
    right = jnp.where(near, edge_ref[...], right_ref[...])
    strip_ref[:, :STRIP] = left
    strip_ref[:, STRIP:] = right
    rows = rows_ref.shape[0]
    up_ref[:3] = rows_ref[:3]
    up_ref[3, :, :LANES] = left[:, :LANES]
    up_ref[3, :, LANES:] = right[:, :LANES]
    down_ref[:3] = rows_ref[rows - 3 :]
    down_ref[3, :, :LANES] = left[:, 2 * LANES :]
    down_ref[3, :, LANES:] = right[:, 2 * LANES :]


def full_strip(strip, above, below, has_above, has_below):
    lane = lane_of(above[:, :LANES].shape)
    from_above = (lane >= 8) & (lane < 32)
    from_below = (lane >= 32) & (lane < 56)
    parts = []
    for side in range(2):
        base = side * STRIP
        theirs = above[:, side * LANES : (side + 1) * LANES] * has_above
        parts.append(jnp.where(from_above, theirs, strip[:, base : base + LANES]))
        parts.append(strip[:, base + LANES : base + 2 * LANES])
        theirs = below[:, side * LANES : (side + 1) * LANES] * has_below
        parts.append(jnp.where(from_below, theirs, strip[:, base + 2 * LANES : base + STRIP]))
    return jnp.concatenate(parts, axis=1)


def strip_taps(strip):
    width = strip.shape[1]
    taps = []
    for a in range(3):
        for e in range(3):
            shift = 8 * (a - 1) + e - 1
            taps.append(strip if shift == 0 else pltpu.roll(strip, -shift % width, axis=1))
    return jnp.concatenate(taps, axis=0)


def store_patches(strip, patch_ref, first, last):
    channels = strip.shape[0]
    near = lane_of((channels, LANES)) % 8 < 4
    for t in range(STRIP // LANES):
        left = strip[:, t * LANES : (t + 1) * LANES]
        right = strip[:, STRIP + t * LANES : STRIP + (t + 1) * LANES]
        mixed = jnp.where(near, left, right)
        for r in range(max(first, 16 * t), min(last, 16 * t + 16)):
            patch_ref[r] = pltpu.roll(mixed, -(8 * (r % 16) + 4) % LANES, axis=1)


def store_three(ref, r, row, patch):
    channels = row.shape[0]
    lane = lane_of((channels, LANES))
    head, tail = row[:, :LANES], row[:, LANES:]
    ref[r, :channels, :LANES] = pltpu.roll(jnp.where(lane == LANES - 1, patch, head), 1, axis=1)
    ref[r, :channels, LANES:] = pltpu.roll(jnp.where(lane == LANES - 1, head, tail), 1, axis=1)
    ref[r, channels : 2 * channels, :] = row
    ref[r, 2 * channels :, :LANES] = pltpu.roll(jnp.where(lane == 0, tail, head), LANES - 1, axis=1)
    ref[r, 2 * channels :, LANES:] = pltpu.roll(jnp.where(lane == 0, patch, tail), LANES - 1, axis=1)


def row_taps(ref, r):
    channels = ref.shape[1]
    return ref[pl.ds(r - 1, 3)].reshape(3 * channels, ref.shape[2])


def matmul(weights, taps):
    return jnp.dot(weights, taps, preferred_element_type=F32)


def state_kernel(
    flag_ref, rows_ref, strip_ref, above_ref, below_ref, weight_ref,
    gates_ref, strip_gates_ref, cell_strip_ref, three, patches,
):
    units = rows_ref.shape[1] // 2
    count = rows_ref.shape[0]
    has_above = flag_ref[0].astype(F32).astype(BF)
    has_below = flag_ref[1].astype(F32).astype(BF)
    strip = full_strip(strip_ref[...], above_ref[3], below_ref[3], has_above, has_below)
    cell_strip_ref[...] = strip[units:]
    strip = strip[:units]
    strip_gates_ref[...] = matmul(weight_ref[...], strip_taps(strip))
    store_patches(strip, patches, 1, count + 7)
    for i in range(3):
        store_three(three, 1 + i, above_ref[i, :units] * has_above, patches[1 + i])
        r = count + PAD + i
        store_three(three, r, below_ref[i, :units] * has_below, patches[r])

    def fill(y, carry):
        store_three(three, y + PAD, rows_ref[y, :units], patches[y + PAD])
        return carry

    lax.fori_loop(0, count, fill, 0, unroll=4)

    def one(i, carry):
        gates_ref[i] = matmul(weight_ref[...], row_taps(three, i + 2))
        return carry

    lax.fori_loop(0, count + 4, one, 0, unroll=4)


def update(gates, memory):
    units = memory.shape[0]
    ingate = 0.5 * jnp.tanh(gates[:units]) + 0.5
    forget = 0.5 * jnp.tanh(gates[units : 2 * units]) + 0.5
    outgate = 0.5 * jnp.tanh(gates[2 * units : 3 * units]) + 0.5
    memory = forget * memory + ingate * jnp.tanh(gates[3 * units :])
    return outgate * jnp.tanh(memory), memory


def window_kernel(
    flag_ref, gates_ref, strip_gates_ref, rows_ref, above_ref, below_ref, cell_strip_ref,
    forcing_ref, forcing_strip_ref, f_above_ref, f_below_ref, in_weight_ref, weight_ref, bias_ref,
    hidden_ref, cell_ref,
    f_three, f_patches, f_gates, first, second, patches, memory, h_rows, c_rows,
):
    units = rows_ref.shape[1] // 2
    count = rows_ref.shape[0]
    has_above = flag_ref[0].astype(F32)
    has_below = flag_ref[1].astype(F32)
    bf_above, bf_below = has_above.astype(BF), has_below.astype(BF)
    bias = jnp.broadcast_to(bias_ref[...], (bias_ref.shape[0], 2 * LANES))

    strip = full_strip(forcing_strip_ref[...], f_above_ref[3], f_below_ref[3], bf_above, bf_below)
    strip_forcing = matmul(in_weight_ref[...], strip_taps(strip)) + bias_ref[...]
    store_patches(strip, f_patches, 1, count + 7)
    for i in range(3):
        store_three(f_three, 1 + i, f_above_ref[i] * bf_above, f_patches[1 + i])
        r = count + PAD + i
        store_three(f_three, r, f_below_ref[i] * bf_below, f_patches[r])

    def fill(y, carry):
        store_three(f_three, y + PAD, forcing_ref[y], f_patches[y + PAD])
        return carry

    lax.fori_loop(0, count, fill, 0, unroll=4)

    row_of_lane = (lane_of((units, 2 * STRIP)) % STRIP) // 8
    keep = jnp.where(row_of_lane < PAD, has_above, 1.0)
    keep = jnp.where(row_of_lane >= PAD + count, has_below, keep)

    strip_memory = cell_strip_ref[...].astype(F32)
    strip_hidden, strip_memory = update(strip_gates_ref[...] + strip_forcing, strip_memory)
    strip_hidden = (strip_hidden * keep).astype(BF)
    store_patches(strip_hidden, patches, 2, count + 6)

    def scale_of(r):
        scale = jnp.where(r < PAD, has_above, 1.0)
        return jnp.where(r >= PAD + count, has_below, scale)

    def first_row(r, old):
        forcing_gates = matmul(in_weight_ref[...], row_taps(f_three, r)) + bias
        f_gates[r] = forcing_gates
        hidden, new = update(gates_ref[r - 2] + forcing_gates, old)
        memory[r] = new
        store_three(first, r, (hidden * scale_of(r)).astype(BF), patches[r])

    for i in range(2):
        first_row(2 + i, above_ref[1 + i, units:].astype(F32))
        first_row(count + PAD + i, below_ref[i, units:].astype(F32))

    def one(y, carry):
        first_row(y + PAD, rows_ref[y, units:].astype(F32))
        return carry

    lax.fori_loop(0, count, one, 0, unroll=2)

    strip_gates = matmul(weight_ref[...], strip_taps(strip_hidden)) + strip_forcing
    strip_hidden, strip_memory = update(strip_gates, strip_memory)
    strip_hidden = (strip_hidden * keep).astype(BF)
    store_patches(strip_hidden, patches, 3, count + 5)

    def two(i, carry):
        r = i + 3
        gates = f_gates[r] + matmul(weight_ref[...], row_taps(first, r))
        hidden, new = update(gates, memory[r])
        memory[r] = new
        store_three(second, r, (hidden * scale_of(r)).astype(BF), patches[r])
        return carry

    lax.fori_loop(0, count + 2, two, 0, unroll=2)

    def three(y, carry):
        r = y + PAD
        gates = f_gates[r] + matmul(weight_ref[...], row_taps(second, r))
        hidden, new = update(gates, memory[r])
        h_rows[y] = hidden.astype(BF)
        c_rows[y] = new.astype(BF)
        return carry

    lax.fori_loop(0, count, three, 0, unroll=2)
    hidden_ref[...] = jnp.swapaxes(h_rows[...], 0, 1)
    cell_ref[...] = jnp.swapaxes(c_rows[...], 0, 1)


def scatter_kernel(target_ref, count_ref, incoming_ref, rows_ref, edge_ref, total):
    slots, channels, width = incoming_ref.shape
    sources = count_ref.shape[0]
    cap = slots // sources
    row_count = rows_ref.shape[0]
    spare = 2 * row_count
    total[...] = jnp.zeros(total.shape, F32)

    def one(p, carry):
        live = count_ref[p]
        for s in range(cap):
            block = jnp.where(s < live, target_ref[p * cap + s], spare)
            total[block] = total[block] + incoming_ref[p * cap + s].astype(F32)
        return carry

    lax.fori_loop(0, sources, one, 0, unroll=4)
    for y in range(row_count):
        rows_ref[y, :, :width] = total[2 * y].astype(BF)
        rows_ref[y, :, width:] = total[2 * y + 1].astype(BF)
    tiles = edge_tiles(lambda y: rows_ref[y], row_count, channels)
    for t, tile in enumerate(tiles):
        edge_ref[:, t * LANES : (t + 1) * LANES] = tile


def around(count):
    return [(i, (i + 1) % count) for i in range(count)]


def back(count):
    return [((i + 1) % count, i) for i in range(count)]


def exchange_columns(edge):
    count = lax.axis_size("lon")
    from_left = lax.ppermute(edge, "lon", around(count))
    from_right = lax.ppermute(edge, "lon", back(count))
    return from_left, from_right


def exchange_rows(up, down):
    count = lax.axis_size("lat")
    from_above = lax.ppermute(down, "lat", around(count))
    from_below = lax.ppermute(up, "lat", back(count))
    return from_above, from_below


def strips_of(rows, edge, name):
    from_left, from_right = exchange_columns(edge)
    channels = edge.shape[0]
    ends = jax.ShapeDtypeStruct((4, channels, rows.shape[2]), BF)
    strip, up, down = call(
        strips_kernel,
        [jax.ShapeDtypeStruct((channels, 2 * STRIP), BF), ends, ends],
        4, 0, [], name, 1000, (rows, edge, from_left, from_right),
    )
    from_above, from_below = exchange_rows(up, down)
    return strip, from_above, from_below


def on_device(
    satellite_blocks,
    slot_source,
    slot_weight,
    slot_target,
    tile_counts,
    gate_input_weight,
    gate_state_weight,
    gate_bias,
    hidden_init,
    cell_init,
):
    _, tiles, cap, band, block = slot_weight.shape
    channels = satellite_blocks.shape[1]
    units, row_count, column_count = hidden_init.shape
    gates = gate_bias.shape[0]
    slots = tiles * cap
    half = jnp.where(jnp.arange(gates) < 3 * units, 0.5, 1.0)
    in_weight = gate_input_weight * half[:, None].astype(BF)
    state_weight = gate_state_weight * half[:, None].astype(BF)
    bias = (gate_bias * half)[:, None]
    lat = lax.axis_index("lat")
    flags = jnp.stack([lat > 0, lat < lax.axis_size("lat") - 1]).astype(jnp.int32)

    rows, edge = call(
        prepare_kernel,
        [
            jax.ShapeDtypeStruct((row_count, 2 * units, column_count), BF),
            jax.ShapeDtypeStruct((2 * units, STRIP), BF),
        ],
        2, 0, [], "prepare", 1000, (hidden_init, cell_init),
    )
    (outgoing,) = call(
        gather_kernel,
        [jax.ShapeDtypeStruct((slots, channels, block), BF)],
        2, 1, [], "gather_band", 2 * slots * channels * block * band,
        (slot_source.reshape(slots), satellite_blocks, slot_weight.reshape(slots, band, block)),
    )
    incoming = lax.all_to_all(
        outgoing.reshape(tiles, cap, channels, block), ("lat", "lon"), split_axis=0, concat_axis=0, tiled=True
    ).reshape(slots, channels, block)

    strip, above, below = strips_of(rows, edge, "state_strips")
    extended = row_count + 4
    state_gates, strip_gates, cell_strip = call(
        state_kernel,
        [
            jax.ShapeDtypeStruct((extended, gates, column_count), F32),
            jax.ShapeDtypeStruct((gates, 2 * STRIP), F32),
            jax.ShapeDtypeStruct((units, 2 * STRIP), BF),
        ],
        5, 1,
        [
            pltpu.VMEM((row_count + 8, 3 * units, column_count), BF),
            pltpu.VMEM((row_count + 8, units, LANES), BF),
        ],
        "state_gates", 2 * gates * 9 * units * extended * column_count,
        (flags, rows, strip, above, below, state_weight),
    )

    forcing, forcing_edge = call(
        scatter_kernel,
        [
            jax.ShapeDtypeStruct((row_count, channels, column_count), BF),
            jax.ShapeDtypeStruct((channels, STRIP), BF),
        ],
        1, 2,
        [pltpu.VMEM((2 * row_count + 1, channels, block), F32)],
        "scatter_add", slots * channels * block,
        (slot_target.reshape(slots), tile_counts.reshape(tiles), incoming),
    )
    forcing_strip, f_above, f_below = strips_of(forcing, forcing_edge, "forcing_strips")
    out = jax.ShapeDtypeStruct((units, row_count, column_count), BF)
    padded = row_count + 8
    return call(
        window_kernel,
        [out, out],
        13, 1,
        [
            pltpu.VMEM((padded, 3 * channels, column_count), BF),
            pltpu.VMEM((padded, channels, LANES), BF),
            pltpu.VMEM((padded, gates, column_count), F32),
            pltpu.VMEM((padded, 3 * units, column_count), BF),
            pltpu.VMEM((padded, 3 * units, column_count), BF),
            pltpu.VMEM((padded, units, LANES), BF),
            pltpu.VMEM((padded, units, column_count), F32),
            pltpu.VMEM((row_count, units, column_count), BF),
            pltpu.VMEM((row_count, units, column_count), BF),
        ],
        "window", 2 * gates * 9 * (channels + 2 * units) * row_count * column_count,
        (flags, state_gates, strip_gates, rows, above, below, cell_strip,
         forcing, forcing_strip, f_above, f_below, in_weight, state_weight, bias),
    )


def solution(mesh):
    placed = (
        P(("lat", "lon"), None, None),
        P(("lat", "lon"), None, None),
        P(("lat", "lon"), None, None, None, None),
        P(("lat", "lon"), None, None),
        P(("lat", "lon"), None),
        P(),
        P(),
        P(),
        P(None, "lat", "lon"),
        P(None, "lat", "lon"),
    )
    return jax.shard_map(
        on_device,
        mesh=mesh,
        in_specs=placed,
        out_specs=(P(None, "lat", "lon"), P(None, "lat", "lon")),
        check_vma=False,
    )
```

```python
import functools

import jax
import jax.numpy as jnp
from jax import lax
from jax.experimental import pallas as pl
from jax.experimental.pallas import tpu as pltpu
from jax.sharding import PartitionSpec as P

STEPS = 3
PAD = 4
LANES = 128
STRIP = 3 * LANES
BATCH = 2
BF = jnp.bfloat16
F32 = jnp.float32


def lane_of(shape):
    return lax.broadcasted_iota(jnp.int32, shape, len(shape) - 1)


def whole(count):
    return [pl.BlockSpec(memory_space=pltpu.VMEM)] * count


def scalars(count):
    return [pl.BlockSpec(memory_space=pltpu.SMEM)] * count


def call(kernel, outs, ins, scalar_count, scratch, name, flops, args):
    nbytes = sum(a.size * a.dtype.itemsize for a in list(args) + list(outs))
    return pl.pallas_call(
        kernel,
        out_shape=tuple(outs),
        in_specs=scalars(scalar_count) + whole(ins),
        out_specs=tuple(whole(len(outs))),
        scratch_shapes=scratch,
        compiler_params=pltpu.CompilerParams(vmem_limit_bytes=40 * 2**20),
        cost_estimate=pl.CostEstimate(flops=flops, bytes_accessed=nbytes, transcendentals=0),
        name=name,
    )(*args)


def edge_tiles(row_of, row_count, channels):
    lane = lane_of((channels, LANES))
    tiles = [jnp.zeros((channels, LANES), BF) for _ in range(STRIP // LANES)]
    for y in range(row_count):
        row = row_of(y)
        both = jnp.where(lane < 64, row[:, :LANES], row[:, -LANES:])
        r = y + PAD
        place = r % 16
        turned = pltpu.roll(both, (8 * place + 4) % LANES, axis=1)
        tiles[r // 16] = jnp.where(lane // 8 == place, turned, tiles[r // 16])
    return tiles


def gather_kernel(source_ref, blocks_ref, weight_ref, out_ref):
    slots, band, width = weight_ref.shape
    channels = blocks_ref.shape[1]
    offset = lax.broadcasted_iota(jnp.int32, (band, width), 0) - band // 2
    spot = lane_of((band, width)) + offset
    inside = (spot >= 0) & (spot < width)

    for slot in range(slots):
        block = blocks_ref[source_ref[slot]]
        factor = jnp.where(inside, weight_ref[slot].astype(F32), 0.0)
        total = jnp.zeros((channels, width), F32)
        for k in range(band):
            moved = block if k == band // 2 else pltpu.roll(block, (band // 2 - k) % width, axis=1)
            total = total + factor[k : k + 1, :] * moved.astype(F32)
        out_ref[slot] = total.astype(BF)


def prepare_kernel(hidden_ref, cell_ref, rows_ref, edge_ref):
    units = hidden_ref.shape[0]
    row_count = hidden_ref.shape[1]
    rows_ref[:, :units, :] = jnp.swapaxes(hidden_ref[...], 0, 1)
    rows_ref[:, units:, :] = jnp.swapaxes(cell_ref[...], 0, 1)
    tiles = edge_tiles(lambda y: rows_ref[y], row_count, 2 * units)
    for t, tile in enumerate(tiles):
        edge_ref[:, t * LANES : (t + 1) * LANES] = tile


def strips_kernel(rows_ref, edge_ref, left_ref, right_ref, strip_ref, up_ref, down_ref):
    channels = edge_ref.shape[0]
    near = lane_of((channels, STRIP)) % 8 < 4
    left = jnp.where(near, left_ref[...], edge_ref[...])
    right = jnp.where(near, edge_ref[...], right_ref[...])
    strip_ref[:, :STRIP] = left
    strip_ref[:, STRIP:] = right
    rows = rows_ref.shape[0]
    up_ref[:3] = rows_ref[:3]
    up_ref[3, :, :LANES] = left[:, :LANES]
    up_ref[3, :, LANES:] = right[:, :LANES]
    down_ref[:3] = rows_ref[rows - 3 :]
    down_ref[3, :, :LANES] = left[:, 2 * LANES :]
    down_ref[3, :, LANES:] = right[:, 2 * LANES :]


def full_strip(strip, above, below, has_above, has_below):
    lane = lane_of(above[:, :LANES].shape)
    from_above = (lane >= 8) & (lane < 32)
    from_below = (lane >= 32) & (lane < 56)
    parts = []
    for side in range(2):
        base = side * STRIP
        theirs = above[:, side * LANES : (side + 1) * LANES] * has_above
        parts.append(jnp.where(from_above, theirs, strip[:, base : base + LANES]))
        parts.append(strip[:, base + LANES : base + 2 * LANES])
        theirs = below[:, side * LANES : (side + 1) * LANES] * has_below
        parts.append(jnp.where(from_below, theirs, strip[:, base + 2 * LANES : base + STRIP]))
    return jnp.concatenate(parts, axis=1)


def strip_taps(strip):
    width = strip.shape[1]
    taps = []
    for a in range(3):
        for e in range(3):
            shift = 8 * (a - 1) + e - 1
            taps.append(strip if shift == 0 else pltpu.roll(strip, -shift % width, axis=1))
    return jnp.concatenate(taps, axis=0)


def store_patches(strip, patch_ref, first, last):
    channels = strip.shape[0]
    near = lane_of((channels, LANES)) % 8 < 4
    for t in range(STRIP // LANES):
        left = strip[:, t * LANES : (t + 1) * LANES]
        right = strip[:, STRIP + t * LANES : STRIP + (t + 1) * LANES]
        mixed = jnp.where(near, left, right)
        for r in range(max(first, 16 * t), min(last, 16 * t + 16)):
            patch_ref[r] = pltpu.roll(mixed, -(8 * (r % 16) + 4) % LANES, axis=1)


def store_three(ref, r, row, patch):
    channels = row.shape[0]
    lane = lane_of((channels, LANES))
    head, tail = row[:, :LANES], row[:, LANES:]
    ref[r, :channels, :LANES] = pltpu.roll(jnp.where(lane == LANES - 1, patch, head), 1, axis=1)
    ref[r, :channels, LANES:] = pltpu.roll(jnp.where(lane == LANES - 1, head, tail), 1, axis=1)
    ref[r, channels : 2 * channels, :] = row
    ref[r, 2 * channels :, :LANES] = pltpu.roll(jnp.where(lane == 0, tail, head), LANES - 1, axis=1)
    ref[r, 2 * channels :, LANES:] = pltpu.roll(jnp.where(lane == 0, patch, tail), LANES - 1, axis=1)


def row_taps(ref, r):
    channels = ref.shape[1]
    return ref[pl.ds(r - 1, 3)].reshape(3 * channels, ref.shape[2])


def matmul(weights, taps):
    return jnp.dot(weights, taps, preferred_element_type=F32)


def state_kernel(
    flag_ref, rows_ref, strip_ref, above_ref, below_ref, weight_ref,
    gates_ref, strip_gates_ref, cell_strip_ref, three, patches,
):
    units = rows_ref.shape[1] // 2
    count = rows_ref.shape[0]
    has_above = flag_ref[0].astype(F32).astype(BF)
    has_below = flag_ref[1].astype(F32).astype(BF)
    strip = full_strip(strip_ref[...], above_ref[3], below_ref[3], has_above, has_below)
    cell_strip_ref[...] = strip[units:]
    strip = strip[:units]
    strip_gates_ref[...] = matmul(weight_ref[...], strip_taps(strip))
    store_patches(strip, patches, 1, count + 7)
    for i in range(3):
        store_three(three, 1 + i, above_ref[i, :units] * has_above, patches[1 + i])
        r = count + PAD + i
        store_three(three, r, below_ref[i, :units] * has_below, patches[r])

    for y in range(count):
        store_three(three, y + PAD, rows_ref[y, :units], patches[y + PAD])
    for i in range(count + 4):
        gates_ref[i] = matmul(weight_ref[...], row_taps(three, i + 2))


def update(gates, memory):
    units = memory.shape[0]
    ingate = 0.5 * jnp.tanh(gates[:units]) + 0.5
    forget = 0.5 * jnp.tanh(gates[units : 2 * units]) + 0.5
    outgate = 0.5 * jnp.tanh(gates[2 * units : 3 * units]) + 0.5
    memory = forget * memory + ingate * jnp.tanh(gates[3 * units :])
    return outgate * jnp.tanh(memory), memory


def window_kernel(
    flag_ref, gates_ref, strip_gates_ref, rows_ref, above_ref, below_ref, cell_strip_ref,
    forcing_ref, forcing_strip_ref, f_above_ref, f_below_ref, in_weight_ref, weight_ref, bias_ref,
    hidden_ref, cell_ref,
    f_three, f_patches, f_gates, first, second, patches, memory, h_rows, c_rows,
):
    units = rows_ref.shape[1] // 2
    count = rows_ref.shape[0]
    has_above = flag_ref[0].astype(F32)
    has_below = flag_ref[1].astype(F32)
    bf_above, bf_below = has_above.astype(BF), has_below.astype(BF)
    bias = jnp.broadcast_to(bias_ref[...], (bias_ref.shape[0], 2 * LANES))

    strip = full_strip(forcing_strip_ref[...], f_above_ref[3], f_below_ref[3], bf_above, bf_below)
    strip_forcing = matmul(in_weight_ref[...], strip_taps(strip)) + bias_ref[...]
    store_patches(strip, f_patches, 1, count + 7)
    for i in range(3):
        store_three(f_three, 1 + i, f_above_ref[i] * bf_above, f_patches[1 + i])
        r = count + PAD + i
        store_three(f_three, r, f_below_ref[i] * bf_below, f_patches[r])

    for y in range(count):
        store_three(f_three, y + PAD, forcing_ref[y], f_patches[y + PAD])

    row_of_lane = (lane_of((units, 2 * STRIP)) % STRIP) // 8
    keep = jnp.where(row_of_lane < PAD, has_above, 1.0)
    keep = jnp.where(row_of_lane >= PAD + count, has_below, keep)

    strip_memory = cell_strip_ref[...].astype(F32)
    strip_hidden, strip_memory = update(strip_gates_ref[...] + strip_forcing, strip_memory)
    strip_hidden = (strip_hidden * keep).astype(BF)
    store_patches(strip_hidden, patches, 2, count + 6)

    def kept(hidden, r):
        if r < PAD:
            hidden = hidden * has_above
        elif r >= PAD + count:
            hidden = hidden * has_below
        return hidden.astype(BF)

    def run(first_r, total, batch, body):
        for start in range(first_r, first_r + total, batch):
            body(range(start, min(start + batch, first_r + total)))

    def first_rows(group, olds):
        sums = [matmul(in_weight_ref[...], row_taps(f_three, r)) + bias for r in group]
        states = [update(gates_ref[r - 2] + s, old) for r, s, old in zip(group, sums, olds)]
        marks = [patches[r] for r in group]
        for r, s, (hidden, new), mark in zip(group, sums, states, marks):
            f_gates[r] = s
            memory[r] = new
            store_three(first, r, kept(hidden, r), mark)

    first_rows(
        [2, 3, count + PAD, count + PAD + 1],
        [ref[i, units:].astype(F32) for ref, i in ((above_ref, 1), (above_ref, 2), (below_ref, 0), (below_ref, 1))],
    )
    run(PAD, count, BATCH, lambda group: first_rows(group, [rows_ref[r - PAD, units:].astype(F32) for r in group]))

    strip_gates = matmul(weight_ref[...], strip_taps(strip_hidden)) + strip_forcing
    strip_hidden, strip_memory = update(strip_gates, strip_memory)
    strip_hidden = (strip_hidden * keep).astype(BF)
    store_patches(strip_hidden, patches, 3, count + 5)

    def later(source, group):
        sums = [f_gates[r] + matmul(weight_ref[...], row_taps(source, r)) for r in group]
        return [update(s, memory[r]) for r, s in zip(group, sums)]

    def second_rows(group):
        states = later(first, group)
        marks = [patches[r] for r in group]
        for r, (hidden, new), mark in zip(group, states, marks):
            memory[r] = new
            store_three(second, r, kept(hidden, r), mark)

    run(PAD - 1, count + 2, BATCH, second_rows)

    def third_rows(group):
        for r, (hidden, new) in zip(group, later(second, group)):
            h_rows[r - PAD] = hidden.astype(BF)
            c_rows[r - PAD] = new.astype(BF)

    run(PAD, count, BATCH, third_rows)
    hidden_ref[...] = jnp.swapaxes(h_rows[...], 0, 1)
    cell_ref[...] = jnp.swapaxes(c_rows[...], 0, 1)


def scatter_kernel(target_ref, count_ref, incoming_ref, rows_ref, edge_ref, total):
    slots, channels, width = incoming_ref.shape
    sources = count_ref.shape[0]
    cap = slots // sources
    row_count = rows_ref.shape[0]
    spare = 2 * row_count
    total[...] = jnp.zeros(total.shape, F32)

    for p in range(sources):
        live = count_ref[p]
        for s in range(cap):
            block = jnp.where(s < live, target_ref[p * cap + s], spare)
            total[block] = total[block] + incoming_ref[p * cap + s].astype(F32)
    for y in range(row_count):
        rows_ref[y, :, :width] = total[2 * y].astype(BF)
        rows_ref[y, :, width:] = total[2 * y + 1].astype(BF)
    tiles = edge_tiles(lambda y: rows_ref[y], row_count, channels)
    for t, tile in enumerate(tiles):
        edge_ref[:, t * LANES : (t + 1) * LANES] = tile


def around(count):
    return [(i, (i + 1) % count) for i in range(count)]


def back(count):
    return [((i + 1) % count, i) for i in range(count)]


def exchange_columns(edge):
    count = lax.axis_size("lon")
    from_left = lax.ppermute(edge, "lon", around(count))
    from_right = lax.ppermute(edge, "lon", back(count))
    return from_left, from_right


def exchange_rows(up, down):
    count = lax.axis_size("lat")
    from_above = lax.ppermute(down, "lat", around(count))
    from_below = lax.ppermute(up, "lat", back(count))
    return from_above, from_below


def strips_of(rows, edge, name):
    from_left, from_right = exchange_columns(edge)
    channels = edge.shape[0]
    ends = jax.ShapeDtypeStruct((4, channels, rows.shape[2]), BF)
    strip, up, down = call(
        strips_kernel,
        [jax.ShapeDtypeStruct((channels, 2 * STRIP), BF), ends, ends],
        4, 0, [], name, 1000, (rows, edge, from_left, from_right),
    )
    from_above, from_below = exchange_rows(up, down)
    return strip, from_above, from_below


def on_device(
    satellite_blocks,
    slot_source,
    slot_weight,
    slot_target,
    tile_counts,
    gate_input_weight,
    gate_state_weight,
    gate_bias,
    hidden_init,
    cell_init,
):
    _, tiles, cap, band, block = slot_weight.shape
    channels = satellite_blocks.shape[1]
    units, row_count, column_count = hidden_init.shape
    gates = gate_bias.shape[0]
    slots = tiles * cap
    half = jnp.where(jnp.arange(gates) < 3 * units, 0.5, 1.0)
    in_weight = gate_input_weight * half[:, None].astype(BF)
    state_weight = gate_state_weight * half[:, None].astype(BF)
    bias = (gate_bias * half)[:, None]
    lat = lax.axis_index("lat")
    flags = jnp.stack([lat > 0, lat < lax.axis_size("lat") - 1]).astype(jnp.int32)

    rows, edge = call(
        prepare_kernel,
        [
            jax.ShapeDtypeStruct((row_count, 2 * units, column_count), BF),
            jax.ShapeDtypeStruct((2 * units, STRIP), BF),
        ],
        2, 0, [], "prepare", 1000, (hidden_init, cell_init),
    )
    (outgoing,) = call(
        gather_kernel,
        [jax.ShapeDtypeStruct((slots, channels, block), BF)],
        2, 1, [], "gather_band", 2 * slots * channels * block * band,
        (slot_source.reshape(slots), satellite_blocks, slot_weight.reshape(slots, band, block)),
    )
    incoming = lax.all_to_all(
        outgoing.reshape(tiles, cap, channels, block), ("lat", "lon"), split_axis=0, concat_axis=0, tiled=True
    ).reshape(slots, channels, block)

    strip, above, below = strips_of(rows, edge, "state_strips")
    extended = row_count + 4
    state_gates, strip_gates, cell_strip = call(
        state_kernel,
        [
            jax.ShapeDtypeStruct((extended, gates, column_count), F32),
            jax.ShapeDtypeStruct((gates, 2 * STRIP), F32),
            jax.ShapeDtypeStruct((units, 2 * STRIP), BF),
        ],
        5, 1,
        [
            pltpu.VMEM((row_count + 8, 3 * units, column_count), BF),
            pltpu.VMEM((row_count + 8, units, LANES), BF),
        ],
        "state_gates", 2 * gates * 9 * units * extended * column_count,
        (flags, rows, strip, above, below, state_weight),
    )

    forcing, forcing_edge = call(
        scatter_kernel,
        [
            jax.ShapeDtypeStruct((row_count, channels, column_count), BF),
            jax.ShapeDtypeStruct((channels, STRIP), BF),
        ],
        1, 2,
        [pltpu.VMEM((2 * row_count + 1, channels, block), F32)],
        "scatter_add", slots * channels * block,
        (slot_target.reshape(slots), tile_counts.reshape(tiles), incoming),
    )
    forcing_strip, f_above, f_below = strips_of(forcing, forcing_edge, "forcing_strips")
    out = jax.ShapeDtypeStruct((units, row_count, column_count), BF)
    padded = row_count + 8
    return call(
        window_kernel,
        [out, out],
        13, 1,
        [
            pltpu.VMEM((padded, 3 * channels, column_count), BF),
            pltpu.VMEM((padded, channels, LANES), BF),
            pltpu.VMEM((padded, gates, column_count), F32),
            pltpu.VMEM((padded, 3 * units, column_count), BF),
            pltpu.VMEM((padded, 3 * units, column_count), BF),
            pltpu.VMEM((padded, units, LANES), BF),
            pltpu.VMEM((padded, units, column_count), F32),
            pltpu.VMEM((row_count, units, column_count), BF),
            pltpu.VMEM((row_count, units, column_count), BF),
        ],
        "window", 2 * gates * 9 * (channels + 2 * units) * row_count * column_count,
        (flags, state_gates, strip_gates, rows, above, below, cell_strip,
         forcing, forcing_strip, f_above, f_below, in_weight, state_weight, bias),
    )


def solution(mesh):
    placed = (
        P(("lat", "lon"), None, None),
        P(("lat", "lon"), None, None),
        P(("lat", "lon"), None, None, None, None),
        P(("lat", "lon"), None, None),
        P(("lat", "lon"), None),
        P(),
        P(),
        P(),
        P(None, "lat", "lon"),
        P(None, "lat", "lon"),
    )
    return jax.shard_map(
        on_device,
        mesh=mesh,
        in_specs=placed,
        out_specs=(P(None, "lat", "lon"), P(None, "lat", "lon")),
        check_vma=False,
    )
```

```python
import functools

import jax
import jax.numpy as jnp
from jax import lax
from jax.experimental import pallas as pl
from jax.experimental.pallas import tpu as pltpu
from jax.sharding import PartitionSpec as P

STEPS = 3
PAD = 4
LANES = 128
STRIP = 3 * LANES
BATCH = 2
BF = jnp.bfloat16
F32 = jnp.float32


def lane_of(shape):
    return lax.broadcasted_iota(jnp.int32, shape, len(shape) - 1)


def whole(count):
    return [pl.BlockSpec(memory_space=pltpu.VMEM)] * count


def scalars(count):
    return [pl.BlockSpec(memory_space=pltpu.SMEM)] * count


def call(kernel, outs, ins, scalar_count, scratch, name, flops, args):
    nbytes = sum(a.size * a.dtype.itemsize for a in list(args) + list(outs))
    return pl.pallas_call(
        kernel,
        out_shape=tuple(outs),
        in_specs=scalars(scalar_count) + whole(ins),
        out_specs=tuple(whole(len(outs))),
        scratch_shapes=scratch,
        compiler_params=pltpu.CompilerParams(vmem_limit_bytes=40 * 2**20),
        cost_estimate=pl.CostEstimate(flops=flops, bytes_accessed=nbytes, transcendentals=0),
        name=name,
    )(*args)


def edge_tiles(row_of, row_count, channels):
    lane = lane_of((channels, LANES))
    tiles = [jnp.zeros((channels, LANES), BF) for _ in range(STRIP // LANES)]
    for y in range(row_count):
        row = row_of(y)
        both = jnp.where(lane < 64, row[:, :LANES], row[:, -LANES:])
        r = y + PAD
        place = r % 16
        turned = pltpu.roll(both, (8 * place + 4) % LANES, axis=1)
        tiles[r // 16] = jnp.where(lane // 8 == place, turned, tiles[r // 16])
    return tiles


def gather_kernel(
    ring, source_ref, blocks_hbm, weight_hbm, out_hbm, blocks, weights, out, block_sem, weight_sem, out_sem
):
    cap, tiles = source_ref.shape
    band, width = weights.shape[1:]
    channels = blocks.shape[1]
    groups = tiles // ring
    share = ring * cap
    fetch = pltpu.make_async_copy(blocks_hbm, blocks, block_sem)
    fetch.start()
    parts = [
        pltpu.make_async_copy(
            weight_hbm.at[pl.ds(g * share, share)], weights.at[pl.ds(g * share, share)], weight_sem.at[g]
        )
        for g in range(groups)
    ]
    for part in parts:
        part.start()
    offset = lax.broadcasted_iota(jnp.int32, (band, width), 0) - band // 2
    spot = lane_of((band, width)) + offset
    inside = (spot >= 0) & (spot < width)
    lane = lane_of((channels, width))
    near = lane_of((channels // 2, width)) % 8 < 4
    fetch.wait()
    sends = []
    for g in range(groups):
        parts[g].wait()
        folded = []
        for j in range(ring):
            q = g * ring + j
            edges = jnp.zeros((channels, width), BF)
            for s in range(cap):
                block = blocks[source_ref[s, q]]
                factor = jnp.where(inside, weights[q * cap + s].astype(F32), 0.0)
                total = jnp.zeros((channels, width), F32)
                for k in range(band):
                    moved = block if k == band // 2 else pltpu.roll(block, (band // 2 - k) % width, axis=1)
                    total = total + factor[k : k + 1, :] * moved.astype(F32)
                rounded = total.astype(BF)
                out[q, s * channels : (s + 1) * channels, :] = rounded
                edges = jnp.where(lane // 8 == s, pltpu.roll(rounded, 8 * s + 4, axis=1), edges)
            wide = edges.astype(F32)
            folded.append(wide[: channels // 2] + pltpu.roll(wide[channels // 2 :], 8 * cap, axis=1))
        for j in range(ring):
            both = jnp.where(near, folded[j - 1], folded[(j + 1) % ring])
            out[g * ring + j, cap * channels :, :] = both.astype(BF)
        send = pltpu.make_async_copy(
            out.at[pl.ds(g * ring, ring)], out_hbm.at[pl.ds(g * ring, ring)], out_sem.at[g]
        )
        send.start()
        sends.append(send)
    for send in sends:
        send.wait()


def prepare_kernel(hidden_ref, cell_ref, mark_ref, rows_ref, edge_ref):
    units = hidden_ref.shape[0]
    row_count = hidden_ref.shape[1]
    rows_ref[:, :units, :] = jnp.swapaxes(hidden_ref[...], 0, 1)
    rows_ref[:, units:, :] = jnp.swapaxes(cell_ref[...], 0, 1)
    tiles = edge_tiles(lambda y: rows_ref[y], row_count, 2 * units)
    for t, tile in enumerate(tiles):
        edge_ref[: 2 * units, t * LANES : (t + 1) * LANES] = tile
    edge_ref[2 * units :, :LANES] = mark_ref[...]
    edge_ref[2 * units :, LANES:] = jnp.zeros((mark_ref.shape[0], STRIP - LANES), BF)


def lay_out(rows_ref, own, from_left, from_right, strip_ref, up_ref, down_ref):
    near = lane_of(own.shape) % 8 < 4
    left = jnp.where(near, from_left, own)
    right = jnp.where(near, own, from_right)
    strip_ref[:, :STRIP] = left
    strip_ref[:, STRIP:] = right
    rows = rows_ref.shape[0]
    up_ref[:3] = rows_ref[:3]
    up_ref[3, :, :LANES] = left[:, :LANES]
    up_ref[3, :, LANES:] = right[:, :LANES]
    down_ref[:3] = rows_ref[rows - 3 :]
    down_ref[3, :, :LANES] = left[:, 2 * LANES :]
    down_ref[3, :, LANES:] = right[:, 2 * LANES :]


def strips_kernel(rows_ref, edge_ref, left_ref, right_ref, strip_ref, up_ref, down_ref, mark_ref):
    channels = rows_ref.shape[1]
    lay_out(
        rows_ref, edge_ref[:channels], left_ref[:channels], right_ref[:channels], strip_ref, up_ref, down_ref
    )
    near = lane_of(mark_ref.shape) % 8 < 4
    from_left = left_ref[channels:, :LANES].astype(F32)
    mark_ref[...] = jnp.where(near, from_left, right_ref[channels:, :LANES].astype(F32))


def full_strip(strip, above, below, has_above, has_below):
    lane = lane_of(above[:, :LANES].shape)
    from_above = (lane >= 8) & (lane < 32)
    from_below = (lane >= 32) & (lane < 56)
    parts = []
    for side in range(2):
        base = side * STRIP
        theirs = above[:, side * LANES : (side + 1) * LANES] * has_above
        parts.append(jnp.where(from_above, theirs, strip[:, base : base + LANES]))
        parts.append(strip[:, base + LANES : base + 2 * LANES])
        theirs = below[:, side * LANES : (side + 1) * LANES] * has_below
        parts.append(jnp.where(from_below, theirs, strip[:, base + 2 * LANES : base + STRIP]))
    return jnp.concatenate(parts, axis=1)


def strip_taps(strip):
    width = strip.shape[1]
    taps = []
    for a in range(3):
        for e in range(3):
            shift = 8 * (a - 1) + e - 1
            taps.append(strip if shift == 0 else pltpu.roll(strip, -shift % width, axis=1))
    return jnp.concatenate(taps, axis=0)


def patches_of(strip, tiles, first, last):
    channels = strip.shape[0]
    near = lane_of((channels, LANES)) % 8 < 4
    found = {}
    for i, t in enumerate(tiles):
        left = strip[:, i * LANES : (i + 1) * LANES]
        right = strip[:, (len(tiles) + i) * LANES : (len(tiles) + i + 1) * LANES]
        mixed = jnp.where(near, left, right)
        for r in range(max(first, 16 * t), min(last, 16 * t + 16)):
            found[r] = pltpu.roll(mixed, -(8 * (r % 16) + 4) % LANES, axis=1)
    return found


def store_patches(strip, patch_ref, first, last):
    for r, patch in patches_of(strip, range(STRIP // LANES), first, last).items():
        patch_ref[r] = patch


def store_three(ref, r, row, patch):
    channels = row.shape[0]
    lane = lane_of((channels, LANES))
    head, tail = row[:, :LANES], row[:, LANES:]
    ref[r, :channels, :LANES] = pltpu.roll(jnp.where(lane == LANES - 1, patch, head), 1, axis=1)
    ref[r, :channels, LANES:] = pltpu.roll(jnp.where(lane == LANES - 1, head, tail), 1, axis=1)
    ref[r, channels : 2 * channels, :] = row
    ref[r, 2 * channels :, :LANES] = pltpu.roll(jnp.where(lane == 0, tail, head), LANES - 1, axis=1)
    ref[r, 2 * channels :, LANES:] = pltpu.roll(jnp.where(lane == 0, patch, tail), LANES - 1, axis=1)


def row_taps(ref, r):
    channels = ref.shape[1]
    return ref[pl.ds(r - 1, 3)].reshape(3 * channels, ref.shape[2])


def matmul(weights, taps):
    return jnp.dot(weights, taps, preferred_element_type=F32)


def state_kernel(
    flag_ref, rows_ref, strip_ref, above_ref, below_ref, weight_ref, bias_ref,
    gates_ref, strip_gates_ref, cell_strip_ref, wide_bias_ref, three, patches,
):
    units = rows_ref.shape[1] // 2
    count = rows_ref.shape[0]
    has_above = flag_ref[0].astype(F32).astype(BF)
    has_below = flag_ref[1].astype(F32).astype(BF)
    strip = full_strip(strip_ref[...], above_ref[3], below_ref[3], has_above, has_below)
    cell_strip_ref[...] = strip[units:]
    wide_bias_ref[...] = jnp.broadcast_to(bias_ref[...], wide_bias_ref.shape)
    strip = strip[:units]
    strip_gates_ref[...] = matmul(weight_ref[...], strip_taps(strip))
    store_patches(strip, patches, 1, count + 7)
    for i in range(3):
        store_three(three, 1 + i, above_ref[i, :units] * has_above, patches[1 + i])
        r = count + PAD + i
        store_three(three, r, below_ref[i, :units] * has_below, patches[r])

    for y in range(count):
        store_three(three, y + PAD, rows_ref[y, :units], patches[y + PAD])
    for i in range(count + 4):
        gates_ref[i] = matmul(weight_ref[...], row_taps(three, i + 2))


def update(gates, memory):
    units = memory.shape[0]
    ingate = 0.5 * jnp.tanh(gates[:units]) + 0.5
    forget = 0.5 * jnp.tanh(gates[units : 2 * units]) + 0.5
    outgate = 0.5 * jnp.tanh(gates[2 * units : 3 * units]) + 0.5
    memory = forget * memory + ingate * jnp.tanh(gates[3 * units :])
    return outgate * jnp.tanh(memory), memory


def inner_kernel(
    gates_ref, strip_gates_ref, rows_ref, cell_strip_ref, forcing_ref, forcing_strip_ref,
    in_weight_ref, weight_ref, bias_ref,
    hidden_ref, cell_ref, sums_ref, first_ref, second_ref, memory_ref,
    f_three, f_patches, f_gates, first, second, patches, memory,
):
    units = rows_ref.shape[1] // 2
    count = rows_ref.shape[0]
    bias = bias_ref[...]

    strip = forcing_strip_ref[...]
    strip_forcing = matmul(in_weight_ref[...], strip_taps(strip)) + jnp.concatenate([bias] * 3, axis=1)
    store_patches(strip, f_patches, PAD, count + PAD)
    for y in range(count):
        store_three(f_three, y + PAD, forcing_ref[y], f_patches[y + PAD])

    strip_memory = cell_strip_ref[...].astype(F32)
    strip_hidden, strip_memory = update(strip_gates_ref[...] + strip_forcing, strip_memory)
    strip_hidden = strip_hidden.astype(BF)
    store_patches(strip_hidden, patches, PAD + 1, count + PAD - 1)

    def run(margin, body):
        stop = PAD + count - margin
        for start in range(PAD + margin, stop, BATCH):
            body(range(start, min(start + BATCH, stop)))

    def first_rows(group):
        sums = [matmul(in_weight_ref[...], row_taps(f_three, r)) + bias for r in group]
        states = [
            update(gates_ref[r - 2] + s, rows_ref[r - PAD, units:].astype(F32)) for r, s in zip(group, sums)
        ]
        marks = [patches[r] for r in group]
        for r, s, (hidden, new), mark in zip(group, sums, states, marks):
            f_gates[r] = s
            memory[r] = new
            store_three(first, r, hidden.astype(BF), mark)

    run(1, first_rows)

    strip_gates = matmul(weight_ref[...], strip_taps(strip_hidden)) + strip_forcing
    strip_hidden, strip_memory = update(strip_gates, strip_memory)
    store_patches(strip_hidden.astype(BF), patches, PAD + 2, count + PAD - 2)

    def later(source, group):
        sums = [f_gates[r] + matmul(weight_ref[...], row_taps(source, r)) for r in group]
        return [update(s, memory[r]) for r, s in zip(group, sums)]

    def second_rows(group):
        states = later(first, group)
        marks = [patches[r] for r in group]
        for r, (hidden, new), mark in zip(group, states, marks):
            memory[r] = new
            store_three(second, r, hidden.astype(BF), mark)

    run(2, second_rows)

    def third_rows(group):
        for r, (hidden, new) in zip(group, later(second, group)):
            hidden_ref[r - PAD - 3] = hidden.astype(BF)
            cell_ref[r - PAD - 3] = new.astype(BF)

    run(3, third_rows)
    for i, r in enumerate(edge_rows(count, 1, 2)):
        sums_ref[i] = f_gates[r]
        first_ref[i] = first[r]
        memory_ref[i] = memory[r]
    for i, r in enumerate(edge_rows(count, 2, 2)):
        second_ref[i] = second[r]


def edge_rows(count, depth, many):
    top = [PAD + depth + i for i in range(many)]
    return top + [PAD + count - 1 - depth - (many - 1) + i for i in range(many)]


def edge_kernel(
    flag_ref, gates_ref, strip_gates_ref, rows_ref, above_ref, below_ref, cell_strip_ref,
    forcing_ref, forcing_strip_ref, f_above_ref, f_below_ref, in_weight_ref, weight_ref, bias_ref,
    inner_hidden_ref, inner_cell_ref, sums_ref, first_ref, second_ref, memory_ref,
    hidden_ref, cell_ref,
    f_three, first, second, h_rows, c_rows,
):
    units = rows_ref.shape[1] // 2
    count = rows_ref.shape[0]
    has_above = flag_ref[0].astype(F32)
    has_below = flag_ref[1].astype(F32)
    bf_above, bf_below = has_above.astype(BF), has_below.astype(BF)
    bias = bias_ref[...]
    tiles = (0, 2)

    def ends(strip):
        return jnp.concatenate([strip[:, t * LANES : (t + 1) * LANES] for t in (0, 2, 3, 5)], axis=1)

    strip = ends(full_strip(forcing_strip_ref[...], f_above_ref[3], f_below_ref[3], bf_above, bf_below))
    strip_forcing = matmul(in_weight_ref[...], strip_taps(strip)) + jnp.concatenate([bias] * 2, axis=1)
    f_patches = patches_of(strip, tiles, 1, 7)
    f_patches.update(patches_of(strip, tiles, count + PAD - 3, count + PAD + 3))
    for i in range(3):
        store_three(f_three, 1 + i, f_above_ref[i] * bf_above, f_patches[1 + i])
        r = count + PAD + i
        store_three(f_three, r, f_below_ref[i] * bf_below, f_patches[r])
    for r in (PAD, PAD + 1, count + PAD - 2, count + PAD - 1):
        store_three(f_three, r, forcing_ref[r - PAD], f_patches[r])

    lane = lane_of((units, len(tiles) * 2 * LANES))
    row_of_lane = (lane % LANES) // 8 + 32 * (lane // LANES % 2)
    keep = jnp.where(row_of_lane < PAD, has_above, 1.0)
    keep = jnp.where(row_of_lane >= PAD + count, has_below, keep)

    def kept(hidden, r):
        if r < PAD:
            hidden = hidden * has_above
        elif r >= PAD + count:
            hidden = hidden * has_below
        return hidden.astype(BF)

    strip_memory = ends(cell_strip_ref[...]).astype(F32)
    strip_hidden, strip_memory = update(ends(strip_gates_ref[...]) + strip_forcing, strip_memory)
    strip_hidden = (strip_hidden * keep).astype(BF)
    marks = patches_of(strip_hidden, tiles, 2, PAD + 1)
    marks.update(patches_of(strip_hidden, tiles, count + PAD - 1, count + PAD + 2))

    def taps(rows):
        return jnp.concatenate(rows, axis=0)

    sums, memory = {}, {}
    for i, r in enumerate(edge_rows(count, 1, 2)):
        sums[r] = sums_ref[i]
        memory[r] = memory_ref[i]
    group = edge_rows(count, -2, 3)
    olds = [above_ref[1, units:], above_ref[2, units:], rows_ref[0, units:]]
    olds += [rows_ref[count - 1, units:], below_ref[0, units:], below_ref[1, units:]]
    for r, old in zip(group, olds):
        sums[r] = matmul(in_weight_ref[...], row_taps(f_three, r)) + bias
        hidden, memory[r] = update(gates_ref[r - 2] + sums[r], old.astype(F32))
        store_three(first, r, kept(hidden, r), marks[r])
    for i, r in enumerate(edge_rows(count, 1, 2)):
        first[r] = first_ref[i]

    strip_gates = matmul(weight_ref[...], strip_taps(strip_hidden)) + strip_forcing
    strip_hidden, strip_memory = update(strip_gates, strip_memory)
    strip_hidden = (strip_hidden * keep).astype(BF)
    marks = patches_of(strip_hidden, tiles, 3, PAD + 2)
    marks.update(patches_of(strip_hidden, tiles, count + PAD - 2, count + PAD + 1))
    for r in edge_rows(count, -1, 3):
        hidden, memory[r] = update(sums[r] + matmul(weight_ref[...], row_taps(first, r)), memory[r])
        store_three(second, r, kept(hidden, r), marks[r])
    for i, r in enumerate(edge_rows(count, 2, 2)):
        second[r] = second_ref[i]

    for r in edge_rows(count, 0, 3):
        hidden, new = update(sums[r] + matmul(weight_ref[...], row_taps(second, r)), memory[r])
        h_rows[r - PAD] = hidden.astype(BF)
        c_rows[r - PAD] = new.astype(BF)
    h_rows[3 : count - 3] = inner_hidden_ref[...]
    c_rows[3 : count - 3] = inner_cell_ref[...]
    hidden_ref[...] = jnp.swapaxes(h_rows[...], 0, 1)
    cell_ref[...] = jnp.swapaxes(c_rows[...], 0, 1)


def beside(incoming_ref, mark_ref, row_count, channels):
    sources = incoming_ref.shape[0]
    base = incoming_ref.shape[1] - channels // 2
    lane = lane_of((channels // 2, LANES))
    group_lanes = 8 * ((base // channels) % 16)
    tiles = [[jnp.zeros((channels // 2, LANES), F32) for _ in range(2)] for _ in range(STRIP // LANES)]
    for start in range(0, row_count, 16):
        sums = [jnp.zeros((channels // 2, LANES), F32) for _ in range(16)]
        for p in range(sources):
            edges = incoming_ref[p, base:, :].astype(F32)
            mark = jnp.broadcast_to(mark_ref[p : p + 1, :], edges.shape)
            for i in range(16):
                sums[i] = sums[i] + jnp.where(mark == float(start + i), edges, 0.0)
        for i in range(16):
            total = sums[i] + pltpu.roll(sums[i], LANES - 8, axis=1)
            total = total + pltpu.roll(total, LANES - 16, axis=1)
            r = start + i + PAD
            for part in range(2):
                moved = pltpu.roll(total, (8 * (r % 16) - part * group_lanes) % LANES, axis=1)
                tiles[r // 16][part] = jnp.where(lane // 8 == r % 16, moved, tiles[r // 16][part])
    halves = [jnp.concatenate([t[part] for t in tiles], axis=1) for part in range(2)]
    return jnp.concatenate(halves, axis=0).astype(BF)


def scatter_kernel(
    target_ref, count_ref, incoming_ref, mark_ref, rows_ref, strip_ref, up_ref, down_ref, total
):
    cap, sources = target_ref.shape
    row_count, channels, width = rows_ref.shape
    width = width // 2
    spare = 2 * row_count
    total[...] = jnp.zeros(total.shape, F32)
    for p in range(sources):
        live = count_ref[0, p]
        for s in range(cap):
            block = jnp.where(s < live, target_ref[s, p], spare)
            total[block] = total[block] + incoming_ref[p, s * channels : (s + 1) * channels, :].astype(F32)
    for y in range(row_count):
        rows_ref[y, :, :width] = total[2 * y].astype(BF)
        rows_ref[y, :, width:] = total[2 * y + 1].astype(BF)
    own = jnp.concatenate(edge_tiles(lambda y: rows_ref[y], row_count, channels), axis=1)
    others = beside(incoming_ref, mark_ref, row_count, channels)
    lay_out(rows_ref, own, others, others, strip_ref, up_ref, down_ref)


def around(count):
    return [(i, (i + 1) % count) for i in range(count)]


def back(count):
    return [((i + 1) % count, i) for i in range(count)]


def exchange_columns(edge):
    count = lax.axis_size("lon")
    from_left = lax.ppermute(edge, "lon", around(count))
    from_right = lax.ppermute(edge, "lon", back(count))
    return from_left, from_right


def exchange_rows(up, down):
    count = lax.axis_size("lat")
    from_above = lax.ppermute(down, "lat", around(count))
    from_below = lax.ppermute(up, "lat", back(count))
    return from_above, from_below


def marks_of(target, live_count, row_count):
    cap = target.shape[1]
    live = jnp.arange(cap, dtype=jnp.int32)[None, :] < live_count[:, None]
    sides = jnp.arange(2, dtype=jnp.int32)
    wanted = live[:, :, None] & (target[:, :, None] % 2 != sides)
    row = jnp.where(wanted, target[:, :, None] // 2, -1)
    row = jnp.repeat(row, 4, axis=2).reshape(target.shape[0], 8 * cap)
    row = jnp.concatenate([row, row], axis=1)
    return jnp.pad(row, ((0, 0), (0, LANES - row.shape[1])), constant_values=-1).astype(BF)


def on_device(
    satellite_blocks,
    slot_source,
    slot_weight,
    slot_target,
    tile_counts,
    gate_input_weight,
    gate_state_weight,
    gate_bias,
    hidden_init,
    cell_init,
):
    _, tiles, cap, band, block = slot_weight.shape
    channels = satellite_blocks.shape[1]
    units, row_count, column_count = hidden_init.shape
    gates = gate_bias.shape[0]
    slots = tiles * cap
    half = jnp.where(jnp.arange(gates) < 3 * units, 0.5, 1.0)
    in_weight = gate_input_weight * half[:, None].astype(BF)
    state_weight = gate_state_weight * half[:, None].astype(BF)
    bias = (gate_bias * half)[:, None]
    lat = lax.axis_index("lat")
    flags = jnp.stack([lat > 0, lat < lax.axis_size("lat") - 1]).astype(jnp.int32)

    ring = lax.axis_size("lon")
    height = cap * channels + channels // 2
    message = jax.ShapeDtypeStruct((tiles, height, block), BF)
    groups = tiles // ring
    outgoing = pl.pallas_call(
        functools.partial(gather_kernel, ring),
        out_shape=message,
        in_specs=scalars(1) + [pl.BlockSpec(memory_space=pl.ANY)] * 2,
        out_specs=pl.BlockSpec(memory_space=pl.ANY),
        scratch_shapes=[
            pltpu.VMEM(satellite_blocks.shape, BF),
            pltpu.VMEM((slots, band, block), BF),
            pltpu.VMEM(message.shape, BF),
            pltpu.SemaphoreType.DMA,
            pltpu.SemaphoreType.DMA((groups,)),
            pltpu.SemaphoreType.DMA((groups,)),
        ],
        compiler_params=pltpu.CompilerParams(vmem_limit_bytes=40 * 2**20),
        name="gather_band",
    )(slot_source[0].T, satellite_blocks, slot_weight.reshape(slots, band, block))
    incoming = lax.all_to_all(outgoing, ("lat", "lon"), split_axis=0, concat_axis=0, tiled=True)

    rows, edge = call(
        prepare_kernel,
        [
            jax.ShapeDtypeStruct((row_count, 2 * units, column_count), BF),
            jax.ShapeDtypeStruct((2 * units + tiles, STRIP), BF),
        ],
        3, 0, [], "prepare", 1000,
        (hidden_init, cell_init, marks_of(slot_target[0], tile_counts[0], row_count)),
    )
    from_left, from_right = exchange_columns(edge)
    ends = jax.ShapeDtypeStruct((4, 2 * units, column_count), BF)
    strip, up, down, marks = call(
        strips_kernel,
        [
            jax.ShapeDtypeStruct((2 * units, 2 * STRIP), BF),
            ends,
            ends,
            jax.ShapeDtypeStruct((tiles, LANES), F32),
        ],
        4, 0, [], "state_strips", 1000, (rows, edge, from_left, from_right),
    )
    above, below = exchange_rows(up, down)
    extended = row_count + 4
    padded = row_count + 8
    state_gates, strip_gates, cell_strip, bias = call(
        state_kernel,
        [
            jax.ShapeDtypeStruct((extended, gates, column_count), F32),
            jax.ShapeDtypeStruct((gates, 2 * STRIP), F32),
            jax.ShapeDtypeStruct((units, 2 * STRIP), BF),
            jax.ShapeDtypeStruct((gates, column_count), F32),
        ],
        6, 1,
        [
            pltpu.VMEM((padded, 3 * units, column_count), BF),
            pltpu.VMEM((padded, units, LANES), BF),
        ],
        "state_gates", 2 * gates * 9 * units * extended * column_count,
        (flags, rows, strip, above, below, state_weight, bias),
    )
    incoming, state_gates, strip_gates, cell_strip, bias, in_weight = lax.optimization_barrier(
        (incoming, state_gates, strip_gates, cell_strip, bias, in_weight)
    )

    ends = jax.ShapeDtypeStruct((4, channels, column_count), BF)
    forcing, forcing_strip, up, down = call(
        scatter_kernel,
        [
            jax.ShapeDtypeStruct((row_count, channels, column_count), BF),
            jax.ShapeDtypeStruct((channels, 2 * STRIP), BF),
            ends,
            ends,
        ],
        2, 2,
        [pltpu.VMEM((2 * row_count + 1, channels, block), F32)],
        "scatter_add", slots * channels * block,
        (slot_target[0].T, tile_counts, incoming, marks),
    )
    f_above, f_below = exchange_rows(up, down)
    inner_rows = jax.ShapeDtypeStruct((row_count - 6, units, column_count), BF)
    threes = jax.ShapeDtypeStruct((4, 3 * units, column_count), BF)
    inner = call(
        inner_kernel,
        [
            inner_rows,
            inner_rows,
            jax.ShapeDtypeStruct((4, gates, column_count), F32),
            threes,
            threes,
            jax.ShapeDtypeStruct((4, units, column_count), F32),
        ],
        9, 0,
        [
            pltpu.VMEM((padded, 3 * channels, column_count), BF),
            pltpu.VMEM((padded, channels, LANES), BF),
            pltpu.VMEM((padded, gates, column_count), F32),
            pltpu.VMEM((padded, 3 * units, column_count), BF),
            pltpu.VMEM((padded, 3 * units, column_count), BF),
            pltpu.VMEM((padded, units, LANES), BF),
            pltpu.VMEM((padded, units, column_count), F32),
        ],
        "inner", 2 * gates * 9 * (channels + 2 * units) * row_count * column_count,
        (state_gates, strip_gates, rows, cell_strip, forcing, forcing_strip, in_weight, state_weight, bias),
    )
    out = jax.ShapeDtypeStruct((units, row_count, column_count), BF)
    return call(
        edge_kernel,
        [out, out],
        19, 1,
        [
            pltpu.VMEM((padded, 3 * channels, column_count), BF),
            pltpu.VMEM((padded, 3 * units, column_count), BF),
            pltpu.VMEM((padded, 3 * units, column_count), BF),
            pltpu.VMEM((row_count, units, column_count), BF),
            pltpu.VMEM((row_count, units, column_count), BF),
        ],
        "edges", 2 * gates * 9 * (channels + 2 * units) * 6 * column_count,
        (flags, state_gates, strip_gates, rows, above, below, cell_strip, forcing, forcing_strip,
         f_above, f_below, in_weight, state_weight, bias, *inner),
    )


def solution(mesh):
    placed = (
        P(("lat", "lon"), None, None),
        P(("lat", "lon"), None, None),
        P(("lat", "lon"), None, None, None, None),
        P(("lat", "lon"), None, None),
        P(("lat", "lon"), None),
        P(),
        P(),
        P(),
        P(None, "lat", "lon"),
        P(None, "lat", "lon"),
    )
    return jax.shard_map(
        on_device,
        mesh=mesh,
        in_specs=placed,
        out_specs=(P(None, "lat", "lon"), P(None, "lat", "lon")),
        check_vma=False,
    )
```

```python
import functools

import jax
import jax.numpy as jnp
from jax import lax
from jax.experimental import pallas as pl
from jax.experimental.pallas import tpu as pltpu
from jax.sharding import PartitionSpec as P

STEPS = 3
PAD = 4
LANES = 128
STRIP = 3 * LANES
BATCH = 2
BF = jnp.bfloat16
F32 = jnp.float32


def lane_of(shape):
    return lax.broadcasted_iota(jnp.int32, shape, len(shape) - 1)


def whole(count):
    return [pl.BlockSpec(memory_space=pltpu.VMEM)] * count


def scalars(count):
    return [pl.BlockSpec(memory_space=pltpu.SMEM)] * count


def call(kernel, outs, ins, scalar_count, scratch, name, flops, args, mib=8):
    nbytes = sum(a.size * a.dtype.itemsize for a in list(args) + list(outs))
    return pl.pallas_call(
        kernel,
        out_shape=tuple(outs),
        in_specs=scalars(scalar_count) + whole(ins),
        out_specs=tuple(whole(len(outs))),
        scratch_shapes=scratch,
        compiler_params=pltpu.CompilerParams(vmem_limit_bytes=mib * 2**20),
        cost_estimate=pl.CostEstimate(flops=flops, bytes_accessed=nbytes, transcendentals=0),
        name=name,
    )(*args)


def edge_tiles(row_of, row_count, channels):
    lane = lane_of((channels, LANES))
    tiles = [jnp.zeros((channels, LANES), BF) for _ in range(STRIP // LANES)]
    for y in range(row_count):
        row = row_of(y)
        both = jnp.where(lane < 64, row[:, :LANES], row[:, -LANES:])
        r = y + PAD
        place = r % 16
        turned = pltpu.roll(both, (8 * place + 4) % LANES, axis=1)
        tiles[r // 16] = jnp.where(lane // 8 == place, turned, tiles[r // 16])
    return tiles


def gather_kernel(
    ring, source_hbm, blocks_hbm, weight_hbm, out_hbm, blocks, weights, out, source_ref, source_sem, block_sem, weight_sem, out_sem
):
    cap, tiles = source_ref.shape
    band, width = weights.shape[1:]
    channels = blocks.shape[1]
    groups = tiles // ring
    share = ring * cap
    fetch = pltpu.make_async_copy(blocks_hbm, blocks, block_sem)
    fetch.start()
    places = pltpu.make_async_copy(source_hbm, source_ref, source_sem)
    places.start()
    parts = [
        pltpu.make_async_copy(
            weight_hbm.at[pl.ds(g * share, share)], weights.at[pl.ds(g * share, share)], weight_sem.at[g]
        )
        for g in range(groups)
    ]
    for part in parts:
        part.start()
    offset = lax.broadcasted_iota(jnp.int32, (band, width), 0) - band // 2
    spot = lane_of((band, width)) + offset
    inside = (spot >= 0) & (spot < width)
    lane = lane_of((channels, width))
    near = lane_of((channels // 2, width)) % 8 < 4
    places.wait()
    fetch.wait()
    sends = []
    for g in range(groups):
        parts[g].wait()
        folded = []
        for j in range(ring):
            q = g * ring + j
            for s in range(cap):
                block = blocks[source_ref[s, q]]
                factor = jnp.where(inside, weights[q * cap + s].astype(F32), 0.0)
                total = jnp.zeros((channels, width), F32)
                for k in range(band):
                    moved = block if k == band // 2 else pltpu.roll(block, (band // 2 - k) % width, axis=1)
                    total = total + factor[k : k + 1, :] * moved.astype(F32)
                rounded = total.astype(BF)
                out[q, s * channels : (s + 1) * channels, :] = rounded
        for j in range(ring):
            edges = jnp.zeros((channels, width), BF)
            for s in range(cap):
                rounded = out[g * ring + j, s * channels : (s + 1) * channels, :]
                edges = jnp.where(lane // 8 == s, pltpu.roll(rounded, 8 * s + 4, axis=1), edges)
            wide = edges.astype(F32)
            folded.append(wide[: channels // 2] + pltpu.roll(wide[channels // 2 :], 8 * cap, axis=1))
        for j in range(ring):
            both = jnp.where(near, folded[j - 1], folded[(j + 1) % ring])
            out[g * ring + j, cap * channels :, :] = both.astype(BF)
        send = pltpu.make_async_copy(
            out.at[pl.ds(g * ring, ring)], out_hbm.at[pl.ds(g * ring, ring)], out_sem.at[g]
        )
        send.start()
        sends.append(send)
    for send in sends:
        send.wait()


def prepare_kernel(
    hidden_hbm, cell_hbm, target_ref, count_ref, rows_ref, edge_ref, hidden, cell, hidden_sem, cell_sem
):
    fetches = [
        pltpu.make_async_copy(hidden_hbm, hidden, hidden_sem),
        pltpu.make_async_copy(cell_hbm, cell, cell_sem),
    ]
    for fetch in fetches:
        fetch.start()
    units, row_count, _ = hidden.shape
    edge_ref[2 * units :, :LANES] = marks_of(target_ref[...], count_ref[...]).astype(BF)
    edge_ref[2 * units :, LANES:] = jnp.zeros((target_ref.shape[1], STRIP - LANES), BF)
    fetches[0].wait()
    rows_ref[:, :units, :] = jnp.swapaxes(hidden[...], 0, 1)
    fetches[1].wait()
    rows_ref[:, units:, :] = jnp.swapaxes(cell[...], 0, 1)
    tiles = edge_tiles(lambda y: rows_ref[y], row_count, 2 * units)
    for t, tile in enumerate(tiles):
        edge_ref[: 2 * units, t * LANES : (t + 1) * LANES] = tile


def marks_of(target, live_count):
    cap, sources = target.shape
    slot = lax.broadcasted_iota(jnp.int32, target.shape, 0)
    live = slot < live_count
    row = target // 2
    odd = target % 2 == 1
    picked = [jnp.where(live & odd, row, -1), jnp.where(live & ~odd, row, -1)]
    rows = jnp.concatenate([p.astype(F32) for p in picked], axis=0)
    lane = lane_of((2 * cap, LANES))
    which = lax.broadcasted_iota(jnp.int32, (2 * cap, LANES), 0)
    spread = (lane // 8 % cap == which % cap) & ((lane % 8 < 4) == (which < cap))
    return lax.dot_general(
        rows.astype(BF),
        jnp.where(spread, 1.0, 0.0).astype(BF),
        (((0,), (0,)), ((), ())),
        preferred_element_type=F32,
    )


def lay_out(rows_ref, own, from_left, from_right, strip_ref, up_ref, down_ref):
    near = lane_of(own.shape) % 8 < 4
    left = jnp.where(near, from_left, own)
    right = jnp.where(near, own, from_right)
    strip_ref[:, :STRIP] = left
    strip_ref[:, STRIP:] = right
    rows = rows_ref.shape[0]
    up_ref[:3] = rows_ref[:3]
    up_ref[3, :, :LANES] = left[:, :LANES]
    up_ref[3, :, LANES:] = right[:, :LANES]
    down_ref[:3] = rows_ref[rows - 3 :]
    down_ref[3, :, :LANES] = left[:, 2 * LANES :]
    down_ref[3, :, LANES:] = right[:, 2 * LANES :]


def strips_kernel(rows_ref, edge_ref, left_ref, right_ref, strip_ref, up_ref, down_ref, mark_ref):
    channels = rows_ref.shape[1]
    lay_out(
        rows_ref, edge_ref[:channels], left_ref[:channels], right_ref[:channels], strip_ref, up_ref, down_ref
    )
    near = lane_of(mark_ref.shape) % 8 < 4
    from_left = left_ref[channels:, :LANES].astype(F32)
    mark_ref[...] = jnp.where(near, from_left, right_ref[channels:, :LANES].astype(F32))


def full_strip(strip, above, below, has_above, has_below):
    lane = lane_of(above[:, :LANES].shape)
    from_above = (lane >= 8) & (lane < 32)
    from_below = (lane >= 32) & (lane < 56)
    parts = []
    for side in range(2):
        base = side * STRIP
        theirs = above[:, side * LANES : (side + 1) * LANES] * has_above
        parts.append(jnp.where(from_above, theirs, strip[:, base : base + LANES]))
        parts.append(strip[:, base + LANES : base + 2 * LANES])
        theirs = below[:, side * LANES : (side + 1) * LANES] * has_below
        parts.append(jnp.where(from_below, theirs, strip[:, base + 2 * LANES : base + STRIP]))
    return jnp.concatenate(parts, axis=1)


def strip_taps(strip):
    width = strip.shape[1]
    taps = []
    for a in range(3):
        for e in range(3):
            shift = 8 * (a - 1) + e - 1
            taps.append(strip if shift == 0 else pltpu.roll(strip, -shift % width, axis=1))
    return jnp.concatenate(taps, axis=0)


def patches_of(strip, tiles, first, last):
    channels = strip.shape[0]
    near = lane_of((channels, LANES)) % 8 < 4
    found = {}
    for i, t in enumerate(tiles):
        left = strip[:, i * LANES : (i + 1) * LANES]
        right = strip[:, (len(tiles) + i) * LANES : (len(tiles) + i + 1) * LANES]
        mixed = jnp.where(near, left, right)
        for r in range(max(first, 16 * t), min(last, 16 * t + 16)):
            found[r] = pltpu.roll(mixed, -(8 * (r % 16) + 4) % LANES, axis=1)
    return found


def store_patches(strip, patch_ref, first, last):
    for r, patch in patches_of(strip, range(STRIP // LANES), first, last).items():
        patch_ref[r] = patch


def store_three(ref, r, row, patch):
    channels = row.shape[0]
    lane = lane_of((channels, LANES))
    head, tail = row[:, :LANES], row[:, LANES:]
    ref[r, :channels, :LANES] = pltpu.roll(jnp.where(lane == LANES - 1, patch, head), 1, axis=1)
    ref[r, :channels, LANES:] = pltpu.roll(jnp.where(lane == LANES - 1, head, tail), 1, axis=1)
    ref[r, channels : 2 * channels, :] = row
    ref[r, 2 * channels :, :LANES] = pltpu.roll(jnp.where(lane == 0, tail, head), LANES - 1, axis=1)
    ref[r, 2 * channels :, LANES:] = pltpu.roll(jnp.where(lane == 0, patch, tail), LANES - 1, axis=1)


def row_taps(ref, r):
    channels = ref.shape[1]
    return ref[pl.ds(r - 1, 3)].reshape(3 * channels, ref.shape[2])


def matmul(weights, taps):
    return jnp.dot(weights, taps, preferred_element_type=F32)


def state_kernel(
    rows_ref, strip_ref, weight_ref, bias_ref,
    gates_ref, strip_gates_ref, wide_bias_ref, three, patches,
):
    units = rows_ref.shape[1] // 2
    count = rows_ref.shape[0]
    wide_bias_ref[...] = jnp.broadcast_to(bias_ref[...], wide_bias_ref.shape)
    strip = strip_ref[:units]
    strip_gates_ref[...] = matmul(weight_ref[...], strip_taps(strip))
    store_patches(strip, patches, PAD, count + PAD)
    for y in range(count):
        store_three(three, y + PAD, rows_ref[y, :units], patches[y + PAD])
    for y in range(1, count - 1):
        gates_ref[y - 1] = matmul(weight_ref[...], row_taps(three, y + PAD))


def ends_of(strip):
    return jnp.concatenate([strip[:, t * LANES : (t + 1) * LANES] for t in (0, 2, 3, 5)], axis=1)


def edge_patches(strip, first, last, count):
    found = patches_of(strip, (0, 2), first, last)
    mirror = count + 2 * PAD - 1
    found.update(patches_of(strip, (0, 2), mirror - last + 1, mirror - first + 1))
    return found


def state_edge_kernel(
    flag_ref, rows_ref, strip_ref, above_ref, below_ref, weight_ref,
    gates_ref, strip_gates_ref, cell_strip_ref, three,
):
    units = rows_ref.shape[1] // 2
    count = rows_ref.shape[0]
    has_above = flag_ref[0].astype(F32).astype(BF)
    has_below = flag_ref[1].astype(F32).astype(BF)
    strip = ends_of(full_strip(strip_ref[...], above_ref[3], below_ref[3], has_above, has_below))
    cell_strip_ref[...] = strip[units:]
    strip = strip[:units]
    strip_gates_ref[...] = matmul(weight_ref[...], strip_taps(strip))
    patches = edge_patches(strip, 1, PAD + 2, count)
    for i in range(3):
        store_three(three, 1 + i, above_ref[i, :units] * has_above, patches[1 + i])
        r = count + PAD + i
        store_three(three, r, below_ref[i, :units] * has_below, patches[r])
    for r in edge_rows(count, 0, 2):
        store_three(three, r, rows_ref[r - PAD, :units], patches[r])
    for i, r in enumerate(edge_rows(count, -2, 3)):
        gates_ref[i] = matmul(weight_ref[...], row_taps(three, r))


def update(gates, memory):
    units = memory.shape[0]
    ingate = 0.5 * jnp.tanh(gates[:units]) + 0.5
    forget = 0.5 * jnp.tanh(gates[units : 2 * units]) + 0.5
    outgate = 0.5 * jnp.tanh(gates[2 * units : 3 * units]) + 0.5
    memory = forget * memory + ingate * jnp.tanh(gates[3 * units :])
    return outgate * jnp.tanh(memory), memory


def inner_kernel(
    gates_ref, strip_gates_ref, rows_ref, strip_ref, forcing_ref, forcing_strip_ref,
    in_weight_ref, weight_ref, bias_ref,
    hidden_ref, cell_ref, sums_ref, first_ref, second_ref, memory_ref,
    f_three, f_patches, f_gates, first, second, patches, memory,
):
    units = rows_ref.shape[1] // 2
    count = rows_ref.shape[0]
    bias = bias_ref[...]

    strip = forcing_strip_ref[...]
    strip_forcing = matmul(in_weight_ref[...], strip_taps(strip)) + jnp.concatenate([bias] * 3, axis=1)
    store_patches(strip, f_patches, PAD, count + PAD)
    for y in range(count):
        store_three(f_three, y + PAD, forcing_ref[y], f_patches[y + PAD])

    strip_memory = strip_ref[units:].astype(F32)
    strip_hidden, strip_memory = update(strip_gates_ref[...] + strip_forcing, strip_memory)
    strip_hidden = strip_hidden.astype(BF)
    store_patches(strip_hidden, patches, PAD + 1, count + PAD - 1)

    def run(margin, body):
        stop = PAD + count - margin
        for start in range(PAD + margin, stop, BATCH):
            body(range(start, min(start + BATCH, stop)))

    def first_rows(group):
        sums = [matmul(in_weight_ref[...], row_taps(f_three, r)) + bias for r in group]
        states = [
            update(gates_ref[r - PAD - 1] + s, rows_ref[r - PAD, units:].astype(F32)) for r, s in zip(group, sums)
        ]
        marks = [patches[r] for r in group]
        for r, s, (hidden, new), mark in zip(group, sums, states, marks):
            f_gates[r] = s
            memory[r] = new
            store_three(first, r, hidden.astype(BF), mark)

    run(1, first_rows)

    strip_gates = matmul(weight_ref[...], strip_taps(strip_hidden)) + strip_forcing
    strip_hidden, strip_memory = update(strip_gates, strip_memory)
    store_patches(strip_hidden.astype(BF), patches, PAD + 2, count + PAD - 2)

    def later(source, group):
        sums = [f_gates[r] + matmul(weight_ref[...], row_taps(source, r)) for r in group]
        return [update(s, memory[r]) for r, s in zip(group, sums)]

    def second_rows(group):
        states = later(first, group)
        marks = [patches[r] for r in group]
        for r, (hidden, new), mark in zip(group, states, marks):
            memory[r] = new
            store_three(second, r, hidden.astype(BF), mark)

    run(2, second_rows)

    def third_rows(group):
        for r, (hidden, new) in zip(group, later(second, group)):
            hidden_ref[r - PAD - 3] = hidden.astype(BF)
            cell_ref[r - PAD - 3] = new.astype(BF)

    run(3, third_rows)
    for i, r in enumerate(edge_rows(count, 1, 2)):
        sums_ref[i] = f_gates[r]
        first_ref[i] = first[r]
        memory_ref[i] = memory[r]
    for i, r in enumerate(edge_rows(count, 2, 2)):
        second_ref[i] = second[r]


def edge_rows(count, depth, many):
    top = [PAD + depth + i for i in range(many)]
    return top + [PAD + count - 1 - depth - (many - 1) + i for i in range(many)]


def edge_kernel(
    flag_ref, gates_ref, strip_gates_ref, rows_ref, above_ref, below_ref, cell_strip_ref,
    forcing_ref, forcing_strip_ref, f_above_ref, f_below_ref, in_weight_ref, weight_ref, bias_ref,
    inner_hidden_ref, inner_cell_ref, sums_ref, first_ref, second_ref, memory_ref,
    hidden_ref, cell_ref,
    f_three, first, second, h_rows, c_rows,
):
    units = rows_ref.shape[1] // 2
    count = rows_ref.shape[0]
    has_above = flag_ref[0].astype(F32)
    has_below = flag_ref[1].astype(F32)
    bf_above, bf_below = has_above.astype(BF), has_below.astype(BF)
    bias = bias_ref[...]

    strip = ends_of(full_strip(forcing_strip_ref[...], f_above_ref[3], f_below_ref[3], bf_above, bf_below))
    strip_forcing = matmul(in_weight_ref[...], strip_taps(strip)) + jnp.concatenate([bias] * 2, axis=1)
    f_patches = edge_patches(strip, 1, PAD + 2, count)
    for i in range(3):
        store_three(f_three, 1 + i, f_above_ref[i] * bf_above, f_patches[1 + i])
        r = count + PAD + i
        store_three(f_three, r, f_below_ref[i] * bf_below, f_patches[r])
    for r in edge_rows(count, 0, 2):
        store_three(f_three, r, forcing_ref[r - PAD], f_patches[r])

    lane = lane_of((units, strip.shape[1]))
    row_of_lane = (lane % LANES) // 8 + 32 * (lane // LANES % 2)
    keep = jnp.where(row_of_lane < PAD, has_above, 1.0)
    keep = jnp.where(row_of_lane >= PAD + count, has_below, keep)

    def kept(hidden, r):
        if r < PAD:
            hidden = hidden * has_above
        elif r >= PAD + count:
            hidden = hidden * has_below
        return hidden.astype(BF)

    strip_memory = cell_strip_ref[...].astype(F32)
    strip_hidden, strip_memory = update(strip_gates_ref[...] + strip_forcing, strip_memory)
    strip_hidden = (strip_hidden * keep).astype(BF)
    marks = edge_patches(strip_hidden, 2, PAD + 1, count)

    def taps(rows):
        return jnp.concatenate(rows, axis=0)

    sums, memory = {}, {}
    for i, r in enumerate(edge_rows(count, 1, 2)):
        sums[r] = sums_ref[i]
        memory[r] = memory_ref[i]
    group = edge_rows(count, -2, 3)
    olds = [above_ref[1, units:], above_ref[2, units:], rows_ref[0, units:]]
    olds += [rows_ref[count - 1, units:], below_ref[0, units:], below_ref[1, units:]]
    for i, (r, old) in enumerate(zip(group, olds)):
        sums[r] = matmul(in_weight_ref[...], row_taps(f_three, r)) + bias
        hidden, memory[r] = update(gates_ref[i] + sums[r], old.astype(F32))
        store_three(first, r, kept(hidden, r), marks[r])
    for i, r in enumerate(edge_rows(count, 1, 2)):
        first[r] = first_ref[i]

    strip_gates = matmul(weight_ref[...], strip_taps(strip_hidden)) + strip_forcing
    strip_hidden, strip_memory = update(strip_gates, strip_memory)
    strip_hidden = (strip_hidden * keep).astype(BF)
    marks = edge_patches(strip_hidden, 3, PAD + 2, count)
    for r in edge_rows(count, -1, 3):
        hidden, memory[r] = update(sums[r] + matmul(weight_ref[...], row_taps(first, r)), memory[r])
        store_three(second, r, kept(hidden, r), marks[r])
    for i, r in enumerate(edge_rows(count, 2, 2)):
        second[r] = second_ref[i]

    for r in edge_rows(count, 0, 3):
        hidden, new = update(sums[r] + matmul(weight_ref[...], row_taps(second, r)), memory[r])
        h_rows[r - PAD] = hidden.astype(BF)
        c_rows[r - PAD] = new.astype(BF)
    h_rows[3 : count - 3] = inner_hidden_ref[...]
    c_rows[3 : count - 3] = inner_cell_ref[...]
    hidden_ref[...] = jnp.swapaxes(h_rows[...], 0, 1)
    cell_ref[...] = jnp.swapaxes(c_rows[...], 0, 1)


def beside(incoming_ref, mark_ref, row_count, channels):
    sources = incoming_ref.shape[0]
    base = incoming_ref.shape[1] - channels // 2
    lane = lane_of((channels // 2, LANES))
    group_lanes = 8 * ((base // channels) % 16)
    tiles = [[jnp.zeros((channels // 2, LANES), F32) for _ in range(2)] for _ in range(STRIP // LANES)]
    for start in range(0, row_count, 16):
        sums = [jnp.zeros((channels // 2, LANES), F32) for _ in range(16)]
        for p in range(sources):
            edges = incoming_ref[p, base:, :].astype(F32)
            mark = jnp.broadcast_to(mark_ref[p : p + 1, :], edges.shape)
            for i in range(16):
                sums[i] = sums[i] + jnp.where(mark == float(start + i), edges, 0.0)
        for i in range(16):
            total = sums[i] + pltpu.roll(sums[i], LANES - 8, axis=1)
            total = total + pltpu.roll(total, LANES - 16, axis=1)
            r = start + i + PAD
            for part in range(2):
                moved = pltpu.roll(total, (8 * (r % 16) - part * group_lanes) % LANES, axis=1)
                tiles[r // 16][part] = jnp.where(lane // 8 == r % 16, moved, tiles[r // 16][part])
    halves = [jnp.concatenate([t[part] for t in tiles], axis=1) for part in range(2)]
    return jnp.concatenate(halves, axis=0).astype(BF)


def scatter_kernel(
    target_ref, count_ref, incoming_ref, mark_ref, rows_ref, strip_ref, up_ref, down_ref, total
):
    cap, sources = target_ref.shape
    row_count, channels, width = rows_ref.shape
    width = width // 2
    spare = 2 * row_count
    total[...] = jnp.zeros(total.shape, F32)
    for p in range(sources):
        live = count_ref[0, p]
        for s in range(cap):
            block = jnp.where(s < live, target_ref[s, p], spare)
            total[block] = total[block] + incoming_ref[p, s * channels : (s + 1) * channels, :].astype(F32)
    for y in range(row_count):
        rows_ref[y, :, :width] = total[2 * y].astype(BF)
        rows_ref[y, :, width:] = total[2 * y + 1].astype(BF)
    own = jnp.concatenate(edge_tiles(lambda y: rows_ref[y], row_count, channels), axis=1)
    others = beside(incoming_ref, mark_ref, row_count, channels)
    lay_out(rows_ref, own, others, others, strip_ref, up_ref, down_ref)


def around(count):
    return [(i, (i + 1) % count) for i in range(count)]


def back(count):
    return [((i + 1) % count, i) for i in range(count)]


def exchange_columns(edge):
    count = lax.axis_size("lon")
    from_left = lax.ppermute(edge, "lon", around(count))
    from_right = lax.ppermute(edge, "lon", back(count))
    return from_left, from_right


def exchange_rows(up, down):
    count = lax.axis_size("lat")
    from_above = lax.ppermute(down, "lat", around(count))
    from_below = lax.ppermute(up, "lat", back(count))
    return from_above, from_below


def on_device(
    satellite_blocks,
    slot_source,
    slot_weight,
    slot_target,
    tile_counts,
    gate_input_weight,
    gate_state_weight,
    gate_bias,
    hidden_init,
    cell_init,
):
    _, tiles, cap, band, block = slot_weight.shape
    channels = satellite_blocks.shape[1]
    units, row_count, column_count = hidden_init.shape
    gates = gate_bias.shape[0]
    slots = tiles * cap
    half = jnp.where(jnp.arange(gates) < 3 * units, 0.5, 1.0)
    in_weight = gate_input_weight * half[:, None].astype(BF)
    state_weight = gate_state_weight * half[:, None].astype(BF)
    bias = (gate_bias * half)[:, None]
    lat = lax.axis_index("lat")
    flags = jnp.stack([lat > 0, lat < lax.axis_size("lat") - 1]).astype(jnp.int32)

    ring = lax.axis_size("lon")
    height = cap * channels + channels // 2
    message = jax.ShapeDtypeStruct((tiles, height, block), BF)
    groups = tiles // ring
    outgoing = pl.pallas_call(
        functools.partial(gather_kernel, ring),
        out_shape=message,
        in_specs=[pl.BlockSpec(memory_space=pl.ANY)] * 3,
        out_specs=pl.BlockSpec(memory_space=pl.ANY),
        scratch_shapes=[
            pltpu.VMEM(satellite_blocks.shape, BF),
            pltpu.VMEM((slots, band, block), BF),
            pltpu.VMEM(message.shape, BF),
            pltpu.SMEM((cap, tiles), jnp.int32),
            pltpu.SemaphoreType.DMA,
            pltpu.SemaphoreType.DMA,
            pltpu.SemaphoreType.DMA((groups,)),
            pltpu.SemaphoreType.DMA((groups,)),
        ],
        compiler_params=pltpu.CompilerParams(vmem_limit_bytes=60 * 2**20),
        name="gather_band",
    )(slot_source[0].T, satellite_blocks, slot_weight.reshape(slots, band, block))
    incoming = lax.all_to_all(outgoing, ("lat", "lon"), split_axis=0, concat_axis=0, tiled=True)

    rows, edge = pl.pallas_call(
        prepare_kernel,
        out_shape=(
            jax.ShapeDtypeStruct((row_count, 2 * units, column_count), BF),
            jax.ShapeDtypeStruct((2 * units + tiles, STRIP), BF),
        ),
        in_specs=[pl.BlockSpec(memory_space=pl.ANY)] * 2 + whole(2),
        out_specs=tuple(whole(2)),
        scratch_shapes=[
            pltpu.VMEM(hidden_init.shape, BF),
            pltpu.VMEM(cell_init.shape, BF),
            pltpu.SemaphoreType.DMA,
            pltpu.SemaphoreType.DMA,
        ],
        compiler_params=pltpu.CompilerParams(vmem_limit_bytes=60 * 2**20),
        name="prepare",
    )(hidden_init, cell_init, slot_target[0].T, tile_counts)
    from_left, from_right = exchange_columns(edge)
    ends = jax.ShapeDtypeStruct((4, 2 * units, column_count), BF)
    strip, up, down, marks = call(
        strips_kernel,
        [
            jax.ShapeDtypeStruct((2 * units, 2 * STRIP), BF),
            ends,
            ends,
            jax.ShapeDtypeStruct((tiles, LANES), F32),
        ],
        4, 0, [], "state_strips", 1000, (rows, edge, from_left, from_right),
    )
    above, below = exchange_rows(up, down)
    padded = row_count + 8
    state_gates, strip_gates, bias = call(
        state_kernel,
        [
            jax.ShapeDtypeStruct((row_count - 2, gates, column_count), F32),
            jax.ShapeDtypeStruct((gates, 2 * STRIP), F32),
            jax.ShapeDtypeStruct((gates, column_count), F32),
        ],
        4, 0,
        [
            pltpu.VMEM((padded, 3 * units, column_count), BF),
            pltpu.VMEM((padded, units, LANES), BF),
        ],
        "state_gates", 2 * gates * 9 * units * row_count * column_count,
        (rows, strip, state_weight, bias), 16,
    )
    edge_gates, edge_strip_gates, cell_strip = call(
        state_edge_kernel,
        [
            jax.ShapeDtypeStruct((6, gates, column_count), F32),
            jax.ShapeDtypeStruct((gates, 4 * LANES), F32),
            jax.ShapeDtypeStruct((units, 4 * LANES), BF),
        ],
        5, 1,
        [pltpu.VMEM((padded, 3 * units, column_count), BF)],
        "state_edges", 2 * gates * 9 * units * 8 * column_count,
        (flags, rows, strip, above, below, state_weight),
    )
    incoming, state_gates, strip_gates, bias, in_weight = lax.optimization_barrier(
        (incoming, state_gates, strip_gates, bias, in_weight)
    )

    ends = jax.ShapeDtypeStruct((4, channels, column_count), BF)
    forcing, forcing_strip, up, down = call(
        scatter_kernel,
        [
            jax.ShapeDtypeStruct((row_count, channels, column_count), BF),
            jax.ShapeDtypeStruct((channels, 2 * STRIP), BF),
            ends,
            ends,
        ],
        2, 2,
        [pltpu.VMEM((2 * row_count + 1, channels, block), F32)],
        "scatter_add", slots * channels * block,
        (slot_target[0].T, tile_counts, incoming, marks),
    )
    f_above, f_below = exchange_rows(up, down)
    inner_rows = jax.ShapeDtypeStruct((row_count - 6, units, column_count), BF)
    threes = jax.ShapeDtypeStruct((4, 3 * units, column_count), BF)
    inner = call(
        inner_kernel,
        [
            inner_rows,
            inner_rows,
            jax.ShapeDtypeStruct((4, gates, column_count), F32),
            threes,
            threes,
            jax.ShapeDtypeStruct((4, units, column_count), F32),
        ],
        9, 0,
        [
            pltpu.VMEM((padded, 3 * channels, column_count), BF),
            pltpu.VMEM((padded, channels, LANES), BF),
            pltpu.VMEM((padded, gates, column_count), F32),
            pltpu.VMEM((padded, 3 * units, column_count), BF),
            pltpu.VMEM((padded, 3 * units, column_count), BF),
            pltpu.VMEM((padded, units, LANES), BF),
            pltpu.VMEM((padded, units, column_count), F32),
        ],
        "inner", 2 * gates * 9 * (channels + 2 * units) * row_count * column_count,
        (state_gates, strip_gates, rows, strip, forcing, forcing_strip, in_weight, state_weight, bias), 24,
    )
    out = jax.ShapeDtypeStruct((units, row_count, column_count), BF)
    return call(
        edge_kernel,
        [out, out],
        19, 1,
        [
            pltpu.VMEM((padded, 3 * channels, column_count), BF),
            pltpu.VMEM((padded, 3 * units, column_count), BF),
            pltpu.VMEM((padded, 3 * units, column_count), BF),
            pltpu.VMEM((row_count, units, column_count), BF),
            pltpu.VMEM((row_count, units, column_count), BF),
        ],
        "edges", 2 * gates * 9 * (channels + 2 * units) * 6 * column_count,
        (flags, edge_gates, edge_strip_gates, rows, above, below, cell_strip, forcing, forcing_strip,
         f_above, f_below, in_weight, state_weight, bias, *inner), 16,
    )


def solution(mesh):
    placed = (
        P(("lat", "lon"), None, None),
        P(("lat", "lon"), None, None),
        P(("lat", "lon"), None, None, None, None),
        P(("lat", "lon"), None, None),
        P(("lat", "lon"), None),
        P(),
        P(),
        P(),
        P(None, "lat", "lon"),
        P(None, "lat", "lon"),
    )
    return jax.shard_map(
        on_device,
        mesh=mesh,
        in_specs=placed,
        out_specs=(P(None, "lat", "lon"), P(None, "lat", "lon")),
        check_vma=False,
    )
```

```python
import functools

import jax
import jax.numpy as jnp
from jax import lax
from jax.experimental import pallas as pl
from jax.experimental.pallas import tpu as pltpu
from jax.sharding import PartitionSpec as P

STEPS = 3
PAD = 4
LANES = 128
STRIP = 3 * LANES
BATCH = 2
PIECE = 6
BF = jnp.bfloat16
F32 = jnp.float32


def lane_of(shape):
    return lax.broadcasted_iota(jnp.int32, shape, len(shape) - 1)


def whole(count):
    return [pl.BlockSpec(memory_space=pltpu.VMEM)] * count


def in_hbm(x):
    return pltpu.with_memory_space_constraint(x, pltpu.HBM)


def scalars(count):
    return [pl.BlockSpec(memory_space=pltpu.SMEM)] * count


def call(
    kernel, outs, ins, scalar_count, scratch, name, flops, args, mib=8, in_specs=None, out_specs=None
):
    nbytes = sum(a.size * a.dtype.itemsize for a in args)
    return pl.pallas_call(
        kernel,
        out_shape=tuple(outs),
        in_specs=in_specs or scalars(scalar_count) + whole(ins),
        out_specs=tuple(out_specs or whole(len(outs))),
        scratch_shapes=scratch,
        compiler_params=pltpu.CompilerParams(vmem_limit_bytes=mib * 2**20),
        cost_estimate=pl.CostEstimate(flops=flops, bytes_accessed=nbytes, transcendentals=0),
        name=name,
    )(*args)


def edge_tiles(row_of, row_count, channels):
    lane = lane_of((channels, LANES))
    tiles = [jnp.zeros((channels, LANES), BF) for _ in range(STRIP // LANES)]
    for y in range(row_count):
        row = row_of(y)
        both = jnp.where(lane < 64, row[:, :LANES], row[:, -LANES:])
        r = y + PAD
        place = r % 16
        turned = pltpu.roll(both, (8 * place + 4) % LANES, axis=1)
        tiles[r // 16] = jnp.where(lane // 8 == place, turned, tiles[r // 16])
    return tiles


def gather_kernel(
    ring, source_hbm, blocks_hbm, weight_hbm, out_hbm, blocks, weights, out, source_ref, source_sem, block_sem, weight_sem, out_sem
):
    cap, tiles = source_ref.shape
    band, width = weights.shape[1:]
    channels = blocks.shape[1]
    groups = tiles // ring
    share = ring * cap
    fetch = pltpu.make_async_copy(blocks_hbm, blocks, block_sem)
    fetch.start()
    places = pltpu.make_async_copy(source_hbm, source_ref, source_sem)
    places.start()
    parts = [
        pltpu.make_async_copy(
            weight_hbm.at[pl.ds(g * share, share)], weights.at[pl.ds(g * share, share)], weight_sem.at[g]
        )
        for g in range(groups)
    ]
    for part in parts:
        part.start()
    offset = lax.broadcasted_iota(jnp.int32, (band, width), 0) - band // 2
    spot = lane_of((band, width)) + offset
    inside = (spot >= 0) & (spot < width)
    lane = lane_of((channels, width))
    near = lane_of((channels // 2, width)) % 8 < 4
    places.wait()
    fetch.wait()
    sends = []
    for g in range(groups):
        parts[g].wait()
        folded = []
        for j in range(ring):
            q = g * ring + j
            for s in range(cap):
                block = blocks[source_ref[s, q]]
                factor = jnp.where(inside, weights[q * cap + s].astype(F32), 0.0)
                total = jnp.zeros((channels, width), F32)
                for k in range(band):
                    moved = block if k == band // 2 else pltpu.roll(block, (band // 2 - k) % width, axis=1)
                    total = total + factor[k : k + 1, :] * moved.astype(F32)
                rounded = total.astype(BF)
                out[q, s * channels : (s + 1) * channels, :] = rounded
        for j in range(ring):
            edges = jnp.zeros((channels, width), BF)
            for s in range(cap):
                rounded = out[g * ring + j, s * channels : (s + 1) * channels, :]
                edges = jnp.where(lane // 8 == s, pltpu.roll(rounded, 8 * s + 4, axis=1), edges)
            wide = edges.astype(F32)
            folded.append(wide[: channels // 2] + pltpu.roll(wide[channels // 2 :], 8 * cap, axis=1))
        for j in range(ring):
            both = jnp.where(near, folded[j - 1], folded[(j + 1) % ring])
            out[g * ring + j, cap * channels :, :] = both.astype(BF)
        send = pltpu.make_async_copy(
            out.at[pl.ds(g * ring, ring)], out_hbm.at[pl.ds(g * ring, ring)], out_sem.at[g]
        )
        send.start()
        sends.append(send)
    for send in sends:
        send.wait()


def prepare_kernel(
    hidden_hbm, cell_hbm, target_ref, count_ref, rows_ref, edge_ref, hidden, cell, hidden_sem, cell_sem
):
    fetches = [
        pltpu.make_async_copy(hidden_hbm, hidden, hidden_sem),
        pltpu.make_async_copy(cell_hbm, cell, cell_sem),
    ]
    for fetch in fetches:
        fetch.start()
    units, row_count, _ = hidden.shape
    edge_ref[2 * units :, :LANES] = marks_of(target_ref[...], count_ref[...]).astype(BF)
    edge_ref[2 * units :, LANES:] = jnp.zeros((target_ref.shape[1], STRIP - LANES), BF)
    fetches[0].wait()
    rows_ref[:, :units, :] = jnp.swapaxes(hidden[...], 0, 1)
    fetches[1].wait()
    rows_ref[:, units:, :] = jnp.swapaxes(cell[...], 0, 1)
    tiles = edge_tiles(lambda y: rows_ref[y], row_count, 2 * units)
    for t, tile in enumerate(tiles):
        edge_ref[: 2 * units, t * LANES : (t + 1) * LANES] = tile


def marks_of(target, live_count):
    cap, sources = target.shape
    slot = lax.broadcasted_iota(jnp.int32, target.shape, 0)
    live = slot < live_count
    row = target // 2
    odd = target % 2 == 1
    picked = [jnp.where(live & odd, row, -1), jnp.where(live & ~odd, row, -1)]
    rows = jnp.concatenate([p.astype(F32) for p in picked], axis=0)
    lane = lane_of((2 * cap, LANES))
    which = lax.broadcasted_iota(jnp.int32, (2 * cap, LANES), 0)
    spread = (lane // 8 % cap == which % cap) & ((lane % 8 < 4) == (which < cap))
    return lax.dot_general(
        rows.astype(BF),
        jnp.where(spread, 1.0, 0.0).astype(BF),
        (((0,), (0,)), ((), ())),
        preferred_element_type=F32,
    )


def lay_out(rows_ref, own, from_left, from_right, strip_ref, up_ref, down_ref):
    near = lane_of(own.shape) % 8 < 4
    left = jnp.where(near, from_left, own)
    right = jnp.where(near, own, from_right)
    strip_ref[:, :STRIP] = left
    strip_ref[:, STRIP:] = right
    rows = rows_ref.shape[0]
    up_ref[:3] = rows_ref[:3]
    up_ref[3, :, :LANES] = left[:, :LANES]
    up_ref[3, :, LANES:] = right[:, :LANES]
    down_ref[:3] = rows_ref[rows - 3 :]
    down_ref[3, :, :LANES] = left[:, 2 * LANES :]
    down_ref[3, :, LANES:] = right[:, 2 * LANES :]


def strips_kernel(rows_ref, edge_ref, left_ref, right_ref, strip_ref, up_ref, down_ref, mark_ref):
    channels = rows_ref.shape[1]
    lay_out(
        rows_ref, edge_ref[:channels], left_ref[:channels], right_ref[:channels], strip_ref, up_ref, down_ref
    )
    near = lane_of(mark_ref.shape) % 8 < 4
    from_left = left_ref[channels:, :LANES].astype(F32)
    mark_ref[...] = jnp.where(near, from_left, right_ref[channels:, :LANES].astype(F32))


def full_strip(strip, above, below, has_above, has_below):
    lane = lane_of(above[:, :LANES].shape)
    from_above = (lane >= 8) & (lane < 32)
    from_below = (lane >= 32) & (lane < 56)
    parts = []
    for side in range(2):
        base = side * STRIP
        theirs = above[:, side * LANES : (side + 1) * LANES] * has_above
        parts.append(jnp.where(from_above, theirs, strip[:, base : base + LANES]))
        parts.append(strip[:, base + LANES : base + 2 * LANES])
        theirs = below[:, side * LANES : (side + 1) * LANES] * has_below
        parts.append(jnp.where(from_below, theirs, strip[:, base + 2 * LANES : base + STRIP]))
    return jnp.concatenate(parts, axis=1)


def strip_taps(strip):
    width = strip.shape[1]
    taps = []
    for a in range(3):
        for e in range(3):
            shift = 8 * (a - 1) + e - 1
            taps.append(strip if shift == 0 else pltpu.roll(strip, -shift % width, axis=1))
    return jnp.concatenate(taps, axis=0)


def patches_of(strip, tiles, first, last):
    channels = strip.shape[0]
    near = lane_of((channels, LANES)) % 8 < 4
    found = {}
    for i, t in enumerate(tiles):
        left = strip[:, i * LANES : (i + 1) * LANES]
        right = strip[:, (len(tiles) + i) * LANES : (len(tiles) + i + 1) * LANES]
        mixed = jnp.where(near, left, right)
        for r in range(max(first, 16 * t), min(last, 16 * t + 16)):
            found[r] = pltpu.roll(mixed, -(8 * (r % 16) + 4) % LANES, axis=1)
    return found


def store_patches(strip, patch_ref, first, last):
    for r, patch in patches_of(strip, range(STRIP // LANES), first, last).items():
        patch_ref[r] = patch


def store_three(ref, r, row, patch):
    channels = row.shape[0]
    lane = lane_of((channels, LANES))
    head, tail = row[:, :LANES], row[:, LANES:]
    ref[r, :channels, :LANES] = pltpu.roll(jnp.where(lane == LANES - 1, patch, head), 1, axis=1)
    ref[r, :channels, LANES:] = pltpu.roll(jnp.where(lane == LANES - 1, head, tail), 1, axis=1)
    ref[r, channels : 2 * channels, :] = row
    ref[r, 2 * channels :, :LANES] = pltpu.roll(jnp.where(lane == 0, tail, head), LANES - 1, axis=1)
    ref[r, 2 * channels :, LANES:] = pltpu.roll(jnp.where(lane == 0, patch, tail), LANES - 1, axis=1)


def row_taps(ref, r):
    channels = ref.shape[1]
    return ref[pl.ds(r - 1, 3)].reshape(3 * channels, ref.shape[2])


def matmul(weights, taps):
    return jnp.dot(weights, taps, preferred_element_type=F32)


def state_kernel(
    rows_ref, strip_ref, weight_ref, bias_ref,
    gates_hbm, strip_gates_ref, wide_bias_ref, gates, three, patches, sems,
):
    units = rows_ref.shape[1] // 2
    count = rows_ref.shape[0]
    wide_bias_ref[...] = jnp.broadcast_to(bias_ref[...], wide_bias_ref.shape)
    strip = strip_ref[:units]
    strip_gates_ref[...] = matmul(weight_ref[...], strip_taps(strip))
    store_patches(strip, patches, PAD, count + PAD)
    for y in range(count):
        store_three(three, y + PAD, rows_ref[y, :units], patches[y + PAD])
    sends = pieces(gates, gates_hbm, sems)
    for y in range(1, count - 1):
        gates[y - 1] = matmul(weight_ref[...], row_taps(three, y + PAD))
        if y % PIECE == 0:
            sends[y // PIECE - 1].start()
    for send in sends:
        send.wait()


def pieces(source, target, sems):
    count = source.shape[0] // PIECE
    spots = [pl.ds(i * PIECE, PIECE) for i in range(count)]
    return [pltpu.make_async_copy(source.at[s], target.at[s], sems.at[i]) for i, s in enumerate(spots)]


def ends_of(strip):
    return jnp.concatenate([strip[:, t * LANES : (t + 1) * LANES] for t in (0, 2, 3, 5)], axis=1)


def edge_patches(strip, first, last, count):
    found = patches_of(strip, (0, 2), first, last)
    mirror = count + 2 * PAD - 1
    found.update(patches_of(strip, (0, 2), mirror - last + 1, mirror - first + 1))
    return found


def state_edge_kernel(
    flag_ref, rows_ref, strip_ref, above_ref, below_ref, weight_ref,
    gates_ref, strip_gates_ref, cell_strip_ref, three,
):
    units = rows_ref.shape[1] // 2
    count = rows_ref.shape[0]
    has_above = flag_ref[0].astype(F32).astype(BF)
    has_below = flag_ref[1].astype(F32).astype(BF)
    strip = ends_of(full_strip(strip_ref[...], above_ref[3], below_ref[3], has_above, has_below))
    cell_strip_ref[...] = strip[units:]
    strip = strip[:units]
    strip_gates_ref[...] = matmul(weight_ref[...], strip_taps(strip))
    patches = edge_patches(strip, 1, PAD + 2, count)
    for i in range(3):
        store_three(three, 1 + i, above_ref[i, :units] * has_above, patches[1 + i])
        r = count + PAD + i
        store_three(three, r, below_ref[i, :units] * has_below, patches[r])
    for r in edge_rows(count, 0, 2):
        store_three(three, r, rows_ref[r - PAD, :units], patches[r])
    for i, r in enumerate(edge_rows(count, -2, 3)):
        gates_ref[i] = matmul(weight_ref[...], row_taps(three, r))


def update(gates, memory):
    units = memory.shape[0]
    ingate = 0.5 * jnp.tanh(gates[:units]) + 0.5
    forget = 0.5 * jnp.tanh(gates[units : 2 * units]) + 0.5
    outgate = 0.5 * jnp.tanh(gates[2 * units : 3 * units]) + 0.5
    memory = forget * memory + ingate * jnp.tanh(gates[3 * units :])
    return outgate * jnp.tanh(memory), memory


def inner_kernel(
    gates_hbm, strip_gates_ref, rows_ref, strip_ref, forcing_ref, forcing_strip_ref,
    in_weight_ref, weight_ref, bias_ref,
    hidden_ref, cell_ref, sums_ref, first_ref, second_ref, memory_ref,
    gates, f_three, f_patches, f_gates, first, second, patches, memory, sems,
):
    units = rows_ref.shape[1] // 2
    count = rows_ref.shape[0]
    bias = bias_ref[...]
    fetches = pieces(gates_hbm, gates, sems)
    for fetch in fetches:
        fetch.start()

    strip = forcing_strip_ref[...]
    strip_forcing = matmul(in_weight_ref[...], strip_taps(strip)) + jnp.concatenate([bias] * 3, axis=1)
    store_patches(strip, f_patches, PAD, count + PAD)
    for y in range(count):
        store_three(f_three, y + PAD, forcing_ref[y], f_patches[y + PAD])

    strip_memory = strip_ref[units:].astype(F32)
    strip_hidden, strip_memory = update(strip_gates_ref[...] + strip_forcing, strip_memory)
    strip_hidden = strip_hidden.astype(BF)
    store_patches(strip_hidden, patches, PAD + 1, count + PAD - 1)

    def run(margin, body):
        stop = PAD + count - margin
        for start in range(PAD + margin, stop, BATCH):
            body(range(start, min(start + BATCH, stop)))

    def first_rows(group):
        for r in group:
            if (r - PAD - 1) % PIECE == 0:
                fetches[(r - PAD - 1) // PIECE].wait()
        sums = [matmul(in_weight_ref[...], row_taps(f_three, r)) + bias for r in group]
        states = [
            update(gates[r - PAD - 1] + s, rows_ref[r - PAD, units:].astype(F32)) for r, s in zip(group, sums)
        ]
        marks = [patches[r] for r in group]
        for r, s, (hidden, new), mark in zip(group, sums, states, marks):
            f_gates[r] = s
            memory[r] = new
            store_three(first, r, hidden.astype(BF), mark)

    run(1, first_rows)

    strip_gates = matmul(weight_ref[...], strip_taps(strip_hidden)) + strip_forcing
    strip_hidden, strip_memory = update(strip_gates, strip_memory)
    store_patches(strip_hidden.astype(BF), patches, PAD + 2, count + PAD - 2)

    def later(source, group):
        sums = [f_gates[r] + matmul(weight_ref[...], row_taps(source, r)) for r in group]
        return [update(s, memory[r]) for r, s in zip(group, sums)]

    def second_rows(group):
        states = later(first, group)
        marks = [patches[r] for r in group]
        for r, (hidden, new), mark in zip(group, states, marks):
            memory[r] = new
            store_three(second, r, hidden.astype(BF), mark)

    run(2, second_rows)

    def third_rows(group):
        for r, (hidden, new) in zip(group, later(second, group)):
            hidden_ref[r - PAD - 3] = hidden.astype(BF)
            cell_ref[r - PAD - 3] = new.astype(BF)

    run(3, third_rows)
    for i, r in enumerate(edge_rows(count, 1, 2)):
        sums_ref[i] = f_gates[r]
        first_ref[i] = first[r]
        memory_ref[i] = memory[r]
    for i, r in enumerate(edge_rows(count, 2, 2)):
        second_ref[i] = second[r]


def edge_rows(count, depth, many):
    top = [PAD + depth + i for i in range(many)]
    return top + [PAD + count - 1 - depth - (many - 1) + i for i in range(many)]


def edge_kernel(
    flag_ref, gates_ref, strip_gates_ref, rows_ref, above_ref, below_ref, cell_strip_ref,
    forcing_ref, forcing_strip_ref, f_above_ref, f_below_ref, in_weight_ref, weight_ref, bias_ref,
    inner_hidden_ref, inner_cell_ref, sums_ref, first_ref, second_ref, memory_ref,
    hidden_ref, cell_ref,
    f_three, first, second, h_rows, c_rows,
):
    units = rows_ref.shape[1] // 2
    count = rows_ref.shape[0]
    has_above = flag_ref[0].astype(F32)
    has_below = flag_ref[1].astype(F32)
    bf_above, bf_below = has_above.astype(BF), has_below.astype(BF)
    bias = bias_ref[...]

    strip = ends_of(full_strip(forcing_strip_ref[...], f_above_ref[3], f_below_ref[3], bf_above, bf_below))
    strip_forcing = matmul(in_weight_ref[...], strip_taps(strip)) + jnp.concatenate([bias] * 2, axis=1)
    f_patches = edge_patches(strip, 1, PAD + 2, count)
    for i in range(3):
        store_three(f_three, 1 + i, f_above_ref[i] * bf_above, f_patches[1 + i])
        r = count + PAD + i
        store_three(f_three, r, f_below_ref[i] * bf_below, f_patches[r])
    for r in edge_rows(count, 0, 2):
        store_three(f_three, r, forcing_ref[r - PAD], f_patches[r])

    lane = lane_of((units, strip.shape[1]))
    row_of_lane = (lane % LANES) // 8 + 32 * (lane // LANES % 2)
    keep = jnp.where(row_of_lane < PAD, has_above, 1.0)
    keep = jnp.where(row_of_lane >= PAD + count, has_below, keep)

    def kept(hidden, r):
        if r < PAD:
            hidden = hidden * has_above
        elif r >= PAD + count:
            hidden = hidden * has_below
        return hidden.astype(BF)

    strip_memory = cell_strip_ref[...].astype(F32)
    strip_hidden, strip_memory = update(strip_gates_ref[...] + strip_forcing, strip_memory)
    strip_hidden = (strip_hidden * keep).astype(BF)
    marks = edge_patches(strip_hidden, 2, PAD + 1, count)

    def taps(rows):
        return jnp.concatenate(rows, axis=0)

    sums, memory = {}, {}
    for i, r in enumerate(edge_rows(count, 1, 2)):
        sums[r] = sums_ref[i]
        memory[r] = memory_ref[i]
    group = edge_rows(count, -2, 3)
    olds = [above_ref[1, units:], above_ref[2, units:], rows_ref[0, units:]]
    olds += [rows_ref[count - 1, units:], below_ref[0, units:], below_ref[1, units:]]
    for i, (r, old) in enumerate(zip(group, olds)):
        sums[r] = matmul(in_weight_ref[...], row_taps(f_three, r)) + bias
        hidden, memory[r] = update(gates_ref[i] + sums[r], old.astype(F32))
        store_three(first, r, kept(hidden, r), marks[r])
    for i, r in enumerate(edge_rows(count, 1, 2)):
        first[r] = first_ref[i]

    strip_gates = matmul(weight_ref[...], strip_taps(strip_hidden)) + strip_forcing
    strip_hidden, strip_memory = update(strip_gates, strip_memory)
    strip_hidden = (strip_hidden * keep).astype(BF)
    marks = edge_patches(strip_hidden, 3, PAD + 2, count)
    for r in edge_rows(count, -1, 3):
        hidden, memory[r] = update(sums[r] + matmul(weight_ref[...], row_taps(first, r)), memory[r])
        store_three(second, r, kept(hidden, r), marks[r])
    for i, r in enumerate(edge_rows(count, 2, 2)):
        second[r] = second_ref[i]

    for r in edge_rows(count, 0, 3):
        hidden, new = update(sums[r] + matmul(weight_ref[...], row_taps(second, r)), memory[r])
        h_rows[r - PAD] = hidden.astype(BF)
        c_rows[r - PAD] = new.astype(BF)
    h_rows[3 : count - 3] = inner_hidden_ref[...]
    c_rows[3 : count - 3] = inner_cell_ref[...]
    hidden_ref[...] = jnp.swapaxes(h_rows[...], 0, 1)
    cell_ref[...] = jnp.swapaxes(c_rows[...], 0, 1)


def beside(incoming_ref, mark_ref, row_count, channels):
    sources = incoming_ref.shape[0]
    base = incoming_ref.shape[1] - channels // 2
    lane = lane_of((channels // 2, LANES))
    group_lanes = 8 * ((base // channels) % 16)
    tiles = [[jnp.zeros((channels // 2, LANES), F32) for _ in range(2)] for _ in range(STRIP // LANES)]
    for start in range(0, row_count, 16):
        sums = [jnp.zeros((channels // 2, LANES), F32) for _ in range(16)]
        for p in range(sources):
            edges = incoming_ref[p, base:, :].astype(F32)
            mark = jnp.broadcast_to(mark_ref[p : p + 1, :], edges.shape)
            for i in range(16):
                sums[i] = sums[i] + jnp.where(mark == float(start + i), edges, 0.0)
        for i in range(16):
            total = sums[i] + pltpu.roll(sums[i], LANES - 8, axis=1)
            total = total + pltpu.roll(total, LANES - 16, axis=1)
            r = start + i + PAD
            for part in range(2):
                moved = pltpu.roll(total, (8 * (r % 16) - part * group_lanes) % LANES, axis=1)
                tiles[r // 16][part] = jnp.where(lane // 8 == r % 16, moved, tiles[r // 16][part])
    halves = [jnp.concatenate([t[part] for t in tiles], axis=1) for part in range(2)]
    return jnp.concatenate(halves, axis=0).astype(BF)


def scatter_kernel(
    target_ref, count_ref, incoming_ref, mark_ref, rows_ref, strip_ref, up_ref, down_ref, total
):
    cap, sources = target_ref.shape
    row_count, channels, width = rows_ref.shape
    width = width // 2
    spare = 2 * row_count
    total[...] = jnp.zeros(total.shape, F32)
    for p in range(sources):
        live = count_ref[0, p]
        for s in range(cap):
            block = jnp.where(s < live, target_ref[s, p], spare)
            total[block] = total[block] + incoming_ref[p, s * channels : (s + 1) * channels, :].astype(F32)
    for y in range(row_count):
        rows_ref[y, :, :width] = total[2 * y].astype(BF)
        rows_ref[y, :, width:] = total[2 * y + 1].astype(BF)
    own = jnp.concatenate(edge_tiles(lambda y: rows_ref[y], row_count, channels), axis=1)
    others = beside(incoming_ref, mark_ref, row_count, channels)
    lay_out(rows_ref, own, others, others, strip_ref, up_ref, down_ref)


def around(count):
    return [(i, (i + 1) % count) for i in range(count)]


def back(count):
    return [((i + 1) % count, i) for i in range(count)]


def exchange_columns(edge):
    count = lax.axis_size("lon")
    from_left = lax.ppermute(edge, "lon", around(count))
    from_right = lax.ppermute(edge, "lon", back(count))
    return from_left, from_right


def exchange_rows(up, down):
    count = lax.axis_size("lat")
    from_above = lax.ppermute(down, "lat", around(count))
    from_below = lax.ppermute(up, "lat", back(count))
    return from_above, from_below


def on_device(
    satellite_blocks,
    slot_source,
    slot_weight,
    slot_target,
    tile_counts,
    gate_input_weight,
    gate_state_weight,
    gate_bias,
    hidden_init,
    cell_init,
):
    _, tiles, cap, band, block = slot_weight.shape
    channels = satellite_blocks.shape[1]
    units, row_count, column_count = hidden_init.shape
    gates = gate_bias.shape[0]
    slots = tiles * cap
    half = jnp.where(jnp.arange(gates) < 3 * units, 0.5, 1.0)
    in_weight = gate_input_weight * half[:, None].astype(BF)
    state_weight = gate_state_weight * half[:, None].astype(BF)
    bias = (gate_bias * half)[:, None]
    lat = lax.axis_index("lat")
    flags = jnp.stack([lat > 0, lat < lax.axis_size("lat") - 1]).astype(jnp.int32)

    ring = lax.axis_size("lon")
    height = cap * channels + channels // 2
    message = jax.ShapeDtypeStruct((tiles, height, block), BF)
    groups = tiles // ring
    outgoing = pl.pallas_call(
        functools.partial(gather_kernel, ring),
        out_shape=pltpu.HBM(message.shape, BF),
        in_specs=[pl.BlockSpec(memory_space=pl.ANY)] * 3,
        out_specs=pl.BlockSpec(memory_space=pl.ANY),
        scratch_shapes=[
            pltpu.VMEM(satellite_blocks.shape, BF),
            pltpu.VMEM((slots, band, block), BF),
            pltpu.VMEM(message.shape, BF),
            pltpu.SMEM((cap, tiles), jnp.int32),
            pltpu.SemaphoreType.DMA,
            pltpu.SemaphoreType.DMA,
            pltpu.SemaphoreType.DMA((groups,)),
            pltpu.SemaphoreType.DMA((groups,)),
        ],
        compiler_params=pltpu.CompilerParams(vmem_limit_bytes=8 * 2**20),
        name="gather_band",
    )(in_hbm(slot_source[0].T), in_hbm(satellite_blocks), in_hbm(slot_weight.reshape(slots, band, block)))
    incoming = lax.all_to_all(outgoing, ("lat", "lon"), split_axis=0, concat_axis=0, tiled=True)

    rows, edge = pl.pallas_call(
        prepare_kernel,
        out_shape=(
            jax.ShapeDtypeStruct((row_count, 2 * units, column_count), BF),
            jax.ShapeDtypeStruct((2 * units + tiles, STRIP), BF),
        ),
        in_specs=[pl.BlockSpec(memory_space=pl.ANY)] * 2 + whole(2),
        out_specs=tuple(whole(2)),
        scratch_shapes=[
            pltpu.VMEM(hidden_init.shape, BF),
            pltpu.VMEM(cell_init.shape, BF),
            pltpu.SemaphoreType.DMA,
            pltpu.SemaphoreType.DMA,
        ],
        compiler_params=pltpu.CompilerParams(vmem_limit_bytes=8 * 2**20),
        name="prepare",
    )(in_hbm(hidden_init), in_hbm(cell_init), slot_target[0].T, tile_counts)
    from_left, from_right = exchange_columns(edge)
    ends = jax.ShapeDtypeStruct((4, 2 * units, column_count), BF)
    strip, up, down, marks = call(
        strips_kernel,
        [
            jax.ShapeDtypeStruct((2 * units, 2 * STRIP), BF),
            ends,
            ends,
            jax.ShapeDtypeStruct((tiles, LANES), F32),
        ],
        4, 0, [], "state_strips", 1000, (rows, edge, from_left, from_right),
    )
    above, below = exchange_rows(up, down)
    padded = row_count + 8
    inside = (row_count - 2, gates, column_count)
    parts = inside[0] // PIECE
    state_gates, strip_gates, bias = call(
        state_kernel,
        [
            pltpu.HBM(inside, F32),
            jax.ShapeDtypeStruct((gates, 2 * STRIP), F32),
            jax.ShapeDtypeStruct((gates, column_count), F32),
        ],
        4, 0,
        [
            pltpu.VMEM(inside, F32),
            pltpu.VMEM((padded, 3 * units, column_count), BF),
            pltpu.VMEM((padded, units, LANES), BF),
            pltpu.SemaphoreType.DMA((parts,)),
        ],
        "state_gates", 2 * gates * 9 * units * row_count * column_count,
        (rows, strip, state_weight, bias), 16,
        out_specs=[pl.BlockSpec(memory_space=pl.ANY)] + whole(2),
    )
    edge_gates, edge_strip_gates, cell_strip = call(
        state_edge_kernel,
        [
            jax.ShapeDtypeStruct((6, gates, column_count), F32),
            jax.ShapeDtypeStruct((gates, 4 * LANES), F32),
            jax.ShapeDtypeStruct((units, 4 * LANES), BF),
        ],
        5, 1,
        [pltpu.VMEM((padded, 3 * units, column_count), BF)],
        "state_edges", 2 * gates * 9 * units * 8 * column_count,
        (flags, rows, strip, above, below, state_weight),
    )
    incoming, state_gates, strip_gates, bias, in_weight = lax.optimization_barrier(
        (incoming, state_gates, strip_gates, bias, in_weight)
    )

    ends = jax.ShapeDtypeStruct((4, channels, column_count), BF)
    forcing, forcing_strip, up, down = call(
        scatter_kernel,
        [
            jax.ShapeDtypeStruct((row_count, channels, column_count), BF),
            jax.ShapeDtypeStruct((channels, 2 * STRIP), BF),
            ends,
            ends,
        ],
        2, 2,
        [pltpu.VMEM((2 * row_count + 1, channels, block), F32)],
        "scatter_add", slots * channels * block,
        (slot_target[0].T, tile_counts, incoming, marks),
    )
    f_above, f_below = exchange_rows(up, down)
    inner_rows = jax.ShapeDtypeStruct((row_count - 6, units, column_count), BF)
    threes = jax.ShapeDtypeStruct((4, 3 * units, column_count), BF)
    inner = call(
        inner_kernel,
        [
            inner_rows,
            inner_rows,
            jax.ShapeDtypeStruct((4, gates, column_count), F32),
            threes,
            threes,
            jax.ShapeDtypeStruct((4, units, column_count), F32),
        ],
        9, 0,
        [
            pltpu.VMEM(inside, F32),
            pltpu.VMEM((padded, 3 * channels, column_count), BF),
            pltpu.VMEM((padded, channels, LANES), BF),
            pltpu.VMEM((padded, gates, column_count), F32),
            pltpu.VMEM((padded, 3 * units, column_count), BF),
            pltpu.VMEM((padded, 3 * units, column_count), BF),
            pltpu.VMEM((padded, units, LANES), BF),
            pltpu.VMEM((padded, units, column_count), F32),
            pltpu.SemaphoreType.DMA((parts,)),
        ],
        "inner", 2 * gates * 9 * (channels + 2 * units) * row_count * column_count,
        (in_hbm(state_gates), strip_gates, rows, strip, forcing, forcing_strip, in_weight, state_weight, bias), 24,
        in_specs=[pl.BlockSpec(memory_space=pl.ANY)] + whole(8),
    )
    out = jax.ShapeDtypeStruct((units, row_count, column_count), BF)
    return call(
        edge_kernel,
        [out, out],
        19, 1,
        [
            pltpu.VMEM((padded, 3 * channels, column_count), BF),
            pltpu.VMEM((padded, 3 * units, column_count), BF),
            pltpu.VMEM((padded, 3 * units, column_count), BF),
            pltpu.VMEM((row_count, units, column_count), BF),
            pltpu.VMEM((row_count, units, column_count), BF),
        ],
        "edges", 2 * gates * 9 * (channels + 2 * units) * 6 * column_count,
        (flags, edge_gates, edge_strip_gates, rows, above, below, cell_strip, forcing, forcing_strip,
         f_above, f_below, in_weight, state_weight, bias, *inner), 16,
    )


def solution(mesh):
    placed = (
        P(("lat", "lon"), None, None),
        P(("lat", "lon"), None, None),
        P(("lat", "lon"), None, None, None, None),
        P(("lat", "lon"), None, None),
        P(("lat", "lon"), None),
        P(),
        P(),
        P(),
        P(None, "lat", "lon"),
        P(None, "lat", "lon"),
    )
    return jax.shard_map(
        on_device,
        mesh=mesh,
        in_specs=placed,
        out_specs=(P(None, "lat", "lon"), P(None, "lat", "lon")),
        check_vma=False,
    )
```

```python
import functools

import jax
import jax.numpy as jnp
from jax import lax
from jax.experimental import pallas as pl
from jax.experimental.pallas import tpu as pltpu
from jax.sharding import PartitionSpec as P

STEPS = 3
PAD = 4
LANES = 128
STRIP = 3 * LANES
BATCH = 2
PIECE = 6
BF = jnp.bfloat16
F32 = jnp.float32


def lane_of(shape):
    return lax.broadcasted_iota(jnp.int32, shape, len(shape) - 1)


def whole(count):
    return [pl.BlockSpec(memory_space=pltpu.VMEM)] * count


def in_hbm(x):
    return pltpu.with_memory_space_constraint(x, pltpu.HBM)


def scalars(count):
    return [pl.BlockSpec(memory_space=pltpu.SMEM)] * count


def call(
    kernel, outs, ins, scalar_count, scratch, name, flops, args, mib=8, in_specs=None, out_specs=None
):
    nbytes = sum(a.size * a.dtype.itemsize for a in args)
    return pl.pallas_call(
        kernel,
        out_shape=tuple(outs),
        in_specs=in_specs or scalars(scalar_count) + whole(ins),
        out_specs=tuple(out_specs or whole(len(outs))),
        scratch_shapes=scratch,
        compiler_params=pltpu.CompilerParams(vmem_limit_bytes=mib * 2**20),
        cost_estimate=pl.CostEstimate(flops=flops, bytes_accessed=nbytes, transcendentals=0),
        name=name,
    )(*args)


def edge_tiles(row_of, row_count, channels):
    lane = lane_of((channels, LANES))
    tiles = [jnp.zeros((channels, LANES), BF) for _ in range(STRIP // LANES)]
    for y in range(row_count):
        row = row_of(y)
        both = jnp.where(lane < 64, row[:, :LANES], row[:, -LANES:])
        r = y + PAD
        place = r % 16
        turned = pltpu.roll(both, (8 * place + 4) % LANES, axis=1)
        tiles[r // 16] = jnp.where(lane // 8 == place, turned, tiles[r // 16])
    return tiles


def gather_kernel(
    ring, source_hbm, blocks_hbm, weight_hbm, out_hbm, blocks, weights, out, source_ref, source_sem, block_sem, weight_sem, out_sem
):
    cap, tiles = source_ref.shape
    band, width = weights.shape[1:]
    channels = blocks.shape[1]
    groups = tiles // ring
    share = ring * cap
    fetch = pltpu.make_async_copy(blocks_hbm, blocks, block_sem)
    fetch.start()
    places = pltpu.make_async_copy(source_hbm, source_ref, source_sem)
    places.start()
    parts = [
        pltpu.make_async_copy(
            weight_hbm.at[pl.ds(g * share, share)], weights.at[pl.ds(g * share, share)], weight_sem.at[g]
        )
        for g in range(groups)
    ]
    for part in parts:
        part.start()
    offset = lax.broadcasted_iota(jnp.int32, (band, width), 0) - band // 2
    spot = lane_of((band, width)) + offset
    inside = (spot >= 0) & (spot < width)
    lane = lane_of((channels, width))
    near = lane_of((channels // 2, width)) % 8 < 4
    places.wait()
    fetch.wait()
    sends = []
    for g in range(groups):
        parts[g].wait()
        folded = []
        for j in range(ring):
            q = g * ring + j
            for s in range(cap):
                block = blocks[source_ref[s, q]]
                factor = jnp.where(inside, weights[q * cap + s].astype(F32), 0.0)
                total = jnp.zeros((channels, width), F32)
                for k in range(band):
                    moved = block if k == band // 2 else pltpu.roll(block, (band // 2 - k) % width, axis=1)
                    total = total + factor[k : k + 1, :] * moved.astype(F32)
                rounded = total.astype(BF)
                out[q, s * channels : (s + 1) * channels, :] = rounded
        for j in range(ring):
            edges = jnp.zeros((channels, width), BF)
            for s in range(cap):
                rounded = out[g * ring + j, s * channels : (s + 1) * channels, :]
                edges = jnp.where(lane // 8 == s, pltpu.roll(rounded, 8 * s + 4, axis=1), edges)
            wide = edges.astype(F32)
            folded.append(wide[: channels // 2] + pltpu.roll(wide[channels // 2 :], 8 * cap, axis=1))
        for j in range(ring):
            both = jnp.where(near, folded[j - 1], folded[(j + 1) % ring])
            out[g * ring + j, cap * channels :, :] = both.astype(BF)
        send = pltpu.make_async_copy(
            out.at[pl.ds(g * ring, ring)], out_hbm.at[pl.ds(g * ring, ring)], out_sem.at[g]
        )
        send.start()
        sends.append(send)
    for send in sends:
        send.wait()


def prepare_kernel(
    hidden_hbm, cell_hbm, target_hbm, count_hbm, rows_ref, edge_ref, hidden, cell, target_ref, count_ref, sems
):
    fetches = [
        pltpu.make_async_copy(source, target, sems.at[i])
        for i, (source, target) in enumerate(
            [(target_hbm, target_ref), (count_hbm, count_ref), (hidden_hbm, hidden), (cell_hbm, cell)]
        )
    ]
    for fetch in fetches:
        fetch.start()
    units, row_count, _ = hidden.shape
    fetches[0].wait()
    fetches[1].wait()
    edge_ref[2 * units :, :LANES] = marks_of(target_ref[...], count_ref[...]).astype(BF)
    edge_ref[2 * units :, LANES:] = jnp.zeros((target_ref.shape[1], STRIP - LANES), BF)
    fetches[2].wait()
    rows_ref[:, :units, :] = jnp.swapaxes(hidden[...], 0, 1)
    fetches[3].wait()
    rows_ref[:, units:, :] = jnp.swapaxes(cell[...], 0, 1)
    tiles = edge_tiles(lambda y: rows_ref[y], row_count, 2 * units)
    for t, tile in enumerate(tiles):
        edge_ref[: 2 * units, t * LANES : (t + 1) * LANES] = tile


def marks_of(target, live_count):
    cap, sources = target.shape
    slot = lax.broadcasted_iota(jnp.int32, target.shape, 0)
    live = slot < live_count
    row = target // 2
    odd = target % 2 == 1
    picked = [jnp.where(live & odd, row, -1), jnp.where(live & ~odd, row, -1)]
    rows = jnp.concatenate([p.astype(F32) for p in picked], axis=0)
    lane = lane_of((2 * cap, LANES))
    which = lax.broadcasted_iota(jnp.int32, (2 * cap, LANES), 0)
    spread = (lane // 8 % cap == which % cap) & ((lane % 8 < 4) == (which < cap))
    return lax.dot_general(
        rows.astype(BF),
        jnp.where(spread, 1.0, 0.0).astype(BF),
        (((0,), (0,)), ((), ())),
        preferred_element_type=F32,
    )


def strips_of(own, from_left, from_right):
    near = lane_of(own.shape) % 8 < 4
    return jnp.where(near, from_left, own), jnp.where(near, own, from_right)


def full_strip(strip, above, below, has_above, has_below):
    lane = lane_of(above[:, :LANES].shape)
    from_above = (lane >= 8) & (lane < 32)
    from_below = (lane >= 32) & (lane < 56)
    parts = []
    for side in range(2):
        base = side * STRIP
        theirs = above[:, side * LANES : (side + 1) * LANES] * has_above
        parts.append(jnp.where(from_above, theirs, strip[:, base : base + LANES]))
        parts.append(strip[:, base + LANES : base + 2 * LANES])
        theirs = below[:, side * LANES : (side + 1) * LANES] * has_below
        parts.append(jnp.where(from_below, theirs, strip[:, base + 2 * LANES : base + STRIP]))
    return jnp.concatenate(parts, axis=1)


def strip_taps(strip):
    width = strip.shape[1]
    taps = []
    for a in range(3):
        for e in range(3):
            shift = 8 * (a - 1) + e - 1
            taps.append(strip if shift == 0 else pltpu.roll(strip, -shift % width, axis=1))
    return jnp.concatenate(taps, axis=0)


def patches_of(strip, tiles, first, last):
    channels = strip.shape[0]
    near = lane_of((channels, LANES)) % 8 < 4
    found = {}
    for i, t in enumerate(tiles):
        left = strip[:, i * LANES : (i + 1) * LANES]
        right = strip[:, (len(tiles) + i) * LANES : (len(tiles) + i + 1) * LANES]
        mixed = jnp.where(near, left, right)
        for r in range(max(first, 16 * t), min(last, 16 * t + 16)):
            found[r] = pltpu.roll(mixed, -(8 * (r % 16) + 4) % LANES, axis=1)
    return found


def store_patches(strip, patch_ref, first, last):
    for r, patch in patches_of(strip, range(STRIP // LANES), first, last).items():
        patch_ref[r] = patch


def store_three(ref, r, row, patch):
    channels = row.shape[0]
    lane = lane_of((channels, LANES))
    head, tail = row[:, :LANES], row[:, LANES:]
    ref[r, :channels, :LANES] = pltpu.roll(jnp.where(lane == LANES - 1, patch, head), 1, axis=1)
    ref[r, :channels, LANES:] = pltpu.roll(jnp.where(lane == LANES - 1, head, tail), 1, axis=1)
    ref[r, channels : 2 * channels, :] = row
    ref[r, 2 * channels :, :LANES] = pltpu.roll(jnp.where(lane == 0, tail, head), LANES - 1, axis=1)
    ref[r, 2 * channels :, LANES:] = pltpu.roll(jnp.where(lane == 0, patch, tail), LANES - 1, axis=1)


def row_taps(ref, r):
    channels = ref.shape[1]
    return ref[pl.ds(r - 1, 3)].reshape(3 * channels, ref.shape[2])


def matmul(weights, taps):
    return jnp.dot(weights, taps, preferred_element_type=F32)


def state_kernel(
    rows_ref, edge_ref, left_ref, right_ref, weight_ref, bias_ref,
    gates_hbm, strip_gates_ref, wide_bias_ref, strip_ref, mark_ref, gates, three, patches, sems,
):
    units = rows_ref.shape[1] // 2
    count = rows_ref.shape[0]
    wide_bias_ref[...] = jnp.broadcast_to(bias_ref[...], wide_bias_ref.shape)
    channels = 2 * units
    left, right = strips_of(edge_ref[:channels], left_ref[:channels], right_ref[:channels])
    strip_ref[:, :STRIP] = left
    strip_ref[:, STRIP:] = right
    near = lane_of(mark_ref.shape) % 8 < 4
    from_left = left_ref[channels:, :LANES].astype(F32)
    mark_ref[...] = jnp.where(near, from_left, right_ref[channels:, :LANES].astype(F32))
    strip = jnp.concatenate([left[:units], right[:units]], axis=1)
    strip_gates_ref[...] = matmul(weight_ref[...], strip_taps(strip))
    store_patches(strip, patches, PAD, count + PAD)
    for y in range(count):
        store_three(three, y + PAD, rows_ref[y, :units], patches[y + PAD])
    sends = pieces(gates, gates_hbm, sems)
    for y in range(1, count - 1):
        gates[y - 1] = matmul(weight_ref[...], row_taps(three, y + PAD))
        if y % PIECE == 0:
            sends[y // PIECE - 1].start()
    for send in sends:
        send.wait()


def pieces(source, target, sems):
    count = source.shape[0] // PIECE
    spots = [pl.ds(i * PIECE, PIECE) for i in range(count)]
    return [pltpu.make_async_copy(source.at[s], target.at[s], sems.at[i]) for i, s in enumerate(spots)]


def ends_of(strip):
    return jnp.concatenate([strip[:, t * LANES : (t + 1) * LANES] for t in (0, 2, 3, 5)], axis=1)


def edge_patches(strip, first, last, count):
    found = patches_of(strip, (0, 2), first, last)
    mirror = count + 2 * PAD - 1
    found.update(patches_of(strip, (0, 2), mirror - last + 1, mirror - first + 1))
    return found


def update(gates, memory):
    units = memory.shape[0]
    ingate = 0.5 * jnp.tanh(gates[:units]) + 0.5
    forget = 0.5 * jnp.tanh(gates[units : 2 * units]) + 0.5
    outgate = 0.5 * jnp.tanh(gates[2 * units : 3 * units]) + 0.5
    memory = forget * memory + ingate * jnp.tanh(gates[3 * units :])
    return outgate * jnp.tanh(memory), memory


def inner_kernel(
    gates_hbm, strip_gates_ref, rows_ref, strip_ref, forcing_ref, forcing_strip_ref,
    in_weight_ref, weight_ref, bias_ref,
    hidden_ref, cell_ref, sums_ref, first_ref, second_ref, memory_ref,
    gates, f_three, f_patches, f_gates, first, second, patches, memory, sems,
):
    units = rows_ref.shape[1] // 2
    count = rows_ref.shape[0]
    bias = bias_ref[...]
    fetches = pieces(gates_hbm, gates, sems)
    for fetch in fetches:
        fetch.start()

    strip = forcing_strip_ref[...]
    strip_forcing = matmul(in_weight_ref[...], strip_taps(strip)) + jnp.concatenate([bias] * 3, axis=1)
    store_patches(strip, f_patches, PAD, count + PAD)
    for y in range(count):
        store_three(f_three, y + PAD, forcing_ref[y], f_patches[y + PAD])

    strip_memory = strip_ref[units:].astype(F32)
    strip_hidden, strip_memory = update(strip_gates_ref[...] + strip_forcing, strip_memory)
    strip_hidden = strip_hidden.astype(BF)
    store_patches(strip_hidden, patches, PAD + 1, count + PAD - 1)

    def run(margin, body):
        stop = PAD + count - margin
        for start in range(PAD + margin, stop, BATCH):
            body(range(start, min(start + BATCH, stop)))

    def first_rows(group):
        for r in group:
            if (r - PAD - 1) % PIECE == 0:
                fetches[(r - PAD - 1) // PIECE].wait()
        sums = [matmul(in_weight_ref[...], row_taps(f_three, r)) + bias for r in group]
        states = [
            update(gates[r - PAD - 1] + s, rows_ref[r - PAD, units:].astype(F32)) for r, s in zip(group, sums)
        ]
        marks = [patches[r] for r in group]
        for r, s, (hidden, new), mark in zip(group, sums, states, marks):
            f_gates[r] = s
            memory[r] = new
            store_three(first, r, hidden.astype(BF), mark)

    run(1, first_rows)

    strip_gates = matmul(weight_ref[...], strip_taps(strip_hidden)) + strip_forcing
    strip_hidden, strip_memory = update(strip_gates, strip_memory)
    store_patches(strip_hidden.astype(BF), patches, PAD + 2, count + PAD - 2)

    def later(source, group):
        sums = [f_gates[r] + matmul(weight_ref[...], row_taps(source, r)) for r in group]
        return [update(s, memory[r]) for r, s in zip(group, sums)]

    def second_rows(group):
        states = later(first, group)
        marks = [patches[r] for r in group]
        for r, (hidden, new), mark in zip(group, states, marks):
            memory[r] = new
            store_three(second, r, hidden.astype(BF), mark)

    run(2, second_rows)

    def third_rows(group):
        for r, (hidden, new) in zip(group, later(second, group)):
            hidden_ref[r - PAD - 3] = hidden.astype(BF)
            cell_ref[r - PAD - 3] = new.astype(BF)

    run(3, third_rows)
    for i, r in enumerate(edge_rows(count, 1, 2)):
        sums_ref[i] = f_gates[r]
        first_ref[i] = first[r]
        memory_ref[i] = memory[r]
    for i, r in enumerate(edge_rows(count, 2, 2)):
        second_ref[i] = second[r]


def edge_rows(count, depth, many):
    top = [PAD + depth + i for i in range(many)]
    return top + [PAD + count - 1 - depth - (many - 1) + i for i in range(many)]


def edge_kernel(
    flag_ref, rows_ref, strip_ref, forcing_ref, forcing_strip_ref, above_ref, below_ref,
    in_weight_ref, weight_ref, bias_ref,
    inner_hidden_ref, inner_cell_ref, sums_ref, first_ref, second_ref, memory_ref,
    hidden_ref, cell_ref,
    f_three, three, first, second, h_rows, c_rows,
):
    units = rows_ref.shape[1] // 2
    count = rows_ref.shape[0]
    has_above = flag_ref[0].astype(F32)
    has_below = flag_ref[1].astype(F32)
    bf_above, bf_below = has_above.astype(BF), has_below.astype(BF)
    bias = bias_ref[...]

    channels = forcing_ref.shape[1]
    joined = jnp.concatenate([forcing_strip_ref[...], strip_ref[...]], axis=0)
    joined = ends_of(full_strip(joined, above_ref[3], below_ref[3], bf_above, bf_below))
    strip = joined[:channels]
    state_strip = joined[channels : channels + units]
    strip_forcing = matmul(in_weight_ref[...], strip_taps(strip)) + jnp.concatenate([bias] * 2, axis=1)
    strip_gates = strip_forcing + matmul(weight_ref[...], strip_taps(state_strip))
    patches = edge_patches(joined[: channels + units], 1, PAD + 2, count)

    def place(r, forcing, hidden):
        store_three(f_three, r, forcing, patches[r][:channels])
        store_three(three, r, hidden, patches[r][channels:])

    for i in range(3):
        ahead = above_ref[i, : channels + units] * bf_above
        place(1 + i, ahead[:channels], ahead[channels:])
        ahead = below_ref[i, : channels + units] * bf_below
        place(count + PAD + i, ahead[:channels], ahead[channels:])
    for r in edge_rows(count, 0, 2):
        place(r, forcing_ref[r - PAD], rows_ref[r - PAD, :units])

    lane = lane_of((units, strip.shape[1]))
    row_of_lane = (lane % LANES) // 8 + 32 * (lane // LANES % 2)
    keep = jnp.where(row_of_lane < PAD, has_above, 1.0)
    keep = jnp.where(row_of_lane >= PAD + count, has_below, keep)

    def kept(hidden, r):
        if r < PAD:
            hidden = hidden * has_above
        elif r >= PAD + count:
            hidden = hidden * has_below
        return hidden.astype(BF)

    strip_memory = joined[channels + units :].astype(F32)
    strip_hidden, strip_memory = update(strip_gates, strip_memory)
    strip_hidden = (strip_hidden * keep).astype(BF)
    marks = edge_patches(strip_hidden, 2, PAD + 1, count)

    sums, memory = {}, {}
    for i, r in enumerate(edge_rows(count, 1, 2)):
        sums[r] = sums_ref[i]
        memory[r] = memory_ref[i]
    group = edge_rows(count, -2, 3)
    cells = channels + units
    olds = [above_ref[1, cells:], above_ref[2, cells:], rows_ref[0, units:]]
    olds += [rows_ref[count - 1, units:], below_ref[0, cells:], below_ref[1, cells:]]
    for r, old in zip(group, olds):
        sums[r] = matmul(in_weight_ref[...], row_taps(f_three, r)) + bias
        first_gates = sums[r] + matmul(weight_ref[...], row_taps(three, r))
        hidden, memory[r] = update(first_gates, old.astype(F32))
        store_three(first, r, kept(hidden, r), marks[r])
    for i, r in enumerate(edge_rows(count, 1, 2)):
        first[r] = first_ref[i]

    strip_gates = matmul(weight_ref[...], strip_taps(strip_hidden)) + strip_forcing
    strip_hidden, strip_memory = update(strip_gates, strip_memory)
    strip_hidden = (strip_hidden * keep).astype(BF)
    marks = edge_patches(strip_hidden, 3, PAD + 2, count)
    for r in edge_rows(count, -1, 3):
        hidden, memory[r] = update(sums[r] + matmul(weight_ref[...], row_taps(first, r)), memory[r])
        store_three(second, r, kept(hidden, r), marks[r])
    for i, r in enumerate(edge_rows(count, 2, 2)):
        second[r] = second_ref[i]

    for r in edge_rows(count, 0, 3):
        hidden, new = update(sums[r] + matmul(weight_ref[...], row_taps(second, r)), memory[r])
        h_rows[r - PAD] = hidden.astype(BF)
        c_rows[r - PAD] = new.astype(BF)
    h_rows[3 : count - 3] = inner_hidden_ref[...]
    c_rows[3 : count - 3] = inner_cell_ref[...]
    hidden_ref[...] = jnp.swapaxes(h_rows[...], 0, 1)
    cell_ref[...] = jnp.swapaxes(c_rows[...], 0, 1)


def beside(incoming_ref, mark_ref, row_count, channels):
    sources = incoming_ref.shape[0]
    base = incoming_ref.shape[1] - channels // 2
    lane = lane_of((channels // 2, LANES))
    group_lanes = 8 * ((base // channels) % 16)
    tiles = [[jnp.zeros((channels // 2, LANES), F32) for _ in range(2)] for _ in range(STRIP // LANES)]
    for start in range(0, row_count, 16):
        sums = [jnp.zeros((channels // 2, LANES), F32) for _ in range(16)]
        for p in range(sources):
            edges = incoming_ref[p, base:, :].astype(F32)
            mark = jnp.broadcast_to(mark_ref[p : p + 1, :], edges.shape)
            for i in range(16):
                sums[i] = sums[i] + jnp.where(mark == float(start + i), edges, 0.0)
        for i in range(16):
            total = sums[i] + pltpu.roll(sums[i], LANES - 8, axis=1)
            total = total + pltpu.roll(total, LANES - 16, axis=1)
            r = start + i + PAD
            for part in range(2):
                moved = pltpu.roll(total, (8 * (r % 16) - part * group_lanes) % LANES, axis=1)
                tiles[r // 16][part] = jnp.where(lane // 8 == r % 16, moved, tiles[r // 16][part])
    halves = [jnp.concatenate([t[part] for t in tiles], axis=1) for part in range(2)]
    return jnp.concatenate(halves, axis=0).astype(BF)


def scatter_kernel(
    target_ref, count_ref, incoming_ref, mark_ref, state_ref, state_strip_ref,
    rows_ref, strip_ref, up_ref, down_ref, total,
):
    cap, sources = target_ref.shape
    row_count, channels, width = rows_ref.shape
    width = width // 2
    spare = 2 * row_count
    total[...] = jnp.zeros(total.shape, F32)
    for p in range(sources):
        live = count_ref[0, p]
        for s in range(cap):
            block = jnp.where(s < live, target_ref[s, p], spare)
            total[block] = total[block] + incoming_ref[p, s * channels : (s + 1) * channels, :].astype(F32)
    for y in range(row_count):
        rows_ref[y, :, :width] = total[2 * y].astype(BF)
        rows_ref[y, :, width:] = total[2 * y + 1].astype(BF)
    own = jnp.concatenate(edge_tiles(lambda y: rows_ref[y], row_count, channels), axis=1)
    others = beside(incoming_ref, mark_ref, row_count, channels)
    left, right = strips_of(own, others, others)
    strip_ref[:, :STRIP] = left
    strip_ref[:, STRIP:] = right
    for ref, first, tile in ((up_ref, 0, 0), (down_ref, row_count - 3, 2)):
        ref[:3, :channels] = rows_ref[first : first + 3]
        ref[:3, channels:] = state_ref[first : first + 3]
        spot = tile * LANES
        ref[3, :channels, :LANES] = left[:, spot : spot + LANES]
        ref[3, :channels, LANES:] = right[:, spot : spot + LANES]
        ref[3, channels:, :LANES] = state_strip_ref[:, spot : spot + LANES]
        ref[3, channels:, LANES:] = state_strip_ref[:, STRIP + spot : STRIP + spot + LANES]


def around(count):
    return [(i, (i + 1) % count) for i in range(count)]


def back(count):
    return [((i + 1) % count, i) for i in range(count)]


def exchange_columns(edge):
    count = lax.axis_size("lon")
    from_left = lax.ppermute(edge, "lon", around(count))
    from_right = lax.ppermute(edge, "lon", back(count))
    return from_left, from_right


def exchange_rows(up, down):
    count = lax.axis_size("lat")
    from_above = lax.ppermute(down, "lat", around(count))
    from_below = lax.ppermute(up, "lat", back(count))
    return from_above, from_below


def on_device(
    satellite_blocks,
    slot_source,
    slot_weight,
    slot_target,
    tile_counts,
    gate_input_weight,
    gate_state_weight,
    gate_bias,
    hidden_init,
    cell_init,
):
    _, tiles, cap, band, block = slot_weight.shape
    channels = satellite_blocks.shape[1]
    units, row_count, column_count = hidden_init.shape
    gates = gate_bias.shape[0]
    slots = tiles * cap
    half = jnp.where(jnp.arange(gates) < 3 * units, 0.5, 1.0)
    in_weight = gate_input_weight * half[:, None].astype(BF)
    state_weight = gate_state_weight * half[:, None].astype(BF)
    bias = (gate_bias * half)[:, None]
    lat = lax.axis_index("lat")
    flags = jnp.stack([lat > 0, lat < lax.axis_size("lat") - 1]).astype(jnp.int32)

    ring = lax.axis_size("lon")
    height = cap * channels + channels // 2
    message = jax.ShapeDtypeStruct((tiles, height, block), BF)
    groups = tiles // ring
    outgoing = pl.pallas_call(
        functools.partial(gather_kernel, ring),
        out_shape=pltpu.HBM(message.shape, BF),
        in_specs=[pl.BlockSpec(memory_space=pl.ANY)] * 3,
        out_specs=pl.BlockSpec(memory_space=pl.ANY),
        scratch_shapes=[
            pltpu.VMEM(satellite_blocks.shape, BF),
            pltpu.VMEM((slots, band, block), BF),
            pltpu.VMEM(message.shape, BF),
            pltpu.SMEM((cap, tiles), jnp.int32),
            pltpu.SemaphoreType.DMA,
            pltpu.SemaphoreType.DMA,
            pltpu.SemaphoreType.DMA((groups,)),
            pltpu.SemaphoreType.DMA((groups,)),
        ],
        compiler_params=pltpu.CompilerParams(vmem_limit_bytes=8 * 2**20),
        name="gather_band",
    )(in_hbm(slot_source[0].T), in_hbm(satellite_blocks), in_hbm(slot_weight.reshape(slots, band, block)))
    incoming = lax.all_to_all(outgoing, ("lat", "lon"), split_axis=0, concat_axis=0, tiled=True)

    rows, edge = pl.pallas_call(
        prepare_kernel,
        out_shape=(
            jax.ShapeDtypeStruct((row_count, 2 * units, column_count), BF),
            jax.ShapeDtypeStruct((2 * units + tiles, STRIP), BF),
        ),
        in_specs=[pl.BlockSpec(memory_space=pl.ANY)] * 4,
        out_specs=tuple(whole(2)),
        scratch_shapes=[
            pltpu.VMEM(hidden_init.shape, BF),
            pltpu.VMEM(cell_init.shape, BF),
            pltpu.VMEM((cap, tiles), jnp.int32),
            pltpu.VMEM((1, tiles), jnp.int32),
            pltpu.SemaphoreType.DMA((4,)),
        ],
        compiler_params=pltpu.CompilerParams(vmem_limit_bytes=8 * 2**20),
        name="prepare",
    )(in_hbm(hidden_init), in_hbm(cell_init), in_hbm(slot_target[0].T), in_hbm(tile_counts))
    from_left, from_right = exchange_columns(edge)
    padded = row_count + 8
    inside = (row_count - 2, gates, column_count)
    parts = inside[0] // PIECE
    state_gates, strip_gates, bias, strip, marks = call(
        state_kernel,
        [
            pltpu.HBM(inside, F32),
            jax.ShapeDtypeStruct((gates, 2 * STRIP), F32),
            jax.ShapeDtypeStruct((gates, column_count), F32),
            jax.ShapeDtypeStruct((2 * units, 2 * STRIP), BF),
            jax.ShapeDtypeStruct((tiles, LANES), F32),
        ],
        6, 0,
        [
            pltpu.VMEM(inside, F32),
            pltpu.VMEM((padded, 3 * units, column_count), BF),
            pltpu.VMEM((padded, units, LANES), BF),
            pltpu.SemaphoreType.DMA((parts,)),
        ],
        "state_gates", 2 * gates * 9 * units * row_count * column_count,
        (rows, edge, from_left, from_right, state_weight, bias), 16,
        out_specs=[pl.BlockSpec(memory_space=pl.ANY)] + whole(4),
    )
    incoming, state_gates, strip_gates, bias, in_weight = lax.optimization_barrier(
        (incoming, state_gates, strip_gates, bias, in_weight)
    )

    ends = jax.ShapeDtypeStruct((4, channels + 2 * units, column_count), BF)
    forcing, forcing_strip, up, down = call(
        scatter_kernel,
        [
            jax.ShapeDtypeStruct((row_count, channels, column_count), BF),
            jax.ShapeDtypeStruct((channels, 2 * STRIP), BF),
            ends,
            ends,
        ],
        4, 2,
        [pltpu.VMEM((2 * row_count + 1, channels, block), F32)],
        "scatter_add", slots * channels * block,
        (slot_target[0].T, tile_counts, incoming, marks, rows, strip),
    )
    above, below = exchange_rows(up, down)
    inner_rows = jax.ShapeDtypeStruct((row_count - 6, units, column_count), BF)
    threes = jax.ShapeDtypeStruct((4, 3 * units, column_count), BF)
    inner = call(
        inner_kernel,
        [
            inner_rows,
            inner_rows,
            jax.ShapeDtypeStruct((4, gates, column_count), F32),
            threes,
            threes,
            jax.ShapeDtypeStruct((4, units, column_count), F32),
        ],
        9, 0,
        [
            pltpu.VMEM(inside, F32),
            pltpu.VMEM((padded, 3 * channels, column_count), BF),
            pltpu.VMEM((padded, channels, LANES), BF),
            pltpu.VMEM((padded, gates, column_count), F32),
            pltpu.VMEM((padded, 3 * units, column_count), BF),
            pltpu.VMEM((padded, 3 * units, column_count), BF),
            pltpu.VMEM((padded, units, LANES), BF),
            pltpu.VMEM((padded, units, column_count), F32),
            pltpu.SemaphoreType.DMA((parts,)),
        ],
        "inner", 2 * gates * 9 * (channels + 2 * units) * row_count * column_count,
        (in_hbm(state_gates), strip_gates, rows, strip, forcing, forcing_strip, in_weight, state_weight, bias), 24,
        in_specs=[pl.BlockSpec(memory_space=pl.ANY)] + whole(8),
    )
    out = jax.ShapeDtypeStruct((units, row_count, column_count), BF)
    return call(
        edge_kernel,
        [out, out],
        15, 1,
        [
            pltpu.VMEM((padded, 3 * channels, column_count), BF),
            pltpu.VMEM((padded, 3 * units, column_count), BF),
            pltpu.VMEM((padded, 3 * units, column_count), BF),
            pltpu.VMEM((padded, 3 * units, column_count), BF),
            pltpu.VMEM((row_count, units, column_count), BF),
            pltpu.VMEM((row_count, units, column_count), BF),
        ],
        "edges", 2 * gates * 9 * (channels + 3 * units) * 6 * column_count,
        (flags, rows, strip, forcing, forcing_strip, above, below, in_weight, state_weight, bias, *inner), 16,
    )


def solution(mesh):
    placed = (
        P(("lat", "lon"), None, None),
        P(("lat", "lon"), None, None),
        P(("lat", "lon"), None, None, None, None),
        P(("lat", "lon"), None, None),
        P(("lat", "lon"), None),
        P(),
        P(),
        P(),
        P(None, "lat", "lon"),
        P(None, "lat", "lon"),
    )
    return jax.shard_map(
        on_device,
        mesh=mesh,
        in_specs=placed,
        out_specs=(P(None, "lat", "lon"), P(None, "lat", "lon")),
        check_vma=False,
    )
```

```python
import functools

import jax
import jax.numpy as jnp
from jax import lax
from jax.experimental import pallas as pl
from jax.experimental.pallas import tpu as pltpu
from jax.sharding import PartitionSpec as P

STEPS = 3
PAD = 4
LANES = 128
STRIP = 3 * LANES
BATCH = 2
PIECE = 6
BF = jnp.bfloat16
F32 = jnp.float32


def lane_of(shape):
    return lax.broadcasted_iota(jnp.int32, shape, len(shape) - 1)


def whole(count):
    return [pl.BlockSpec(memory_space=pltpu.VMEM)] * count


def in_hbm(x):
    return pltpu.with_memory_space_constraint(x, pltpu.HBM)


def scalars(count):
    return [pl.BlockSpec(memory_space=pltpu.SMEM)] * count


def call(
    kernel, outs, ins, scalar_count, scratch, name, flops, args, mib=8, in_specs=None, out_specs=None
):
    nbytes = sum(a.size * a.dtype.itemsize for a in args)
    return pl.pallas_call(
        kernel,
        out_shape=tuple(outs),
        in_specs=in_specs or scalars(scalar_count) + whole(ins),
        out_specs=tuple(out_specs or whole(len(outs))),
        scratch_shapes=scratch,
        compiler_params=pltpu.CompilerParams(vmem_limit_bytes=mib * 2**20),
        cost_estimate=pl.CostEstimate(flops=flops, bytes_accessed=nbytes, transcendentals=0),
        name=name,
    )(*args)


def edge_tiles(row_of, row_count, channels):
    lane = lane_of((channels, LANES))
    tiles = [jnp.zeros((channels, LANES), BF) for _ in range(STRIP // LANES)]
    for y in range(row_count):
        row = row_of(y)
        both = jnp.where(lane < 64, row[:, :LANES], row[:, -LANES:])
        r = y + PAD
        place = r % 16
        turned = pltpu.roll(both, (8 * place + 4) % LANES, axis=1)
        tiles[r // 16] = jnp.where(lane // 8 == place, turned, tiles[r // 16])
    return tiles


def gather_kernel(
    ring, source_hbm, blocks_hbm, weight_hbm, out_hbm, blocks, weights, out, source_ref, source_sem, block_sem, weight_sem, out_sem
):
    cap, tiles = source_ref.shape
    band, width = weights.shape[1:]
    channels = blocks.shape[1]
    groups = tiles // ring
    share = ring * cap
    fetch = pltpu.make_async_copy(blocks_hbm, blocks, block_sem)
    fetch.start()
    places = pltpu.make_async_copy(source_hbm, source_ref, source_sem)
    places.start()
    parts = [
        pltpu.make_async_copy(
            weight_hbm.at[pl.ds(g * share, share)], weights.at[pl.ds(g * share, share)], weight_sem.at[g]
        )
        for g in range(groups)
    ]
    for part in parts:
        part.start()
    offset = lax.broadcasted_iota(jnp.int32, (band, width), 0) - band // 2
    spot = lane_of((band, width)) + offset
    inside = (spot >= 0) & (spot < width)
    lane = lane_of((channels, width))
    near = lane_of((channels // 2, width)) % 8 < 4
    places.wait()
    fetch.wait()
    sends = []
    for g in range(groups):
        parts[g].wait()
        folded = []
        for j in range(ring):
            q = g * ring + j
            for s in range(cap):
                block = blocks[source_ref[s, q]]
                factor = jnp.where(inside, weights[q * cap + s].astype(F32), 0.0)
                total = jnp.zeros((channels, width), F32)
                for k in range(band):
                    moved = block if k == band // 2 else pltpu.roll(block, (band // 2 - k) % width, axis=1)
                    total = total + factor[k : k + 1, :] * moved.astype(F32)
                rounded = total.astype(BF)
                out[q, s * channels : (s + 1) * channels, :] = rounded
        for j in range(ring):
            edges = jnp.zeros((channels, width), BF)
            for s in range(cap):
                rounded = out[g * ring + j, s * channels : (s + 1) * channels, :]
                edges = jnp.where(lane // 8 == s, pltpu.roll(rounded, 8 * s + 4, axis=1), edges)
            wide = edges.astype(F32)
            folded.append(wide[: channels // 2] + pltpu.roll(wide[channels // 2 :], 8 * cap, axis=1))
        for j in range(ring):
            both = jnp.where(near, folded[j - 1], folded[(j + 1) % ring])
            out[g * ring + j, cap * channels :, :] = both.astype(BF)
        send = pltpu.make_async_copy(
            out.at[pl.ds(g * ring, ring)], out_hbm.at[pl.ds(g * ring, ring)], out_sem.at[g]
        )
        send.start()
        sends.append(send)
    for send in sends:
        send.wait()


def prepare_kernel(
    hidden_hbm, cell_hbm, target_hbm, count_hbm, rows_ref, edge_ref, hidden, cell, target_ref, count_ref, sems
):
    fetches = [
        pltpu.make_async_copy(source, target, sems.at[i])
        for i, (source, target) in enumerate(
            [(target_hbm, target_ref), (count_hbm, count_ref), (hidden_hbm, hidden), (cell_hbm, cell)]
        )
    ]
    for fetch in fetches:
        fetch.start()
    units, row_count, _ = hidden.shape
    fetches[0].wait()
    fetches[1].wait()
    edge_ref[2 * units :, :LANES] = marks_of(target_ref[...], count_ref[...]).astype(BF)
    edge_ref[2 * units :, LANES:] = jnp.zeros((target_ref.shape[1], STRIP - LANES), BF)
    fetches[2].wait()
    rows_ref[:, :units, :] = jnp.swapaxes(hidden[...], 0, 1)
    fetches[3].wait()
    rows_ref[:, units:, :] = jnp.swapaxes(cell[...], 0, 1)
    tiles = edge_tiles(lambda y: rows_ref[y], row_count, 2 * units)
    for t, tile in enumerate(tiles):
        edge_ref[: 2 * units, t * LANES : (t + 1) * LANES] = tile


def marks_of(target, live_count):
    cap, sources = target.shape
    slot = lax.broadcasted_iota(jnp.int32, target.shape, 0)
    live = slot < live_count
    row = target // 2
    odd = target % 2 == 1
    picked = [jnp.where(live & odd, row, -1), jnp.where(live & ~odd, row, -1)]
    rows = jnp.concatenate([p.astype(F32) for p in picked], axis=0)
    lane = lane_of((2 * cap, LANES))
    which = lax.broadcasted_iota(jnp.int32, (2 * cap, LANES), 0)
    spread = (lane // 8 % cap == which % cap) & ((lane % 8 < 4) == (which < cap))
    return lax.dot_general(
        rows.astype(BF),
        jnp.where(spread, 1.0, 0.0).astype(BF),
        (((0,), (0,)), ((), ())),
        preferred_element_type=F32,
    )


def strips_of(own, from_left, from_right):
    near = lane_of(own.shape) % 8 < 4
    return jnp.where(near, from_left, own), jnp.where(near, own, from_right)


def pack_strips(left, right):
    return jnp.where(lane_of(left.shape) < 64, left, pltpu.roll(right, 64, axis=1))


def full_strip(strip, above, below):
    lane = lane_of(above.shape)
    from_above = (lane >= 8) & (lane < 32)
    from_below = (lane >= 32) & (lane < 56)
    parts = []
    for side in range(2):
        base = side * STRIP
        if side:
            above, below = pltpu.roll(above, 64, axis=1), pltpu.roll(below, 64, axis=1)
        parts.append(jnp.where(from_above, above, strip[:, base : base + LANES]))
        parts.append(strip[:, base + LANES : base + 2 * LANES])
        parts.append(jnp.where(from_below, below, strip[:, base + 2 * LANES : base + STRIP]))
    return jnp.concatenate(parts, axis=1)


def strip_taps(strip):
    width = strip.shape[1]
    taps = []
    for a in range(3):
        for e in range(3):
            shift = 8 * (a - 1) + e - 1
            taps.append(strip if shift == 0 else pltpu.roll(strip, -shift % width, axis=1))
    return jnp.concatenate(taps, axis=0)


def patches_of(strip, tiles, first, last):
    channels = strip.shape[0]
    near = lane_of((channels, LANES)) % 8 < 4
    found = {}
    for i, t in enumerate(tiles):
        left = strip[:, i * LANES : (i + 1) * LANES]
        right = strip[:, (len(tiles) + i) * LANES : (len(tiles) + i + 1) * LANES]
        mixed = jnp.where(near, left, right)
        for r in range(max(first, 16 * t), min(last, 16 * t + 16)):
            found[r] = pltpu.roll(mixed, -(8 * (r % 16) + 4) % LANES, axis=1)
    return found


def store_patches(strip, patch_ref, first, last):
    for r, patch in patches_of(strip, range(STRIP // LANES), first, last).items():
        patch_ref[r] = patch


def store_three(ref, r, row, patch):
    channels = row.shape[0]
    lane = lane_of((channels, LANES))
    head, tail = row[:, :LANES], row[:, LANES:]
    ref[r, :channels, :LANES] = pltpu.roll(jnp.where(lane == LANES - 1, patch, head), 1, axis=1)
    ref[r, :channels, LANES:] = pltpu.roll(jnp.where(lane == LANES - 1, head, tail), 1, axis=1)
    ref[r, channels : 2 * channels, :] = row
    ref[r, 2 * channels :, :LANES] = pltpu.roll(jnp.where(lane == 0, tail, head), LANES - 1, axis=1)
    ref[r, 2 * channels :, LANES:] = pltpu.roll(jnp.where(lane == 0, patch, tail), LANES - 1, axis=1)


def row_taps(ref, r):
    channels = ref.shape[1]
    return ref[pl.ds(r - 1, 3)].reshape(3 * channels, ref.shape[2])


def matmul(weights, taps):
    return jnp.dot(weights, taps, preferred_element_type=F32)


def state_kernel(
    rows_ref, edge_ref, left_ref, right_ref, weight_ref, bias_ref,
    gates_hbm, strip_gates_ref, wide_bias_ref, strip_ref, mark_ref, up_ref, down_ref,
    gates, three, patches, sems,
):
    units = rows_ref.shape[1] // 2
    count = rows_ref.shape[0]
    wide_bias_ref[...] = jnp.broadcast_to(bias_ref[...], wide_bias_ref.shape)
    channels = 2 * units
    left, right = strips_of(edge_ref[:channels], left_ref[:channels], right_ref[:channels])
    strip_ref[:, :STRIP] = left
    strip_ref[:, STRIP:] = right
    for ref, hidden_row, cell_row in ((up_ref, 0, 0), (down_ref, count - 3, count - 2)):
        ref[:3] = rows_ref[hidden_row : hidden_row + 3, :units]
        ref[3:] = rows_ref[cell_row : cell_row + 2, units:]
    near = lane_of(mark_ref.shape) % 8 < 4
    from_left = left_ref[channels:, :LANES].astype(F32)
    mark_ref[...] = jnp.where(near, from_left, right_ref[channels:, :LANES].astype(F32))
    strip = jnp.concatenate([left[:units], right[:units]], axis=1)
    strip_gates_ref[...] = matmul(weight_ref[...], strip_taps(strip))
    store_patches(strip, patches, PAD, count + PAD)
    for y in range(count):
        store_three(three, y + PAD, rows_ref[y, :units], patches[y + PAD])
    sends = pieces(gates, gates_hbm, sems)
    for y in range(1, count - 1):
        gates[y - 1] = matmul(weight_ref[...], row_taps(three, y + PAD))
        if y % PIECE == 0:
            sends[y // PIECE - 1].start()
    for send in sends:
        send.wait()


def pieces(source, target, sems):
    count = source.shape[0] // PIECE
    spots = [pl.ds(i * PIECE, PIECE) for i in range(count)]
    return [pltpu.make_async_copy(source.at[s], target.at[s], sems.at[i]) for i, s in enumerate(spots)]


def ends_of(strip):
    return jnp.concatenate([strip[:, t * LANES : (t + 1) * LANES] for t in (0, 2, 3, 5)], axis=1)


def edge_patches(strip, first, last, count):
    found = patches_of(strip, (0, 2), first, last)
    mirror = count + 2 * PAD - 1
    found.update(patches_of(strip, (0, 2), mirror - last + 1, mirror - first + 1))
    return found


def update(gates, memory):
    units = memory.shape[0]
    ingate = 0.5 * jnp.tanh(gates[:units]) + 0.5
    forget = 0.5 * jnp.tanh(gates[units : 2 * units]) + 0.5
    outgate = 0.5 * jnp.tanh(gates[2 * units : 3 * units]) + 0.5
    memory = forget * memory + ingate * jnp.tanh(gates[3 * units :])
    return outgate * jnp.tanh(memory), memory


def inner_kernel(
    gates_hbm, strip_gates_ref, rows_ref, strip_ref, forcing_ref, forcing_strip_ref,
    in_weight_ref, weight_ref, bias_ref,
    hidden_ref, cell_ref, sums_ref, first_ref, second_ref, memory_ref,
    gates, f_three, f_patches, f_gates, first, second, patches, memory, sems,
):
    units = rows_ref.shape[1] // 2
    count = rows_ref.shape[0]
    bias = bias_ref[...]
    fetches = pieces(gates_hbm, gates, sems)
    for fetch in fetches:
        fetch.start()

    strip = forcing_strip_ref[...]
    strip_forcing = matmul(in_weight_ref[...], strip_taps(strip)) + jnp.concatenate([bias] * 3, axis=1)
    store_patches(strip, f_patches, PAD, count + PAD)
    for y in range(count):
        store_three(f_three, y + PAD, forcing_ref[y], f_patches[y + PAD])

    strip_memory = strip_ref[units:].astype(F32)
    strip_hidden, strip_memory = update(strip_gates_ref[...] + strip_forcing, strip_memory)
    strip_hidden = strip_hidden.astype(BF)
    store_patches(strip_hidden, patches, PAD + 1, count + PAD - 1)

    def run(margin, body):
        stop = PAD + count - margin
        for start in range(PAD + margin, stop, BATCH):
            body(range(start, min(start + BATCH, stop)))

    def first_rows(group):
        for r in group:
            if (r - PAD - 1) % PIECE == 0:
                fetches[(r - PAD - 1) // PIECE].wait()
        sums = [matmul(in_weight_ref[...], row_taps(f_three, r)) + bias for r in group]
        states = [
            update(gates[r - PAD - 1] + s, rows_ref[r - PAD, units:].astype(F32)) for r, s in zip(group, sums)
        ]
        marks = [patches[r] for r in group]
        for r, s, (hidden, new), mark in zip(group, sums, states, marks):
            f_gates[r] = s
            memory[r] = new
            store_three(first, r, hidden.astype(BF), mark)

    run(1, first_rows)

    strip_gates = matmul(weight_ref[...], strip_taps(strip_hidden)) + strip_forcing
    strip_hidden, strip_memory = update(strip_gates, strip_memory)
    store_patches(strip_hidden.astype(BF), patches, PAD + 2, count + PAD - 2)

    def later(source, group):
        sums = [f_gates[r] + matmul(weight_ref[...], row_taps(source, r)) for r in group]
        return [update(s, memory[r]) for r, s in zip(group, sums)]

    def second_rows(group):
        states = later(first, group)
        marks = [patches[r] for r in group]
        for r, (hidden, new), mark in zip(group, states, marks):
            memory[r] = new
            store_three(second, r, hidden.astype(BF), mark)

    run(2, second_rows)

    def third_rows(group):
        for r, (hidden, new) in zip(group, later(second, group)):
            hidden_ref[r - PAD - 3] = hidden.astype(BF)
            cell_ref[r - PAD - 3] = new.astype(BF)

    run(3, third_rows)
    for i, r in enumerate(edge_rows(count, 1, 2)):
        sums_ref[i] = f_gates[r]
        first_ref[i] = first[r]
        memory_ref[i] = memory[r]
    for i, r in enumerate(edge_rows(count, 2, 2)):
        second_ref[i] = second[r]


def edge_rows(count, depth, many):
    top = [PAD + depth + i for i in range(many)]
    return top + [PAD + count - 1 - depth - (many - 1) + i for i in range(many)]


def edge_kernel(
    flag_ref, rows_ref, strip_ref, forcing_ref, forcing_strip_ref,
    above_ref, below_ref, f_above_ref, f_below_ref,
    in_weight_ref, weight_ref, bias_ref,
    inner_hidden_ref, inner_cell_ref, sums_ref, first_ref, second_ref, memory_ref,
    hidden_ref, cell_ref,
    f_three, three, first, second, h_rows, c_rows,
):
    units = rows_ref.shape[1] // 2
    count = rows_ref.shape[0]
    has_above = flag_ref[0].astype(F32)
    has_below = flag_ref[1].astype(F32)
    bf_above, bf_below = has_above.astype(BF), has_below.astype(BF)
    bias = bias_ref[...]

    channels = forcing_ref.shape[1]
    joined = jnp.concatenate([forcing_strip_ref[...], strip_ref[...]], axis=0)

    def strips_in(ref, present):
        packed = ref[3 * channels :] * present
        return jnp.concatenate([packed[:, :LANES], packed[channels:, LANES:]], axis=0)

    joined = full_strip(joined, strips_in(f_above_ref, bf_above), strips_in(f_below_ref, bf_below))
    joined = ends_of(joined)
    strip = joined[:channels]
    state_strip = joined[channels : channels + units]
    strip_forcing = matmul(in_weight_ref[...], strip_taps(strip)) + jnp.concatenate([bias] * 2, axis=1)
    strip_gates = strip_forcing + matmul(weight_ref[...], strip_taps(state_strip))
    patches = edge_patches(joined[: channels + units], 1, PAD + 2, count)

    def place(r, forcing, hidden):
        store_three(f_three, r, forcing, patches[r][:channels])
        store_three(three, r, hidden, patches[r][channels:])

    for i in range(3):
        line = slice(i * channels, (i + 1) * channels)
        place(1 + i, f_above_ref[line] * bf_above, above_ref[i] * bf_above)
        place(count + PAD + i, f_below_ref[line] * bf_below, below_ref[i] * bf_below)
    for r in edge_rows(count, 0, 2):
        place(r, forcing_ref[r - PAD], rows_ref[r - PAD, :units])

    lane = lane_of((units, strip.shape[1]))
    row_of_lane = (lane % LANES) // 8 + 32 * (lane // LANES % 2)
    keep = jnp.where(row_of_lane < PAD, has_above, 1.0)
    keep = jnp.where(row_of_lane >= PAD + count, has_below, keep)

    def kept(hidden, r):
        if r < PAD:
            hidden = hidden * has_above
        elif r >= PAD + count:
            hidden = hidden * has_below
        return hidden.astype(BF)

    strip_memory = joined[channels + units :].astype(F32)
    strip_hidden, strip_memory = update(strip_gates, strip_memory)
    strip_hidden = (strip_hidden * keep).astype(BF)
    marks = edge_patches(strip_hidden, 2, PAD + 1, count)

    sums, memory = {}, {}
    for i, r in enumerate(edge_rows(count, 1, 2)):
        sums[r] = sums_ref[i]
        memory[r] = memory_ref[i]
    group = edge_rows(count, -2, 3)
    olds = [above_ref[3], above_ref[4], rows_ref[0, units:]]
    olds += [rows_ref[count - 1, units:], below_ref[3], below_ref[4]]
    for r, old in zip(group, olds):
        sums[r] = matmul(in_weight_ref[...], row_taps(f_three, r)) + bias
        first_gates = sums[r] + matmul(weight_ref[...], row_taps(three, r))
        hidden, memory[r] = update(first_gates, old.astype(F32))
        store_three(first, r, kept(hidden, r), marks[r])
    for i, r in enumerate(edge_rows(count, 1, 2)):
        first[r] = first_ref[i]

    strip_gates = matmul(weight_ref[...], strip_taps(strip_hidden)) + strip_forcing
    strip_hidden, strip_memory = update(strip_gates, strip_memory)
    strip_hidden = (strip_hidden * keep).astype(BF)
    marks = edge_patches(strip_hidden, 3, PAD + 2, count)
    for r in edge_rows(count, -1, 3):
        hidden, memory[r] = update(sums[r] + matmul(weight_ref[...], row_taps(first, r)), memory[r])
        store_three(second, r, kept(hidden, r), marks[r])
    for i, r in enumerate(edge_rows(count, 2, 2)):
        second[r] = second_ref[i]

    for r in edge_rows(count, 0, 3):
        hidden, new = update(sums[r] + matmul(weight_ref[...], row_taps(second, r)), memory[r])
        h_rows[r - PAD] = hidden.astype(BF)
        c_rows[r - PAD] = new.astype(BF)
    h_rows[3 : count - 3] = inner_hidden_ref[...]
    c_rows[3 : count - 3] = inner_cell_ref[...]
    hidden_ref[...] = jnp.swapaxes(h_rows[...], 0, 1)
    cell_ref[...] = jnp.swapaxes(c_rows[...], 0, 1)


def beside(incoming_ref, mark_ref, row_count, channels):
    sources = incoming_ref.shape[0]
    base = incoming_ref.shape[1] - channels // 2
    lane = lane_of((channels // 2, LANES))
    group_lanes = 8 * ((base // channels) % 16)
    tiles = [[jnp.zeros((channels // 2, LANES), F32) for _ in range(2)] for _ in range(STRIP // LANES)]
    for start in range(0, row_count, 16):
        sums = [jnp.zeros((channels // 2, LANES), F32) for _ in range(16)]
        for p in range(sources):
            edges = incoming_ref[p, base:, :].astype(F32)
            mark = jnp.broadcast_to(mark_ref[p : p + 1, :], edges.shape)
            for i in range(16):
                sums[i] = sums[i] + jnp.where(mark == float(start + i), edges, 0.0)
        for i in range(16):
            total = sums[i] + pltpu.roll(sums[i], LANES - 8, axis=1)
            total = total + pltpu.roll(total, LANES - 16, axis=1)
            r = start + i + PAD
            for part in range(2):
                moved = pltpu.roll(total, (8 * (r % 16) - part * group_lanes) % LANES, axis=1)
                tiles[r // 16][part] = jnp.where(lane // 8 == r % 16, moved, tiles[r // 16][part])
    halves = [jnp.concatenate([t[part] for t in tiles], axis=1) for part in range(2)]
    return jnp.concatenate(halves, axis=0).astype(BF)


def scatter_kernel(
    target_ref, count_ref, incoming_ref, mark_ref, state_strip_ref,
    rows_ref, strip_ref, up_ref, down_ref, total,
):
    cap, sources = target_ref.shape
    row_count, channels, width = rows_ref.shape
    width = width // 2
    spare = 2 * row_count
    total[...] = jnp.zeros(total.shape, F32)
    for p in range(sources):
        live = count_ref[0, p]
        for s in range(cap):
            block = jnp.where(s < live, target_ref[s, p], spare)
            total[block] = total[block] + incoming_ref[p, s * channels : (s + 1) * channels, :].astype(F32)
    for y in range(row_count):
        rows_ref[y, :, :width] = total[2 * y].astype(BF)
        rows_ref[y, :, width:] = total[2 * y + 1].astype(BF)
    own = jnp.concatenate(edge_tiles(lambda y: rows_ref[y], row_count, channels), axis=1)
    others = beside(incoming_ref, mark_ref, row_count, channels)
    left, right = strips_of(own, others, others)
    strip_ref[:, :STRIP] = left
    strip_ref[:, STRIP:] = right
    state = state_strip_ref.shape[0] // 2
    for ref, first, tile in ((up_ref, 0, 0), (down_ref, row_count - 3, 2)):
        for i in range(3):
            ref[i * channels : (i + 1) * channels, :] = rows_ref[first + i]
        spots = [slice(base + tile * LANES, base + (tile + 1) * LANES) for base in (0, STRIP)]
        packed = pack_strips(*[state_strip_ref[:, spot] for spot in spots])
        own_packed = pack_strips(left[:, spots[0]], right[:, spots[0]])
        ref[3 * channels :, :LANES] = jnp.concatenate([own_packed, packed[:state]], axis=0)
        ref[3 * channels :, LANES:] = jnp.concatenate([own_packed, packed[state:]], axis=0)


def around(count):
    return [(i, (i + 1) % count) for i in range(count)]


def back(count):
    return [((i + 1) % count, i) for i in range(count)]


def exchange_columns(edge):
    count = lax.axis_size("lon")
    from_left = lax.ppermute(edge, "lon", around(count))
    from_right = lax.ppermute(edge, "lon", back(count))
    return from_left, from_right


def exchange_rows(up, down):
    count = lax.axis_size("lat")
    from_above = lax.ppermute(down, "lat", around(count))
    from_below = lax.ppermute(up, "lat", back(count))
    return from_above, from_below


def on_device(
    satellite_blocks,
    slot_source,
    slot_weight,
    slot_target,
    tile_counts,
    gate_input_weight,
    gate_state_weight,
    gate_bias,
    hidden_init,
    cell_init,
):
    _, tiles, cap, band, block = slot_weight.shape
    channels = satellite_blocks.shape[1]
    units, row_count, column_count = hidden_init.shape
    gates = gate_bias.shape[0]
    slots = tiles * cap
    half = jnp.where(jnp.arange(gates) < 3 * units, 0.5, 1.0)
    in_weight = gate_input_weight * half[:, None].astype(BF)
    state_weight = gate_state_weight * half[:, None].astype(BF)
    bias = (gate_bias * half)[:, None]
    lat = lax.axis_index("lat")
    flags = jnp.stack([lat > 0, lat < lax.axis_size("lat") - 1]).astype(jnp.int32)

    ring = lax.axis_size("lon")
    height = cap * channels + channels // 2
    message = jax.ShapeDtypeStruct((tiles, height, block), BF)
    groups = tiles // ring
    outgoing = pl.pallas_call(
        functools.partial(gather_kernel, ring),
        out_shape=pltpu.HBM(message.shape, BF),
        in_specs=[pl.BlockSpec(memory_space=pl.ANY)] * 3,
        out_specs=pl.BlockSpec(memory_space=pl.ANY),
        scratch_shapes=[
            pltpu.VMEM(satellite_blocks.shape, BF),
            pltpu.VMEM((slots, band, block), BF),
            pltpu.VMEM(message.shape, BF),
            pltpu.SMEM((cap, tiles), jnp.int32),
            pltpu.SemaphoreType.DMA,
            pltpu.SemaphoreType.DMA,
            pltpu.SemaphoreType.DMA((groups,)),
            pltpu.SemaphoreType.DMA((groups,)),
        ],
        compiler_params=pltpu.CompilerParams(vmem_limit_bytes=8 * 2**20),
        name="gather_band",
    )(in_hbm(slot_source[0].T), in_hbm(satellite_blocks), in_hbm(slot_weight.reshape(slots, band, block)))
    incoming = lax.all_to_all(outgoing, ("lat", "lon"), split_axis=0, concat_axis=0, tiled=True)

    rows, edge = pl.pallas_call(
        prepare_kernel,
        out_shape=(
            jax.ShapeDtypeStruct((row_count, 2 * units, column_count), BF),
            jax.ShapeDtypeStruct((2 * units + tiles, STRIP), BF),
        ),
        in_specs=[pl.BlockSpec(memory_space=pl.ANY)] * 4,
        out_specs=tuple(whole(2)),
        scratch_shapes=[
            pltpu.VMEM(hidden_init.shape, BF),
            pltpu.VMEM(cell_init.shape, BF),
            pltpu.VMEM((cap, tiles), jnp.int32),
            pltpu.VMEM((1, tiles), jnp.int32),
            pltpu.SemaphoreType.DMA((4,)),
        ],
        compiler_params=pltpu.CompilerParams(vmem_limit_bytes=8 * 2**20),
        name="prepare",
    )(in_hbm(hidden_init), in_hbm(cell_init), in_hbm(slot_target[0].T), in_hbm(tile_counts))
    from_left, from_right = exchange_columns(edge)
    padded = row_count + 8
    inside = (row_count - 2, gates, column_count)
    parts = inside[0] // PIECE
    ends = jax.ShapeDtypeStruct((5, units, column_count), BF)
    state_gates, strip_gates, bias, strip, marks, up, down = call(
        state_kernel,
        [
            pltpu.HBM(inside, F32),
            jax.ShapeDtypeStruct((gates, 2 * STRIP), F32),
            jax.ShapeDtypeStruct((gates, column_count), F32),
            jax.ShapeDtypeStruct((2 * units, 2 * STRIP), BF),
            jax.ShapeDtypeStruct((tiles, LANES), F32),
            ends,
            ends,
        ],
        6, 0,
        [
            pltpu.VMEM(inside, F32),
            pltpu.VMEM((padded, 3 * units, column_count), BF),
            pltpu.VMEM((padded, units, LANES), BF),
            pltpu.SemaphoreType.DMA((parts,)),
        ],
        "state_gates", 2 * gates * 9 * units * row_count * column_count,
        (rows, edge, from_left, from_right, state_weight, bias), 16,
        out_specs=[pl.BlockSpec(memory_space=pl.ANY)] + whole(6),
    )
    above, below = exchange_rows(up, down)
    incoming, state_gates, strip_gates, bias, in_weight = lax.optimization_barrier(
        (incoming, state_gates, strip_gates, bias, in_weight)
    )

    ends = jax.ShapeDtypeStruct((4 * channels + units, column_count), BF)
    forcing, forcing_strip, up, down = call(
        scatter_kernel,
        [
            jax.ShapeDtypeStruct((row_count, channels, column_count), BF),
            jax.ShapeDtypeStruct((channels, 2 * STRIP), BF),
            ends,
            ends,
        ],
        3, 2,
        [pltpu.VMEM((2 * row_count + 1, channels, block), F32)],
        "scatter_add", slots * channels * block,
        (slot_target[0].T, tile_counts, incoming, marks, strip),
    )
    f_above, f_below = exchange_rows(up, down)
    inner_rows = jax.ShapeDtypeStruct((row_count - 6, units, column_count), BF)
    threes = jax.ShapeDtypeStruct((4, 3 * units, column_count), BF)
    inner = call(
        inner_kernel,
        [
            inner_rows,
            inner_rows,
            jax.ShapeDtypeStruct((4, gates, column_count), F32),
            threes,
            threes,
            jax.ShapeDtypeStruct((4, units, column_count), F32),
        ],
        9, 0,
        [
            pltpu.VMEM(inside, F32),
            pltpu.VMEM((padded, 3 * channels, column_count), BF),
            pltpu.VMEM((padded, channels, LANES), BF),
            pltpu.VMEM((padded, gates, column_count), F32),
            pltpu.VMEM((padded, 3 * units, column_count), BF),
            pltpu.VMEM((padded, 3 * units, column_count), BF),
            pltpu.VMEM((padded, units, LANES), BF),
            pltpu.VMEM((padded, units, column_count), F32),
            pltpu.SemaphoreType.DMA((parts,)),
        ],
        "inner", 2 * gates * 9 * (channels + 2 * units) * row_count * column_count,
        (in_hbm(state_gates), strip_gates, rows, strip, forcing, forcing_strip, in_weight, state_weight, bias), 24,
        in_specs=[pl.BlockSpec(memory_space=pl.ANY)] + whole(8),
    )
    out = jax.ShapeDtypeStruct((units, row_count, column_count), BF)
    return call(
        edge_kernel,
        [out, out],
        17, 1,
        [
            pltpu.VMEM((padded, 3 * channels, column_count), BF),
            pltpu.VMEM((padded, 3 * units, column_count), BF),
            pltpu.VMEM((padded, 3 * units, column_count), BF),
            pltpu.VMEM((padded, 3 * units, column_count), BF),
            pltpu.VMEM((row_count, units, column_count), BF),
            pltpu.VMEM((row_count, units, column_count), BF),
        ],
        "edges", 2 * gates * 9 * (channels + 3 * units) * 6 * column_count,
        (flags, rows, strip, forcing, forcing_strip, above, below, f_above, f_below,
         in_weight, state_weight, bias, *inner), 16,
    )


def solution(mesh):
    placed = (
        P(("lat", "lon"), None, None),
        P(("lat", "lon"), None, None),
        P(("lat", "lon"), None, None, None, None),
        P(("lat", "lon"), None, None),
        P(("lat", "lon"), None),
        P(),
        P(),
        P(),
        P(None, "lat", "lon"),
        P(None, "lat", "lon"),
    )
    return jax.shard_map(
        on_device,
        mesh=mesh,
        in_specs=placed,
        out_specs=(P(None, "lat", "lon"), P(None, "lat", "lon")),
        check_vma=False,
    )
```

```python
import functools

import jax
import jax.numpy as jnp
from jax import lax
from jax.experimental import pallas as pl
from jax.experimental.pallas import tpu as pltpu
from jax.sharding import PartitionSpec as P

STEPS = 3
PAD = 4
LANES = 128
STRIP = 3 * LANES
BATCH = 2
PIECE = 6
BF = jnp.bfloat16
F32 = jnp.float32


def lane_of(shape):
    return lax.broadcasted_iota(jnp.int32, shape, len(shape) - 1)


def whole(count):
    return [pl.BlockSpec(memory_space=pltpu.VMEM)] * count


def in_hbm(x):
    return pltpu.with_memory_space_constraint(x, pltpu.HBM)


def scalars(count):
    return [pl.BlockSpec(memory_space=pltpu.SMEM)] * count


def call(
    kernel, outs, ins, scalar_count, scratch, name, flops, args, mib=8, in_specs=None, out_specs=None
):
    nbytes = sum(a.size * a.dtype.itemsize for a in args)
    return pl.pallas_call(
        kernel,
        out_shape=tuple(outs),
        in_specs=in_specs or scalars(scalar_count) + whole(ins),
        out_specs=tuple(out_specs or whole(len(outs))),
        scratch_shapes=scratch,
        compiler_params=pltpu.CompilerParams(vmem_limit_bytes=mib * 2**20),
        cost_estimate=pl.CostEstimate(flops=flops, bytes_accessed=nbytes, transcendentals=0),
        name=name,
    )(*args)


def edge_tiles(row_of, row_count, channels):
    lane = lane_of((channels, LANES))
    tiles = [jnp.zeros((channels, LANES), BF) for _ in range(STRIP // LANES)]
    for y in range(row_count):
        row = row_of(y)
        both = jnp.where(lane < 64, row[:, :LANES], row[:, -LANES:])
        r = y + PAD
        place = r % 16
        turned = pltpu.roll(both, (8 * place + 4) % LANES, axis=1)
        tiles[r // 16] = jnp.where(lane // 8 == place, turned, tiles[r // 16])
    return tiles


def gather_kernel(
    ring, source_hbm, blocks_hbm, weight_hbm, out_hbm, blocks, weights, out, source_ref, source_sem, block_sem, weight_sem, out_sem
):
    cap, tiles = source_ref.shape
    band, width = weights.shape[1:]
    channels = blocks.shape[1]
    groups = tiles // ring
    share = ring * cap
    fetch = pltpu.make_async_copy(blocks_hbm, blocks, block_sem)
    fetch.start()
    places = pltpu.make_async_copy(source_hbm, source_ref, source_sem)
    places.start()
    parts = [
        pltpu.make_async_copy(
            weight_hbm.at[pl.ds(g * share, share)], weights.at[pl.ds(g * share, share)], weight_sem.at[g]
        )
        for g in range(groups)
    ]
    for part in parts:
        part.start()
    offset = lax.broadcasted_iota(jnp.int32, (band, width), 0) - band // 2
    spot = lane_of((band, width)) + offset
    inside = (spot >= 0) & (spot < width)
    lane = lane_of((channels, width))
    near = lane_of((channels // 2, width)) % 8 < 4
    places.wait()
    fetch.wait()
    sends = []
    for g in range(groups):
        parts[g].wait()
        folded = []
        for j in range(ring):
            q = g * ring + j
            for s in range(cap):
                block = blocks[source_ref[s, q]]
                factor = jnp.where(inside, weights[q * cap + s].astype(F32), 0.0)
                total = jnp.zeros((channels, width), F32)
                for k in range(band):
                    moved = block if k == band // 2 else pltpu.roll(block, (band // 2 - k) % width, axis=1)
                    total = total + factor[k : k + 1, :] * moved.astype(F32)
                rounded = total.astype(BF)
                out[q, s * channels : (s + 1) * channels, :] = rounded
        for j in range(ring):
            edges = jnp.zeros((channels, width), BF)
            for s in range(cap):
                rounded = out[g * ring + j, s * channels : (s + 1) * channels, :]
                edges = jnp.where(lane // 8 == s, pltpu.roll(rounded, 8 * s + 4, axis=1), edges)
            wide = edges.astype(F32)
            folded.append(wide[: channels // 2] + pltpu.roll(wide[channels // 2 :], 8 * cap, axis=1))
        for j in range(ring):
            both = jnp.where(near, folded[j - 1], folded[(j + 1) % ring])
            out[g * ring + j, cap * channels :, :] = both.astype(BF)
        send = pltpu.make_async_copy(
            out.at[pl.ds(g * ring, ring)], out_hbm.at[pl.ds(g * ring, ring)], out_sem.at[g]
        )
        send.start()
        sends.append(send)
    for send in sends:
        send.wait()


def prepare_kernel(
    flag_ref, hidden_hbm, cell_hbm, target_hbm, count_hbm, rows_ref, edge_ref, outer_ref, inner_ref,
    hidden, cell, target_ref, count_ref, sems,
):
    fetches = [
        pltpu.make_async_copy(source, target, sems.at[i])
        for i, (source, target) in enumerate(
            [(target_hbm, target_ref), (count_hbm, count_ref), (hidden_hbm, hidden), (cell_hbm, cell)]
        )
    ]
    for fetch in fetches:
        fetch.start()
    units, row_count, _ = hidden.shape
    fetches[0].wait()
    fetches[1].wait()
    edge_ref[2 * units :, :LANES] = marks_of(target_ref[...], count_ref[...]).astype(BF)
    edge_ref[2 * units :, LANES:] = jnp.zeros((target_ref.shape[1], STRIP - LANES), BF)
    fetches[2].wait()
    rows_ref[:, :units, :] = jnp.swapaxes(hidden[...], 0, 1)
    fetches[3].wait()
    rows_ref[:, units:, :] = jnp.swapaxes(cell[...], 0, 1)
    hidden_rows = rows_ref[:3, :units], rows_ref[row_count - 3 :, :units]
    cell_rows = rows_ref[:2, units:], rows_ref[row_count - 2 :, units:]
    outer_ref[:3], inner_ref[:3] = for_partners(flag_ref[2], *hidden_rows)
    outer_ref[3:], inner_ref[3:] = for_partners(flag_ref[2], *cell_rows)
    tiles = edge_tiles(lambda y: rows_ref[y], row_count, 2 * units)
    for t, tile in enumerate(tiles):
        edge_ref[: 2 * units, t * LANES : (t + 1) * LANES] = tile


def marks_of(target, live_count):
    cap, sources = target.shape
    slot = lax.broadcasted_iota(jnp.int32, target.shape, 0)
    live = slot < live_count
    row = target // 2
    odd = target % 2 == 1
    picked = [jnp.where(live & odd, row, -1), jnp.where(live & ~odd, row, -1)]
    rows = jnp.concatenate([p.astype(F32) for p in picked], axis=0)
    lane = lane_of((2 * cap, LANES))
    which = lax.broadcasted_iota(jnp.int32, (2 * cap, LANES), 0)
    spread = (lane // 8 % cap == which % cap) & ((lane % 8 < 4) == (which < cap))
    return lax.dot_general(
        rows.astype(BF),
        jnp.where(spread, 1.0, 0.0).astype(BF),
        (((0,), (0,)), ((), ())),
        preferred_element_type=F32,
    )


def strips_of(own, from_left, from_right):
    near = lane_of(own.shape) % 8 < 4
    return jnp.where(near, from_left, own), jnp.where(near, own, from_right)


def pack_strips(left, right):
    return jnp.where(lane_of(left.shape) < 64, left, pltpu.roll(right, 64, axis=1))


def full_strip(strip, above, below):
    lane = lane_of(above.shape)
    from_above = (lane >= 8) & (lane < 32)
    from_below = (lane >= 32) & (lane < 56)
    parts = []
    for side in range(2):
        base = side * STRIP
        if side:
            above, below = pltpu.roll(above, 64, axis=1), pltpu.roll(below, 64, axis=1)
        parts.append(jnp.where(from_above, above, strip[:, base : base + LANES]))
        parts.append(strip[:, base + LANES : base + 2 * LANES])
        parts.append(jnp.where(from_below, below, strip[:, base + 2 * LANES : base + STRIP]))
    return jnp.concatenate(parts, axis=1)


def strip_taps(strip):
    width = strip.shape[1]
    taps = []
    for a in range(3):
        for e in range(3):
            shift = 8 * (a - 1) + e - 1
            taps.append(strip if shift == 0 else pltpu.roll(strip, -shift % width, axis=1))
    return jnp.concatenate(taps, axis=0)


def patches_of(strip, tiles, first, last):
    channels = strip.shape[0]
    near = lane_of((channels, LANES)) % 8 < 4
    found = {}
    for i, t in enumerate(tiles):
        left = strip[:, i * LANES : (i + 1) * LANES]
        right = strip[:, (len(tiles) + i) * LANES : (len(tiles) + i + 1) * LANES]
        mixed = jnp.where(near, left, right)
        for r in range(max(first, 16 * t), min(last, 16 * t + 16)):
            found[r] = pltpu.roll(mixed, -(8 * (r % 16) + 4) % LANES, axis=1)
    return found


def store_patches(strip, patch_ref, first, last):
    for r, patch in patches_of(strip, range(STRIP // LANES), first, last).items():
        patch_ref[r] = patch


def store_three(ref, r, row, patch):
    channels = row.shape[0]
    lane = lane_of((channels, LANES))
    head, tail = row[:, :LANES], row[:, LANES:]
    ref[r, :channels, :LANES] = pltpu.roll(jnp.where(lane == LANES - 1, patch, head), 1, axis=1)
    ref[r, :channels, LANES:] = pltpu.roll(jnp.where(lane == LANES - 1, head, tail), 1, axis=1)
    ref[r, channels : 2 * channels, :] = row
    ref[r, 2 * channels :, :LANES] = pltpu.roll(jnp.where(lane == 0, tail, head), LANES - 1, axis=1)
    ref[r, 2 * channels :, LANES:] = pltpu.roll(jnp.where(lane == 0, patch, tail), LANES - 1, axis=1)


def row_taps(ref, r):
    channels = ref.shape[1]
    return ref[pl.ds(r - 1, 3)].reshape(3 * channels, ref.shape[2])


def matmul(weights, taps):
    return jnp.dot(weights, taps, preferred_element_type=F32)


def for_partners(odd, up, down):
    odd = odd == 1
    return jnp.where(odd, up, down), jnp.where(odd, down, up)


def state_kernel(
    rows_ref, edge_ref, left_ref, right_ref, weight_ref, bias_ref,
    gates_hbm, wide_bias_ref, strip_ref, mark_ref,
    gates, three, patches, sems,
):
    units = rows_ref.shape[1] // 2
    count = rows_ref.shape[0]
    wide_bias_ref[...] = jnp.broadcast_to(bias_ref[...], wide_bias_ref.shape)
    channels = 2 * units
    left, right = strips_of(edge_ref[:channels], left_ref[:channels], right_ref[:channels])
    strip_ref[:, :STRIP] = left
    strip_ref[:, STRIP:] = right
    near = lane_of(mark_ref.shape) % 8 < 4
    from_left = left_ref[channels:, :LANES].astype(F32)
    mark_ref[...] = jnp.where(near, from_left, right_ref[channels:, :LANES].astype(F32))
    strip = jnp.concatenate([left[:units], right[:units]], axis=1)
    store_patches(strip, patches, PAD, count + PAD)
    for y in range(count):
        store_three(three, y + PAD, rows_ref[y, :units], patches[y + PAD])
    sends = pieces(gates, gates_hbm, sems)
    for y in range(1, count - 1):
        gates[y - 1] = matmul(weight_ref[...], row_taps(three, y + PAD))
        if y % PIECE == 0:
            sends[y // PIECE - 1].start()
    for send in sends:
        send.wait()


def pieces(source, target, sems):
    count = source.shape[0] // PIECE
    spots = [pl.ds(i * PIECE, PIECE) for i in range(count)]
    return [pltpu.make_async_copy(source.at[s], target.at[s], sems.at[i]) for i, s in enumerate(spots)]


def update(gates, memory):
    units = memory.shape[0]
    ingate = 0.5 * jnp.tanh(gates[:units]) + 0.5
    forget = 0.5 * jnp.tanh(gates[units : 2 * units]) + 0.5
    outgate = 0.5 * jnp.tanh(gates[2 * units : 3 * units]) + 0.5
    memory = forget * memory + ingate * jnp.tanh(gates[3 * units :])
    return outgate * jnp.tanh(memory), memory


def early_kernel(
    gates_hbm, rows_ref, forcing_ref, forcing_strip_ref, in_weight_ref, bias_ref,
    sums_ref, hidden_ref, memory_ref, gates, f_three, f_patches, sems,
):
    units = hidden_ref.shape[1]
    count = rows_ref.shape[0]
    bias = bias_ref[...]
    fetches = pieces(gates_hbm, gates, sems)
    for fetch in fetches:
        fetch.start()
    store_patches(forcing_strip_ref[...], f_patches, PAD, count + PAD)
    for y in range(count):
        store_three(f_three, y + PAD, forcing_ref[y], f_patches[y + PAD])
    for i in range(count - 2):
        if i % PIECE == 0:
            fetches[i // PIECE].wait()
        sums = matmul(in_weight_ref[...], row_taps(f_three, i + 1 + PAD)) + bias
        hidden, memory = update(gates[i] + sums, rows_ref[i + 1, units:].astype(F32))
        sums_ref[i] = sums
        hidden_ref[i] = hidden.astype(BF)
        memory_ref[i] = memory


def edge_rows(count, depth, many):
    top = [PAD + depth + i for i in range(many)]
    return top + [PAD + count - 1 - depth - (many - 1) + i for i in range(many)]


def late_kernel(
    flag_ref, rows_ref, strip_ref, forcing_ref, forcing_strip_ref,
    outer_ref, inner_ref, f_outer_ref, f_inner_ref, in_weight_ref, weight_ref, bias_ref,
    inner_sums_ref, inner_hidden_ref, inner_memory_ref,
    hidden_hbm, cell_hbm,
    f_three, three, first, second, sums, memory, patches, h_rows, c_rows, h_out, c_out, sems,
):
    units = rows_ref.shape[1] // 2
    count = rows_ref.shape[0]
    channels = forcing_ref.shape[1]
    has_above = flag_ref[0].astype(F32)
    has_below = flag_ref[1].astype(F32)
    bf_above, bf_below = has_above.astype(BF), has_below.astype(BF)
    bias = bias_ref[...]

    above, below = for_partners(flag_ref[2], outer_ref[...], inner_ref[...])
    f_above, f_below = for_partners(flag_ref[2], f_outer_ref[...], f_inner_ref[...])

    def strips_in(message, present):
        packed = message[3 * channels :] * present
        return jnp.concatenate([packed[:, :LANES], packed[channels:, LANES:]], axis=0)

    joined = jnp.concatenate([forcing_strip_ref[...], strip_ref[...]], axis=0)
    joined = full_strip(joined, strips_in(f_above, bf_above), strips_in(f_below, bf_below))
    strip_forcing = matmul(in_weight_ref[...], strip_taps(joined[:channels]))
    strip_forcing = strip_forcing + jnp.concatenate([bias] * 3, axis=1)
    state_strip = joined[channels : channels + units]
    strip_gates = strip_forcing + matmul(weight_ref[...], strip_taps(state_strip))
    found = patches_of(joined[: channels + units], range(STRIP // LANES), 1, PAD + 2)
    found.update(patches_of(joined[: channels + units], range(STRIP // LANES), count + PAD - 2, count + PAD + 3))

    def place(r, forcing, hidden):
        store_three(f_three, r, forcing, found[r][:channels])
        store_three(three, r, hidden, found[r][channels:])

    for i in range(3):
        line = slice(i * channels, (i + 1) * channels)
        place(1 + i, f_above[line] * bf_above, above[i] * bf_above)
        place(count + PAD + i, f_below[line] * bf_below, below[i] * bf_below)
    for r in edge_rows(count, 0, 2):
        place(r, forcing_ref[r - PAD], rows_ref[r - PAD, :units])

    lane = lane_of((units, 2 * STRIP))
    row_of_lane = lane % STRIP // 8
    keep = jnp.where(row_of_lane < PAD, has_above, 1.0)
    keep = jnp.where(row_of_lane >= PAD + count, has_below, keep)

    def kept(hidden, r):
        if r < PAD:
            hidden = hidden * has_above
        elif r >= PAD + count:
            hidden = hidden * has_below
        return hidden.astype(BF)

    strip_hidden, strip_memory = update(strip_gates, joined[channels + units :].astype(F32))
    strip_hidden = (strip_hidden * keep).astype(BF)
    store_patches(strip_hidden, patches, 2, count + 6)
    olds = [above[3], above[4], rows_ref[0, units:]]
    olds += [rows_ref[count - 1, units:], below[3], below[4]]
    for r, old in zip(edge_rows(count, -2, 3), olds):
        sums[r] = matmul(in_weight_ref[...], row_taps(f_three, r)) + bias
        first_gates = sums[r] + matmul(weight_ref[...], row_taps(three, r))
        hidden, memory[r] = update(first_gates, old.astype(F32))
        store_three(first, r, kept(hidden, r), patches[r])
    inner = range(PAD + 1, PAD + count - 1)
    for i, r in enumerate(inner):
        store_three(first, r, inner_hidden_ref[i], patches[r])

    strip_gates = matmul(weight_ref[...], strip_taps(strip_hidden)) + strip_forcing
    strip_hidden, strip_memory = update(strip_gates, strip_memory)
    strip_hidden = (strip_hidden * keep).astype(BF)
    store_patches(strip_hidden, patches, 3, count + 5)

    def later(source, r, old):
        total = inner_sums_ref[r - PAD - 1] if r in inner else sums[r]
        return update(total + matmul(weight_ref[...], row_taps(source, r)), old)

    for r in range(PAD - 1, PAD + count + 1):
        old = inner_memory_ref[r - PAD - 1] if r in inner else memory[r]
        hidden, memory[r] = later(first, r, old)
        store_three(second, r, kept(hidden, r), patches[r])

    sends = []
    part = count // 2
    for start in (0, part):
        for y in range(start, start + part):
            hidden, new = later(second, y + PAD, memory[y + PAD])
            h_rows[y] = hidden.astype(BF)
            c_rows[y] = new.astype(BF)
        spot = pl.ds(start, part)
        h_out[:, start : start + part, :] = jnp.swapaxes(h_rows[start : start + part], 0, 1)
        c_out[:, start : start + part, :] = jnp.swapaxes(c_rows[start : start + part], 0, 1)
        for source, target in ((h_out, hidden_hbm), (c_out, cell_hbm)):
            sends.append(pltpu.make_async_copy(source.at[:, spot], target.at[:, spot], sems.at[len(sends)]))
            sends[-1].start()
    for send in sends:
        send.wait()


def beside(incoming_ref, mark_ref, row_count, channels):
    sources = incoming_ref.shape[0]
    base = incoming_ref.shape[1] - channels // 2
    lane = lane_of((channels // 2, LANES))
    group_lanes = 8 * ((base // channels) % 16)
    tiles = [[jnp.zeros((channels // 2, LANES), F32) for _ in range(2)] for _ in range(STRIP // LANES)]
    for start in range(0, row_count, 16):
        sums = [jnp.zeros((channels // 2, LANES), F32) for _ in range(16)]
        for p in range(sources):
            edges = incoming_ref[p, base:, :].astype(F32)
            mark = jnp.broadcast_to(mark_ref[p : p + 1, :], edges.shape)
            for i in range(16):
                sums[i] = sums[i] + jnp.where(mark == float(start + i), edges, 0.0)
        for i in range(16):
            total = sums[i] + pltpu.roll(sums[i], LANES - 8, axis=1)
            total = total + pltpu.roll(total, LANES - 16, axis=1)
            r = start + i + PAD
            for part in range(2):
                moved = pltpu.roll(total, (8 * (r % 16) - part * group_lanes) % LANES, axis=1)
                tiles[r // 16][part] = jnp.where(lane // 8 == r % 16, moved, tiles[r // 16][part])
    halves = [jnp.concatenate([t[part] for t in tiles], axis=1) for part in range(2)]
    return jnp.concatenate(halves, axis=0).astype(BF)


def scatter_kernel(
    flag_ref, target_ref, count_ref, incoming_ref, mark_ref, state_strip_ref,
    rows_ref, strip_ref, outer_ref, inner_ref, *totals,
):
    cap, sources = target_ref.shape
    row_count, channels, width = rows_ref.shape
    width = width // 2
    spare = 2 * row_count
    for total in totals:
        total[...] = jnp.zeros(total.shape, F32)
    for p in range(sources):
        live = count_ref[0, p]
        for s in range(cap):
            block = jnp.where(s < live, target_ref[s, p], spare)
            total = totals[s % len(totals)]
            total[block] = total[block] + incoming_ref[p, s * channels : (s + 1) * channels, :].astype(F32)
    for y in range(row_count):
        for half in range(2):
            block = sum(total[2 * y + half] for total in totals)
            rows_ref[y, :, half * width : (half + 1) * width] = block.astype(BF)
    own = jnp.concatenate(edge_tiles(lambda y: rows_ref[y], row_count, channels), axis=1)
    others = beside(incoming_ref, mark_ref, row_count, channels)
    left, right = strips_of(own, others, others)
    strip_ref[:, :STRIP] = left
    strip_ref[:, STRIP:] = right
    state = state_strip_ref.shape[0] // 2
    messages = []
    for first, tile in ((0, 0), (row_count - 3, 2)):
        lines = [rows_ref[first + i] for i in range(3)]
        spots = [slice(base + tile * LANES, base + (tile + 1) * LANES) for base in (0, STRIP)]
        packed = pack_strips(*[state_strip_ref[:, spot] for spot in spots])
        own_packed = pack_strips(left[:, spots[0]], right[:, spots[0]])
        halves = [jnp.concatenate([own_packed, part], axis=0) for part in (packed[:state], packed[state:])]
        messages.append(jnp.concatenate([*lines, jnp.concatenate(halves, axis=1)], axis=0))
    outer_ref[...], inner_ref[...] = for_partners(flag_ref[2], *messages)


def around(count):
    return [(i, (i + 1) % count) for i in range(count)]


def back(count):
    return [((i + 1) % count, i) for i in range(count)]


def exchange_columns(edge):
    count = lax.axis_size("lon")
    from_left = lax.ppermute(edge, "lon", around(count))
    from_right = lax.ppermute(edge, "lon", back(count))
    return from_left, from_right


def exchange_rows(outer, inner):
    count = lax.axis_size("lat")

    def swap(x, first):
        partner = list(range(count))
        for i in range(first, count - 1, 2):
            partner[i], partner[i + 1] = i + 1, i
        return lax.ppermute(x, "lat", list(enumerate(partner)))

    got_outer = swap(outer, 0)
    got_inner = swap(inner, 1)
    return got_outer, got_inner


def on_device(
    satellite_blocks,
    slot_source,
    slot_weight,
    slot_target,
    tile_counts,
    gate_input_weight,
    gate_state_weight,
    gate_bias,
    hidden_init,
    cell_init,
):
    _, tiles, cap, band, block = slot_weight.shape
    channels = satellite_blocks.shape[1]
    units, row_count, column_count = hidden_init.shape
    gates = gate_bias.shape[0]
    slots = tiles * cap
    half = jnp.where(jnp.arange(gates) < 3 * units, 0.5, 1.0)
    in_weight = gate_input_weight * half[:, None].astype(BF)
    state_weight = gate_state_weight * half[:, None].astype(BF)
    bias = (gate_bias * half)[:, None]
    lat = lax.axis_index("lat")
    flags = jnp.stack([lat > 0, lat < lax.axis_size("lat") - 1, lat % 2 == 1]).astype(jnp.int32)

    ring = lax.axis_size("lon")
    height = cap * channels + channels // 2
    message = jax.ShapeDtypeStruct((tiles, height, block), BF)
    groups = tiles // ring
    outgoing = pl.pallas_call(
        functools.partial(gather_kernel, ring),
        out_shape=pltpu.HBM(message.shape, BF),
        in_specs=[pl.BlockSpec(memory_space=pl.ANY)] * 3,
        out_specs=pl.BlockSpec(memory_space=pl.ANY),
        scratch_shapes=[
            pltpu.VMEM(satellite_blocks.shape, BF),
            pltpu.VMEM((slots, band, block), BF),
            pltpu.VMEM(message.shape, BF),
            pltpu.SMEM((cap, tiles), jnp.int32),
            pltpu.SemaphoreType.DMA,
            pltpu.SemaphoreType.DMA,
            pltpu.SemaphoreType.DMA((groups,)),
            pltpu.SemaphoreType.DMA((groups,)),
        ],
        compiler_params=pltpu.CompilerParams(vmem_limit_bytes=8 * 2**20),
        name="gather_band",
    )(in_hbm(slot_source[0].T), in_hbm(satellite_blocks), in_hbm(slot_weight.reshape(slots, band, block)))
    incoming = lax.all_to_all(outgoing, ("lat", "lon"), split_axis=0, concat_axis=0, tiled=True)

    ends = jax.ShapeDtypeStruct((5, units, column_count), BF)
    rows, edge, outer, inner = pl.pallas_call(
        prepare_kernel,
        out_shape=(
            jax.ShapeDtypeStruct((row_count, 2 * units, column_count), BF),
            jax.ShapeDtypeStruct((2 * units + tiles, STRIP), BF),
            ends,
            ends,
        ),
        in_specs=scalars(1) + [pl.BlockSpec(memory_space=pl.ANY)] * 4,
        out_specs=tuple(whole(4)),
        scratch_shapes=[
            pltpu.VMEM(hidden_init.shape, BF),
            pltpu.VMEM(cell_init.shape, BF),
            pltpu.VMEM((cap, tiles), jnp.int32),
            pltpu.VMEM((1, tiles), jnp.int32),
            pltpu.SemaphoreType.DMA((4,)),
        ],
        compiler_params=pltpu.CompilerParams(vmem_limit_bytes=8 * 2**20),
        name="prepare",
    )(flags, in_hbm(hidden_init), in_hbm(cell_init), in_hbm(slot_target[0].T), in_hbm(tile_counts))
    from_left, from_right = exchange_columns(edge)
    outer, inner = exchange_rows(outer, inner)
    padded = row_count + 8
    inside = (row_count - 2, gates, column_count)
    parts = inside[0] // PIECE
    state_gates, bias, strip, marks = call(
        state_kernel,
        [
            pltpu.HBM(inside, F32),
            jax.ShapeDtypeStruct((gates, column_count), F32),
            jax.ShapeDtypeStruct((2 * units, 2 * STRIP), BF),
            jax.ShapeDtypeStruct((tiles, LANES), F32),
        ],
        6, 0,
        [
            pltpu.VMEM(inside, F32),
            pltpu.VMEM((padded, 3 * units, column_count), BF),
            pltpu.VMEM((padded, units, LANES), BF),
            pltpu.SemaphoreType.DMA((parts,)),
        ],
        "state_gates", 2 * gates * 9 * units * row_count * column_count,
        (rows, edge, from_left, from_right, state_weight, bias), 16,
        out_specs=[pl.BlockSpec(memory_space=pl.ANY)] + whole(3),
    )
    incoming, state_gates, bias, in_weight = lax.optimization_barrier((incoming, state_gates, bias, in_weight))

    ends = jax.ShapeDtypeStruct((4 * channels + units, column_count), BF)
    forcing, forcing_strip, f_outer, f_inner = call(
        scatter_kernel,
        [
            jax.ShapeDtypeStruct((row_count, channels, column_count), BF),
            jax.ShapeDtypeStruct((channels, 2 * STRIP), BF),
            ends,
            ends,
        ],
        3, 3,
        [pltpu.VMEM((2 * row_count + 1, channels, block), F32)] * 2,
        "scatter_add", slots * channels * block,
        (flags, slot_target[0].T, tile_counts, incoming, marks, strip),
    )
    f_outer, f_inner = exchange_rows(f_outer, f_inner)
    sums, hidden, memory = call(
        early_kernel,
        [
            jax.ShapeDtypeStruct(inside, F32),
            jax.ShapeDtypeStruct((inside[0], units, column_count), BF),
            jax.ShapeDtypeStruct((inside[0], units, column_count), F32),
        ],
        6, 0,
        [
            pltpu.VMEM(inside, F32),
            pltpu.VMEM((padded, 3 * channels, column_count), BF),
            pltpu.VMEM((padded, channels, LANES), BF),
            pltpu.SemaphoreType.DMA((parts,)),
        ],
        "first_step", 2 * gates * 9 * channels * row_count * column_count,
        (in_hbm(state_gates), rows, forcing, forcing_strip, in_weight, bias), 16,
        in_specs=[pl.BlockSpec(memory_space=pl.ANY)] + whole(5),
    )
    return call(
        late_kernel,
        [pltpu.HBM(hidden_init.shape, BF)] * 2,
        14, 1,
        [
            pltpu.VMEM((padded, 3 * channels, column_count), BF),
            pltpu.VMEM((padded, 3 * units, column_count), BF),
            pltpu.VMEM((padded, 3 * units, column_count), BF),
            pltpu.VMEM((padded, 3 * units, column_count), BF),
            pltpu.VMEM((padded, gates, column_count), F32),
            pltpu.VMEM((padded, units, column_count), F32),
            pltpu.VMEM((padded, units, LANES), BF),
            pltpu.VMEM((row_count, units, column_count), BF),
            pltpu.VMEM((row_count, units, column_count), BF),
            pltpu.VMEM(hidden_init.shape, BF),
            pltpu.VMEM(hidden_init.shape, BF),
            pltpu.SemaphoreType.DMA((4,)),
        ],
        "later_steps", 2 * gates * 9 * 2 * units * row_count * column_count,
        (flags, rows, strip, forcing, forcing_strip, outer, inner, f_outer, f_inner,
         in_weight, state_weight, bias, sums, hidden, memory), 24,
        out_specs=[pl.BlockSpec(memory_space=pl.ANY)] * 2,
    )


def solution(mesh):
    placed = (
        P(("lat", "lon"), None, None),
        P(("lat", "lon"), None, None),
        P(("lat", "lon"), None, None, None, None),
        P(("lat", "lon"), None, None),
        P(("lat", "lon"), None),
        P(),
        P(),
        P(),
        P(None, "lat", "lon"),
        P(None, "lat", "lon"),
    )
    return jax.shard_map(
        on_device,
        mesh=mesh,
        in_specs=placed,
        out_specs=(P(None, "lat", "lon"), P(None, "lat", "lon")),
        check_vma=False,
    )
```

```python
import functools

import jax
import jax.numpy as jnp
from jax import lax
from jax.experimental import pallas as pl
from jax.experimental.pallas import tpu as pltpu
from jax.sharding import PartitionSpec as P

STEPS = 3
PAD = 4
LANES = 128
STRIP = 3 * LANES
BATCH = 2
PIECE = 6
BF = jnp.bfloat16
F32 = jnp.float32


def lane_of(shape):
    return lax.broadcasted_iota(jnp.int32, shape, len(shape) - 1)


def whole(count):
    return [pl.BlockSpec(memory_space=pltpu.VMEM)] * count


def in_hbm(x):
    return pltpu.with_memory_space_constraint(x, pltpu.HBM)


def scalars(count):
    return [pl.BlockSpec(memory_space=pltpu.SMEM)] * count


def call(
    kernel, outs, ins, scalar_count, scratch, name, flops, args, mib=8, in_specs=None, out_specs=None
):
    nbytes = sum(a.size * a.dtype.itemsize for a in args)
    return pl.pallas_call(
        kernel,
        out_shape=tuple(outs),
        in_specs=in_specs or scalars(scalar_count) + whole(ins),
        out_specs=tuple(out_specs or whole(len(outs))),
        scratch_shapes=scratch,
        compiler_params=pltpu.CompilerParams(vmem_limit_bytes=mib * 2**20),
        cost_estimate=pl.CostEstimate(flops=flops, bytes_accessed=nbytes, transcendentals=0),
        name=name,
    )(*args)


def edge_tiles(row_of, row_count, channels):
    lane = lane_of((channels, LANES))
    tiles = [jnp.zeros((channels, LANES), BF) for _ in range(STRIP // LANES)]
    for y in range(row_count):
        row = row_of(y)
        both = jnp.where(lane < 64, row[:, :LANES], row[:, -LANES:])
        r = y + PAD
        place = r % 16
        turned = pltpu.roll(both, (8 * place + 4) % LANES, axis=1)
        tiles[r // 16] = jnp.where(lane // 8 == place, turned, tiles[r // 16])
    return tiles


def gather_kernel(
    ring, source_hbm, blocks_hbm, weight_hbm, out_hbm, blocks, weights, out, source_ref, source_sem, block_sem, weight_sem, out_sem
):
    cap, tiles = source_ref.shape
    band, width = weights.shape[1:]
    channels = blocks.shape[1]
    groups = tiles // ring
    share = ring * cap
    fetch = pltpu.make_async_copy(blocks_hbm, blocks, block_sem)
    fetch.start()
    places = pltpu.make_async_copy(source_hbm, source_ref, source_sem)
    places.start()
    parts = [
        pltpu.make_async_copy(
            weight_hbm.at[pl.ds(g * share, share)], weights.at[pl.ds(g * share, share)], weight_sem.at[g]
        )
        for g in range(groups)
    ]
    for part in parts:
        part.start()
    offset = lax.broadcasted_iota(jnp.int32, (band, width), 0) - band // 2
    spot = lane_of((band, width)) + offset
    inside = (spot >= 0) & (spot < width)
    lane = lane_of((channels, width))
    near = lane_of((channels // 2, width)) % 8 < 4
    places.wait()
    fetch.wait()
    sends = []
    for g in range(groups):
        parts[g].wait()
        folded = []
        for j in range(ring):
            q = g * ring + j
            for s in range(cap):
                block = blocks[source_ref[s, q]]
                factor = jnp.where(inside, weights[q * cap + s].astype(F32), 0.0)
                total = jnp.zeros((channels, width), F32)
                for k in range(band):
                    moved = block if k == band // 2 else pltpu.roll(block, (band // 2 - k) % width, axis=1)
                    total = total + factor[k : k + 1, :] * moved.astype(F32)
                rounded = total.astype(BF)
                out[q, s * channels : (s + 1) * channels, :] = rounded
        for j in range(ring):
            edges = jnp.zeros((channels, width), BF)
            for s in range(cap):
                rounded = out[g * ring + j, s * channels : (s + 1) * channels, :]
                edges = jnp.where(lane // 8 == s, pltpu.roll(rounded, 8 * s + 4, axis=1), edges)
            wide = edges.astype(F32)
            folded.append(wide[: channels // 2] + pltpu.roll(wide[channels // 2 :], 8 * cap, axis=1))
        for j in range(ring):
            both = jnp.where(near, folded[j - 1], folded[(j + 1) % ring])
            out[g * ring + j, cap * channels :, :] = both.astype(BF)
        send = pltpu.make_async_copy(
            out.at[pl.ds(g * ring, ring)], out_hbm.at[pl.ds(g * ring, ring)], out_sem.at[g]
        )
        send.start()
        sends.append(send)
    for send in sends:
        send.wait()


def prepare_kernel(
    flag_ref, hidden_hbm, cell_hbm, target_hbm, count_hbm, rows_ref, edge_ref, outer_ref, inner_ref,
    hidden, cell, target_ref, count_ref, sems,
):
    fetches = [
        pltpu.make_async_copy(source, target, sems.at[i])
        for i, (source, target) in enumerate(
            [(target_hbm, target_ref), (count_hbm, count_ref), (hidden_hbm, hidden), (cell_hbm, cell)]
        )
    ]
    for fetch in fetches:
        fetch.start()
    units, row_count, _ = hidden.shape
    fetches[0].wait()
    fetches[1].wait()
    edge_ref[2 * units :, :LANES] = marks_of(target_ref[...], count_ref[...]).astype(BF)
    edge_ref[2 * units :, LANES:] = jnp.zeros((target_ref.shape[1], STRIP - LANES), BF)
    fetches[2].wait()
    rows_ref[:, :units, :] = jnp.swapaxes(hidden[...], 0, 1)
    fetches[3].wait()
    rows_ref[:, units:, :] = jnp.swapaxes(cell[...], 0, 1)
    hidden_rows = rows_ref[:3, :units], rows_ref[row_count - 3 :, :units]
    cell_rows = rows_ref[:2, units:], rows_ref[row_count - 2 :, units:]
    outer_ref[:3], inner_ref[:3] = for_partners(flag_ref[2], *hidden_rows)
    outer_ref[3:], inner_ref[3:] = for_partners(flag_ref[2], *cell_rows)
    tiles = edge_tiles(lambda y: rows_ref[y], row_count, 2 * units)
    for t, tile in enumerate(tiles):
        edge_ref[: 2 * units, t * LANES : (t + 1) * LANES] = tile


def marks_of(target, live_count):
    cap, sources = target.shape
    slot = lax.broadcasted_iota(jnp.int32, target.shape, 0)
    live = slot < live_count
    row = target // 2
    odd = target % 2 == 1
    picked = [jnp.where(live & odd, row, -1), jnp.where(live & ~odd, row, -1)]
    rows = jnp.concatenate([p.astype(F32) for p in picked], axis=0)
    lane = lane_of((2 * cap, LANES))
    which = lax.broadcasted_iota(jnp.int32, (2 * cap, LANES), 0)
    spread = (lane // 8 % cap == which % cap) & ((lane % 8 < 4) == (which < cap))
    return lax.dot_general(
        rows.astype(BF),
        jnp.where(spread, 1.0, 0.0).astype(BF),
        (((0,), (0,)), ((), ())),
        preferred_element_type=F32,
    )


def strips_of(own, from_left, from_right):
    near = lane_of(own.shape) % 8 < 4
    return jnp.where(near, from_left, own), jnp.where(near, own, from_right)


def pack_strips(left, right):
    return jnp.where(lane_of(left.shape) < 64, left, pltpu.roll(right, 64, axis=1))


def full_strip(strip, above, below):
    lane = lane_of(above.shape)
    from_above = (lane >= 8) & (lane < 32)
    from_below = (lane >= 32) & (lane < 56)
    parts = []
    for side in range(2):
        base = side * STRIP
        if side:
            above, below = pltpu.roll(above, 64, axis=1), pltpu.roll(below, 64, axis=1)
        parts.append(jnp.where(from_above, above, strip[:, base : base + LANES]))
        parts.append(strip[:, base + LANES : base + 2 * LANES])
        parts.append(jnp.where(from_below, below, strip[:, base + 2 * LANES : base + STRIP]))
    return jnp.concatenate(parts, axis=1)


def strip_taps(strip):
    width = strip.shape[1]
    taps = []
    for a in range(3):
        for e in range(3):
            shift = 8 * (a - 1) + e - 1
            taps.append(strip if shift == 0 else pltpu.roll(strip, -shift % width, axis=1))
    return jnp.concatenate(taps, axis=0)


def patches_of(strip, tiles, first, last):
    channels = strip.shape[0]
    beside_left = lane_of((channels, LANES)) % 8 == 3
    found = {}
    for i, t in enumerate(tiles):
        left = strip[:, i * LANES : (i + 1) * LANES]
        right = strip[:, (len(tiles) + i) * LANES : (len(tiles) + i + 1) * LANES]
        mixed = jnp.where(beside_left, left, pltpu.roll(right, LANES - 2, axis=1))
        for r in range(max(first, 16 * t), min(last, 16 * t + 16)):
            found[r] = pltpu.roll(mixed, -(8 * (r % 16) + 3) % LANES, axis=1)
    return found


def store_patches(strip, patch_ref, first, last):
    for r, patch in patches_of(strip, range(STRIP // LANES), first, last).items():
        patch_ref[r] = patch


def store_three(ref, r, row, patch):
    channels = row.shape[0]
    lane = lane_of((channels, LANES))
    head, tail = row[:, :LANES], row[:, LANES:]
    first, last = lane == 0, lane == LANES - 1
    head_up, tail_up = pltpu.roll(head, 1, axis=1), pltpu.roll(tail, 1, axis=1)
    ref[r, :channels, :LANES] = jnp.where(first, patch, head_up)
    ref[r, :channels, LANES:] = jnp.where(first, head_up, tail_up)
    ref[r, channels : 2 * channels, :] = row
    head_down, tail_down = pltpu.roll(head, LANES - 1, axis=1), pltpu.roll(tail, LANES - 1, axis=1)
    ref[r, 2 * channels :, :LANES] = jnp.where(last, tail_down, head_down)
    ref[r, 2 * channels :, LANES:] = jnp.where(last, patch, tail_down)


def row_taps(ref, r):
    channels = ref.shape[1]
    return ref[pl.ds(r - 1, 3)].reshape(3 * channels, ref.shape[2])


def matmul(weights, taps):
    return jnp.dot(weights, taps, preferred_element_type=F32)


def for_partners(odd, up, down):
    odd = odd == 1
    return jnp.where(odd, up, down), jnp.where(odd, down, up)


def state_kernel(
    rows_ref, edge_ref, left_ref, right_ref, weight_ref, bias_ref,
    gates_hbm, wide_bias_ref, strip_ref, mark_ref,
    gates, three, patches, sems,
):
    units = rows_ref.shape[1] // 2
    count = rows_ref.shape[0]
    wide_bias_ref[...] = jnp.broadcast_to(bias_ref[...], wide_bias_ref.shape)
    channels = 2 * units
    left, right = strips_of(edge_ref[:channels], left_ref[:channels], right_ref[:channels])
    strip_ref[:, :STRIP] = left
    strip_ref[:, STRIP:] = right
    near = lane_of(mark_ref.shape) % 8 < 4
    from_left = left_ref[channels:, :LANES].astype(F32)
    mark_ref[...] = jnp.where(near, from_left, right_ref[channels:, :LANES].astype(F32))
    strip = jnp.concatenate([left[:units], right[:units]], axis=1)
    store_patches(strip, patches, PAD, count + PAD)
    for y in range(count):
        store_three(three, y + PAD, rows_ref[y, :units], patches[y + PAD])
    sends = pieces(gates, gates_hbm, sems)
    for y in range(1, count - 1):
        gates[y - 1] = matmul(weight_ref[...], row_taps(three, y + PAD))
        if y % PIECE == 0:
            sends[y // PIECE - 1].start()
    for send in sends:
        send.wait()


def pieces(source, target, sems):
    count = source.shape[0] // PIECE
    spots = [pl.ds(i * PIECE, PIECE) for i in range(count)]
    return [pltpu.make_async_copy(source.at[s], target.at[s], sems.at[i]) for i, s in enumerate(spots)]


def update(gates, memory):
    units = memory.shape[0]
    ingate = 0.5 * jnp.tanh(gates[:units]) + 0.5
    forget = 0.5 * jnp.tanh(gates[units : 2 * units]) + 0.5
    outgate = 0.5 * jnp.tanh(gates[2 * units : 3 * units]) + 0.5
    memory = forget * memory + ingate * jnp.tanh(gates[3 * units :])
    return outgate * jnp.tanh(memory), memory


def early_kernel(
    gates_hbm, rows_ref, forcing_ref, forcing_strip_ref, in_weight_ref, bias_ref,
    sums_ref, hidden_ref, memory_ref, gates, f_three, f_patches, sems,
):
    units = hidden_ref.shape[1]
    count = rows_ref.shape[0]
    bias = bias_ref[...]
    fetches = pieces(gates_hbm, gates, sems)
    for fetch in fetches:
        fetch.start()
    store_patches(forcing_strip_ref[...], f_patches, PAD, count + PAD)
    for y in range(count):
        store_three(f_three, y + PAD, forcing_ref[y], f_patches[y + PAD])
    for i in range(count - 2):
        if i % PIECE == 0:
            fetches[i // PIECE].wait()
        sums = matmul(in_weight_ref[...], row_taps(f_three, i + 1 + PAD)) + bias
        hidden, memory = update(gates[i] + sums, rows_ref[i + 1, units:].astype(F32))
        sums_ref[i] = sums
        hidden_ref[i] = hidden.astype(BF)
        memory_ref[i] = memory


def edge_rows(count, depth, many):
    top = [PAD + depth + i for i in range(many)]
    return top + [PAD + count - 1 - depth - (many - 1) + i for i in range(many)]


def late_kernel(
    flag_ref, rows_ref, strip_ref, forcing_ref, forcing_strip_ref,
    outer_ref, inner_ref, f_outer_ref, f_inner_ref, in_weight_ref, weight_ref, bias_ref,
    inner_sums_ref, inner_hidden_ref, inner_memory_ref,
    hidden_hbm, cell_hbm,
    f_three, three, first, second, sums, memory, patches, h_rows, c_rows, h_out, c_out, sems,
):
    units = rows_ref.shape[1] // 2
    count = rows_ref.shape[0]
    channels = forcing_ref.shape[1]
    has_above = flag_ref[0].astype(F32)
    has_below = flag_ref[1].astype(F32)
    bf_above, bf_below = has_above.astype(BF), has_below.astype(BF)
    bias = bias_ref[...]

    above, below = for_partners(flag_ref[2], outer_ref[...], inner_ref[...])
    f_above, f_below = for_partners(flag_ref[2], f_outer_ref[...], f_inner_ref[...])

    def strips_in(message, present):
        packed = message[3 * channels :] * present
        return jnp.concatenate([packed[:, :LANES], packed[channels:, LANES:]], axis=0)

    joined = jnp.concatenate([forcing_strip_ref[...], strip_ref[...]], axis=0)
    joined = full_strip(joined, strips_in(f_above, bf_above), strips_in(f_below, bf_below))
    strip_forcing = matmul(in_weight_ref[...], strip_taps(joined[:channels]))
    strip_forcing = strip_forcing + jnp.concatenate([bias] * 3, axis=1)
    state_strip = joined[channels : channels + units]
    strip_gates = strip_forcing + matmul(weight_ref[...], strip_taps(state_strip))
    found = patches_of(joined[: channels + units], range(STRIP // LANES), 1, PAD + 2)
    found.update(patches_of(joined[: channels + units], range(STRIP // LANES), count + PAD - 2, count + PAD + 3))

    def place(r, forcing, hidden):
        store_three(f_three, r, forcing, found[r][:channels])
        store_three(three, r, hidden, found[r][channels:])

    for i in range(3):
        line = slice(i * channels, (i + 1) * channels)
        place(1 + i, f_above[line] * bf_above, above[i] * bf_above)
        place(count + PAD + i, f_below[line] * bf_below, below[i] * bf_below)
    for r in edge_rows(count, 0, 2):
        place(r, forcing_ref[r - PAD], rows_ref[r - PAD, :units])

    lane = lane_of((units, 2 * STRIP))
    row_of_lane = lane % STRIP // 8
    keep = jnp.where(row_of_lane < PAD, has_above, 1.0)
    keep = jnp.where(row_of_lane >= PAD + count, has_below, keep)

    def kept(hidden, r):
        if r < PAD:
            hidden = hidden * has_above
        elif r >= PAD + count:
            hidden = hidden * has_below
        return hidden.astype(BF)

    strip_hidden, strip_memory = update(strip_gates, joined[channels + units :].astype(F32))
    strip_hidden = (strip_hidden * keep).astype(BF)
    store_patches(strip_hidden, patches, 2, count + 6)
    olds = [above[3], above[4], rows_ref[0, units:]]
    olds += [rows_ref[count - 1, units:], below[3], below[4]]
    for r, old in zip(edge_rows(count, -2, 3), olds):
        sums[r] = matmul(in_weight_ref[...], row_taps(f_three, r)) + bias
        first_gates = sums[r] + matmul(weight_ref[...], row_taps(three, r))
        hidden, memory[r] = update(first_gates, old.astype(F32))
        store_three(first, r, kept(hidden, r), patches[r])
    inner = range(PAD + 1, PAD + count - 1)
    for i, r in enumerate(inner):
        store_three(first, r, inner_hidden_ref[i], patches[r])

    strip_gates = matmul(weight_ref[...], strip_taps(strip_hidden)) + strip_forcing
    strip_hidden, strip_memory = update(strip_gates, strip_memory)
    strip_hidden = (strip_hidden * keep).astype(BF)
    store_patches(strip_hidden, patches, 3, count + 5)

    def later(source, r, old):
        total = inner_sums_ref[r - PAD - 1] if r in inner else sums[r]
        return update(total + matmul(weight_ref[...], row_taps(source, r)), old)

    for r in range(PAD - 1, PAD + count + 1):
        old = inner_memory_ref[r - PAD - 1] if r in inner else memory[r]
        hidden, memory[r] = later(first, r, old)
        store_three(second, r, kept(hidden, r), patches[r])

    sends = []
    part = count // 2
    for start in (0, part):
        for y in range(start, start + part):
            hidden, new = later(second, y + PAD, memory[y + PAD])
            h_rows[y] = hidden.astype(BF)
            c_rows[y] = new.astype(BF)
        spot = pl.ds(start, part)
        h_out[:, start : start + part, :] = jnp.swapaxes(h_rows[start : start + part], 0, 1)
        c_out[:, start : start + part, :] = jnp.swapaxes(c_rows[start : start + part], 0, 1)
        for source, target in ((h_out, hidden_hbm), (c_out, cell_hbm)):
            sends.append(pltpu.make_async_copy(source.at[:, spot], target.at[:, spot], sems.at[len(sends)]))
            sends[-1].start()
    for send in sends:
        send.wait()


def beside(incoming_ref, mark_ref, row_count, channels):
    sources = incoming_ref.shape[0]
    base = incoming_ref.shape[1] - channels // 2
    lane = lane_of((channels // 2, LANES))
    group_lanes = 8 * ((base // channels) % 16)
    tiles = [[jnp.zeros((channels // 2, LANES), F32) for _ in range(2)] for _ in range(STRIP // LANES)]
    for start in range(0, row_count, 16):
        sums = [jnp.zeros((channels // 2, LANES), F32) for _ in range(16)]
        for p in range(sources):
            edges = incoming_ref[p, base:, :].astype(F32)
            mark = jnp.broadcast_to(mark_ref[p : p + 1, :], edges.shape)
            for i in range(16):
                sums[i] = sums[i] + jnp.where(mark == float(start + i), edges, 0.0)
        for i in range(16):
            total = sums[i] + pltpu.roll(sums[i], LANES - 8, axis=1)
            total = total + pltpu.roll(total, LANES - 16, axis=1)
            r = start + i + PAD
            for part in range(2):
                moved = pltpu.roll(total, (8 * (r % 16) - part * group_lanes) % LANES, axis=1)
                tiles[r // 16][part] = jnp.where(lane // 8 == r % 16, moved, tiles[r // 16][part])
    halves = [jnp.concatenate([t[part] for t in tiles], axis=1) for part in range(2)]
    return jnp.concatenate(halves, axis=0).astype(BF)


def scatter_kernel(
    flag_ref, target_ref, count_ref, incoming_ref, mark_ref, state_strip_ref,
    rows_ref, strip_ref, outer_ref, inner_ref, *totals,
):
    cap, sources = target_ref.shape
    row_count, channels, width = rows_ref.shape
    width = width // 2
    spare = 2 * row_count
    for total in totals:
        total[...] = jnp.zeros(total.shape, F32)
    for p in range(sources):
        live = count_ref[0, p]
        for s in range(cap):
            block = jnp.where(s < live, target_ref[s, p], spare)
            total = totals[s % len(totals)]
            total[block] = total[block] + incoming_ref[p, s * channels : (s + 1) * channels, :].astype(F32)
    for y in range(row_count):
        for half in range(2):
            block = sum(total[2 * y + half] for total in totals)
            rows_ref[y, :, half * width : (half + 1) * width] = block.astype(BF)
    own = jnp.concatenate(edge_tiles(lambda y: rows_ref[y], row_count, channels), axis=1)
    others = beside(incoming_ref, mark_ref, row_count, channels)
    left, right = strips_of(own, others, others)
    strip_ref[:, :STRIP] = left
    strip_ref[:, STRIP:] = right
    state = state_strip_ref.shape[0] // 2
    messages = []
    for first, tile in ((0, 0), (row_count - 3, 2)):
        lines = [rows_ref[first + i] for i in range(3)]
        spots = [slice(base + tile * LANES, base + (tile + 1) * LANES) for base in (0, STRIP)]
        packed = pack_strips(*[state_strip_ref[:, spot] for spot in spots])
        own_packed = pack_strips(left[:, spots[0]], right[:, spots[0]])
        halves = [jnp.concatenate([own_packed, part], axis=0) for part in (packed[:state], packed[state:])]
        messages.append(jnp.concatenate([*lines, jnp.concatenate(halves, axis=1)], axis=0))
    outer_ref[...], inner_ref[...] = for_partners(flag_ref[2], *messages)


def around(count):
    return [(i, (i + 1) % count) for i in range(count)]


def back(count):
    return [((i + 1) % count, i) for i in range(count)]


def exchange_columns(edge):
    count = lax.axis_size("lon")
    from_left = lax.ppermute(edge, "lon", around(count))
    from_right = lax.ppermute(edge, "lon", back(count))
    return from_left, from_right


def exchange_rows(outer, inner):
    count = lax.axis_size("lat")

    def swap(x, first):
        partner = list(range(count))
        for i in range(first, count - 1, 2):
            partner[i], partner[i + 1] = i + 1, i
        return lax.ppermute(x, "lat", list(enumerate(partner)))

    got_outer = swap(outer, 0)
    got_inner = swap(inner, 1)
    return got_outer, got_inner


def on_device(
    satellite_blocks,
    slot_source,
    slot_weight,
    slot_target,
    tile_counts,
    gate_input_weight,
    gate_state_weight,
    gate_bias,
    hidden_init,
    cell_init,
):
    _, tiles, cap, band, block = slot_weight.shape
    channels = satellite_blocks.shape[1]
    units, row_count, column_count = hidden_init.shape
    gates = gate_bias.shape[0]
    slots = tiles * cap
    half = jnp.where(jnp.arange(gates) < 3 * units, 0.5, 1.0)
    in_weight = gate_input_weight * half[:, None].astype(BF)
    state_weight = gate_state_weight * half[:, None].astype(BF)
    bias = (gate_bias * half)[:, None]
    lat = lax.axis_index("lat")
    flags = jnp.stack([lat > 0, lat < lax.axis_size("lat") - 1, lat % 2 == 1]).astype(jnp.int32)

    ring = lax.axis_size("lon")
    height = cap * channels + channels // 2
    message = jax.ShapeDtypeStruct((tiles, height, block), BF)
    groups = tiles // ring
    outgoing = pl.pallas_call(
        functools.partial(gather_kernel, ring),
        out_shape=pltpu.HBM(message.shape, BF),
        in_specs=[pl.BlockSpec(memory_space=pl.ANY)] * 3,
        out_specs=pl.BlockSpec(memory_space=pl.ANY),
        scratch_shapes=[
            pltpu.VMEM(satellite_blocks.shape, BF),
            pltpu.VMEM((slots, band, block), BF),
            pltpu.VMEM(message.shape, BF),
            pltpu.SMEM((cap, tiles), jnp.int32),
            pltpu.SemaphoreType.DMA,
            pltpu.SemaphoreType.DMA,
            pltpu.SemaphoreType.DMA((groups,)),
            pltpu.SemaphoreType.DMA((groups,)),
        ],
        compiler_params=pltpu.CompilerParams(vmem_limit_bytes=8 * 2**20),
        name="gather_band",
    )(in_hbm(slot_source[0].T), in_hbm(satellite_blocks), in_hbm(slot_weight.reshape(slots, band, block)))
    incoming = lax.all_to_all(outgoing, ("lat", "lon"), split_axis=0, concat_axis=0, tiled=True)

    ends = jax.ShapeDtypeStruct((5, units, column_count), BF)
    rows, edge, outer, inner = pl.pallas_call(
        prepare_kernel,
        out_shape=(
            jax.ShapeDtypeStruct((row_count, 2 * units, column_count), BF),
            jax.ShapeDtypeStruct((2 * units + tiles, STRIP), BF),
            ends,
            ends,
        ),
        in_specs=scalars(1) + [pl.BlockSpec(memory_space=pl.ANY)] * 4,
        out_specs=tuple(whole(4)),
        scratch_shapes=[
            pltpu.VMEM(hidden_init.shape, BF),
            pltpu.VMEM(cell_init.shape, BF),
            pltpu.VMEM((cap, tiles), jnp.int32),
            pltpu.VMEM((1, tiles), jnp.int32),
            pltpu.SemaphoreType.DMA((4,)),
        ],
        compiler_params=pltpu.CompilerParams(vmem_limit_bytes=8 * 2**20),
        name="prepare",
    )(flags, in_hbm(hidden_init), in_hbm(cell_init), in_hbm(slot_target[0].T), in_hbm(tile_counts))
    from_left, from_right = exchange_columns(edge)
    outer, inner = exchange_rows(outer, inner)
    padded = row_count + 8
    inside = (row_count - 2, gates, column_count)
    parts = inside[0] // PIECE
    state_gates, bias, strip, marks = call(
        state_kernel,
        [
            pltpu.HBM(inside, F32),
            jax.ShapeDtypeStruct((gates, column_count), F32),
            jax.ShapeDtypeStruct((2 * units, 2 * STRIP), BF),
            jax.ShapeDtypeStruct((tiles, LANES), F32),
        ],
        6, 0,
        [
            pltpu.VMEM(inside, F32),
            pltpu.VMEM((padded, 3 * units, column_count), BF),
            pltpu.VMEM((padded, units, LANES), BF),
            pltpu.SemaphoreType.DMA((parts,)),
        ],
        "state_gates", 2 * gates * 9 * units * row_count * column_count,
        (rows, edge, from_left, from_right, state_weight, bias), 16,
        out_specs=[pl.BlockSpec(memory_space=pl.ANY)] + whole(3),
    )
    incoming, state_gates, bias, in_weight = lax.optimization_barrier((incoming, state_gates, bias, in_weight))

    ends = jax.ShapeDtypeStruct((4 * channels + units, column_count), BF)
    forcing, forcing_strip, f_outer, f_inner = call(
        scatter_kernel,
        [
            jax.ShapeDtypeStruct((row_count, channels, column_count), BF),
            jax.ShapeDtypeStruct((channels, 2 * STRIP), BF),
            ends,
            ends,
        ],
        3, 3,
        [pltpu.VMEM((2 * row_count + 1, channels, block), F32)] * 4,
        "scatter_add", slots * channels * block,
        (flags, slot_target[0].T, tile_counts, incoming, marks, strip),
    )
    f_outer, f_inner = exchange_rows(f_outer, f_inner)
    sums, hidden, memory = call(
        early_kernel,
        [
            jax.ShapeDtypeStruct(inside, F32),
            jax.ShapeDtypeStruct((inside[0], units, column_count), BF),
            jax.ShapeDtypeStruct((inside[0], units, column_count), F32),
        ],
        6, 0,
        [
            pltpu.VMEM(inside, F32),
            pltpu.VMEM((padded, 3 * channels, column_count), BF),
            pltpu.VMEM((padded, channels, LANES), BF),
            pltpu.SemaphoreType.DMA((parts,)),
        ],
        "first_step", 2 * gates * 9 * channels * row_count * column_count,
        (in_hbm(state_gates), rows, forcing, forcing_strip, in_weight, bias), 16,
        in_specs=[pl.BlockSpec(memory_space=pl.ANY)] + whole(5),
    )
    return call(
        late_kernel,
        [pltpu.HBM(hidden_init.shape, BF)] * 2,
        14, 1,
        [
            pltpu.VMEM((padded, 3 * channels, column_count), BF),
            pltpu.VMEM((padded, 3 * units, column_count), BF),
            pltpu.VMEM((padded, 3 * units, column_count), BF),
            pltpu.VMEM((padded, 3 * units, column_count), BF),
            pltpu.VMEM((padded, gates, column_count), F32),
            pltpu.VMEM((padded, units, column_count), F32),
            pltpu.VMEM((padded, units, LANES), BF),
            pltpu.VMEM((row_count, units, column_count), BF),
            pltpu.VMEM((row_count, units, column_count), BF),
            pltpu.VMEM(hidden_init.shape, BF),
            pltpu.VMEM(hidden_init.shape, BF),
            pltpu.SemaphoreType.DMA((4,)),
        ],
        "later_steps", 2 * gates * 9 * 2 * units * row_count * column_count,
        (flags, rows, strip, forcing, forcing_strip, outer, inner, f_outer, f_inner,
         in_weight, state_weight, bias, sums, hidden, memory), 24,
        out_specs=[pl.BlockSpec(memory_space=pl.ANY)] * 2,
    )


def solution(mesh):
    placed = (
        P(("lat", "lon"), None, None),
        P(("lat", "lon"), None, None),
        P(("lat", "lon"), None, None, None, None),
        P(("lat", "lon"), None, None),
        P(("lat", "lon"), None),
        P(),
        P(),
        P(),
        P(None, "lat", "lon"),
        P(None, "lat", "lon"),
    )
    return jax.shard_map(
        on_device,
        mesh=mesh,
        in_specs=placed,
        out_specs=(P(None, "lat", "lon"), P(None, "lat", "lon")),
        check_vma=False,
    )
```

```python
import functools

import jax
import jax.numpy as jnp
from jax import lax
from jax.experimental import pallas as pl
from jax.experimental.pallas import tpu as pltpu
from jax.sharding import PartitionSpec as P

STEPS = 3
PAD = 4
LANES = 128
STRIP = 3 * LANES
BATCH = 2
PIECE = 6
BF = jnp.bfloat16
F32 = jnp.float32


def lane_of(shape):
    return lax.broadcasted_iota(jnp.int32, shape, len(shape) - 1)


def whole(count):
    return [pl.BlockSpec(memory_space=pltpu.VMEM)] * count


def in_hbm(x):
    return pltpu.with_memory_space_constraint(x, pltpu.HBM)


def scalars(count):
    return [pl.BlockSpec(memory_space=pltpu.SMEM)] * count


def call(
    kernel, outs, ins, scalar_count, scratch, name, flops, args, mib=8, in_specs=None, out_specs=None
):
    nbytes = sum(a.size * a.dtype.itemsize for a in args)
    return pl.pallas_call(
        kernel,
        out_shape=tuple(outs),
        in_specs=in_specs or scalars(scalar_count) + whole(ins),
        out_specs=tuple(out_specs or whole(len(outs))),
        scratch_shapes=scratch,
        compiler_params=pltpu.CompilerParams(vmem_limit_bytes=mib * 2**20),
        cost_estimate=pl.CostEstimate(flops=flops, bytes_accessed=nbytes, transcendentals=0),
        name=name,
    )(*args)


def edge_tiles(row_of, row_count, channels):
    lane = lane_of((channels, LANES))
    tiles = [jnp.zeros((channels, LANES), BF) for _ in range(STRIP // LANES)]
    for y in range(row_count):
        row = row_of(y)
        both = jnp.where(lane < 64, row[:, :LANES], row[:, -LANES:])
        r = y + PAD
        place = r % 16
        turned = pltpu.roll(both, (8 * place + 4) % LANES, axis=1)
        tiles[r // 16] = jnp.where(lane // 8 == place, turned, tiles[r // 16])
    return tiles


def gather_kernel(
    ring, source_hbm, blocks_hbm, weight_hbm, out_hbm, blocks, weights, out, source_ref, source_sem, block_sem, weight_sem, out_sem
):
    cap, tiles = source_ref.shape
    band, width = weights.shape[1:]
    channels = blocks.shape[1]
    groups = tiles // ring
    share = ring * cap
    fetch = pltpu.make_async_copy(blocks_hbm, blocks, block_sem)
    fetch.start()
    places = pltpu.make_async_copy(source_hbm, source_ref, source_sem)
    places.start()
    parts = [
        pltpu.make_async_copy(
            weight_hbm.at[pl.ds(g * share, share)], weights.at[pl.ds(g * share, share)], weight_sem.at[g]
        )
        for g in range(groups)
    ]
    for part in parts:
        part.start()
    offset = lax.broadcasted_iota(jnp.int32, (band, width), 0) - band // 2
    spot = lane_of((band, width)) + offset
    inside = (spot >= 0) & (spot < width)
    lane = lane_of((channels, width))
    near = lane_of((channels // 2, width)) % 8 < 4
    places.wait()
    fetch.wait()
    sends = []
    for g in range(groups):
        parts[g].wait()
        folded = []
        for j in range(ring):
            q = g * ring + j
            for s in range(cap):
                block = blocks[source_ref[s, q]]
                factor = jnp.where(inside, weights[q * cap + s].astype(F32), 0.0)
                total = jnp.zeros((channels, width), F32)
                for k in range(band):
                    moved = block if k == band // 2 else pltpu.roll(block, (band // 2 - k) % width, axis=1)
                    total = total + factor[k : k + 1, :] * moved.astype(F32)
                rounded = total.astype(BF)
                out[q, s * channels : (s + 1) * channels, :] = rounded
        for j in range(ring):
            edges = jnp.zeros((channels, width), BF)
            for s in range(cap):
                rounded = out[g * ring + j, s * channels : (s + 1) * channels, :]
                edges = jnp.where(lane // 8 == s, pltpu.roll(rounded, 8 * s + 4, axis=1), edges)
            wide = edges.astype(F32)
            folded.append(wide[: channels // 2] + pltpu.roll(wide[channels // 2 :], 8 * cap, axis=1))
        for j in range(ring):
            both = jnp.where(near, folded[j - 1], folded[(j + 1) % ring])
            both = jnp.concatenate([both, jnp.zeros_like(both)], axis=0)
            out[g * ring + j, cap * channels :, :] = both.astype(BF)
        send = pltpu.make_async_copy(
            out.at[pl.ds(g * ring, ring)], out_hbm.at[pl.ds(g * ring, ring)], out_sem.at[g]
        )
        send.start()
        sends.append(send)
    for send in sends:
        send.wait()


def prepare_kernel(
    flag_ref, hidden_hbm, cell_hbm, target_hbm, count_hbm, rows_ref, edge_ref, outer_ref, inner_ref,
    hidden, cell, target_ref, count_ref, sems,
):
    fetches = [
        pltpu.make_async_copy(source, target, sems.at[i])
        for i, (source, target) in enumerate(
            [(target_hbm, target_ref), (count_hbm, count_ref), (hidden_hbm, hidden), (cell_hbm, cell)]
        )
    ]
    for fetch in fetches:
        fetch.start()
    units, row_count, _ = hidden.shape
    fetches[0].wait()
    fetches[1].wait()
    edge_ref[2 * units :, :LANES] = marks_of(target_ref[...], count_ref[...]).astype(BF)
    edge_ref[2 * units :, LANES:] = jnp.zeros((target_ref.shape[1], STRIP - LANES), BF)
    fetches[2].wait()
    rows_ref[:, :units, :] = jnp.swapaxes(hidden[...], 0, 1)
    fetches[3].wait()
    rows_ref[:, units:, :] = jnp.swapaxes(cell[...], 0, 1)
    hidden_rows = rows_ref[:3, :units], rows_ref[row_count - 3 :, :units]
    cell_rows = rows_ref[:2, units:], rows_ref[row_count - 2 :, units:]
    outer_ref[:3], inner_ref[:3] = for_partners(flag_ref[2], *hidden_rows)
    outer_ref[3:], inner_ref[3:] = for_partners(flag_ref[2], *cell_rows)
    tiles = edge_tiles(lambda y: rows_ref[y], row_count, 2 * units)
    for t, tile in enumerate(tiles):
        edge_ref[: 2 * units, t * LANES : (t + 1) * LANES] = tile


def marks_of(target, live_count):
    cap, sources = target.shape
    slot = lax.broadcasted_iota(jnp.int32, target.shape, 0)
    live = slot < live_count
    row = target // 2
    odd = target % 2 == 1
    picked = [jnp.where(live & odd, row, -1), jnp.where(live & ~odd, row, -1)]
    rows = jnp.concatenate([p.astype(F32) for p in picked], axis=0)
    lane = lane_of((2 * cap, LANES))
    which = lax.broadcasted_iota(jnp.int32, (2 * cap, LANES), 0)
    spread = (lane // 8 % cap == which % cap) & ((lane % 8 < 4) == (which < cap))
    return lax.dot_general(
        rows.astype(BF),
        jnp.where(spread, 1.0, 0.0).astype(BF),
        (((0,), (0,)), ((), ())),
        preferred_element_type=F32,
    )


def strips_of(own, from_left, from_right):
    near = lane_of(own.shape) % 8 < 4
    return jnp.where(near, from_left, own), jnp.where(near, own, from_right)


def pack_strips(left, right):
    return jnp.where(lane_of(left.shape) < 64, left, pltpu.roll(right, 64, axis=1))


def full_strip(strip, above, below):
    lane = lane_of(above.shape)
    from_above = (lane >= 8) & (lane < 32)
    from_below = (lane >= 32) & (lane < 56)
    parts = []
    for side in range(2):
        base = side * STRIP
        if side:
            above, below = pltpu.roll(above, 64, axis=1), pltpu.roll(below, 64, axis=1)
        parts.append(jnp.where(from_above, above, strip[:, base : base + LANES]))
        parts.append(strip[:, base + LANES : base + 2 * LANES])
        parts.append(jnp.where(from_below, below, strip[:, base + 2 * LANES : base + STRIP]))
    return jnp.concatenate(parts, axis=1)


def strip_taps(strip):
    width = strip.shape[1]
    taps = []
    for a in range(3):
        for e in range(3):
            shift = 8 * (a - 1) + e - 1
            taps.append(strip if shift == 0 else pltpu.roll(strip, -shift % width, axis=1))
    return jnp.concatenate(taps, axis=0)


def patches_of(strip, tiles, first, last):
    channels = strip.shape[0]
    beside_left = lane_of((channels, LANES)) % 8 == 3
    found = {}
    for i, t in enumerate(tiles):
        left = strip[:, i * LANES : (i + 1) * LANES]
        right = strip[:, (len(tiles) + i) * LANES : (len(tiles) + i + 1) * LANES]
        mixed = jnp.where(beside_left, left, pltpu.roll(right, LANES - 2, axis=1))
        for r in range(max(first, 16 * t), min(last, 16 * t + 16)):
            found[r] = pltpu.roll(mixed, -(8 * (r % 16) + 3) % LANES, axis=1)
    return found


def store_patches(strip, patch_ref, first, last):
    for r, patch in patches_of(strip, range(STRIP // LANES), first, last).items():
        patch_ref[r] = patch


def store_three(ref, r, row, patch):
    channels = row.shape[0]
    lane = lane_of((channels, LANES))
    head, tail = row[:, :LANES], row[:, LANES:]
    first, last = lane == 0, lane == LANES - 1
    head_up, tail_up = pltpu.roll(head, 1, axis=1), pltpu.roll(tail, 1, axis=1)
    ref[r, :channels, :LANES] = jnp.where(first, patch, head_up)
    ref[r, :channels, LANES:] = jnp.where(first, head_up, tail_up)
    ref[r, channels : 2 * channels, :] = row
    head_down, tail_down = pltpu.roll(head, LANES - 1, axis=1), pltpu.roll(tail, LANES - 1, axis=1)
    ref[r, 2 * channels :, :LANES] = jnp.where(last, tail_down, head_down)
    ref[r, 2 * channels :, LANES:] = jnp.where(last, patch, tail_down)


def row_taps(ref, r):
    channels = ref.shape[1]
    return ref[pl.ds(r - 1, 3)].reshape(3 * channels, ref.shape[2])


def matmul(weights, taps):
    return jnp.dot(weights, taps, preferred_element_type=F32)


def for_partners(odd, up, down):
    odd = odd == 1
    return jnp.where(odd, up, down), jnp.where(odd, down, up)


def state_kernel(
    rows_ref, edge_ref, left_ref, right_ref, weight_ref, bias_ref,
    gates_hbm, wide_bias_ref, strip_ref, mark_ref,
    gates, three, patches, sems,
):
    units = rows_ref.shape[1] // 2
    count = rows_ref.shape[0]
    wide_bias_ref[...] = jnp.broadcast_to(bias_ref[...], wide_bias_ref.shape)
    channels = 2 * units
    left, right = strips_of(edge_ref[:channels], left_ref[:channels], right_ref[:channels])
    strip_ref[:, :STRIP] = left
    strip_ref[:, STRIP:] = right
    near = lane_of(mark_ref.shape) % 8 < 4
    from_left = left_ref[channels:, :LANES].astype(F32)
    mark_ref[...] = jnp.where(near, from_left, right_ref[channels:, :LANES].astype(F32))
    strip = jnp.concatenate([left[:units], right[:units]], axis=1)
    store_patches(strip, patches, PAD, count + PAD)
    for y in range(count):
        store_three(three, y + PAD, rows_ref[y, :units], patches[y + PAD])
    sends = pieces(gates, gates_hbm, sems)
    for y in range(1, count - 1):
        gates[y - 1] = matmul(weight_ref[...], row_taps(three, y + PAD))
        if y % PIECE == 0:
            sends[y // PIECE - 1].start()
    for send in sends:
        send.wait()


def pieces(source, target, sems):
    count = source.shape[0] // PIECE
    spots = [pl.ds(i * PIECE, PIECE) for i in range(count)]
    return [pltpu.make_async_copy(source.at[s], target.at[s], sems.at[i]) for i, s in enumerate(spots)]


def update(gates, memory):
    units = memory.shape[0]
    ingate = 0.5 * jnp.tanh(gates[:units]) + 0.5
    forget = 0.5 * jnp.tanh(gates[units : 2 * units]) + 0.5
    outgate = 0.5 * jnp.tanh(gates[2 * units : 3 * units]) + 0.5
    memory = forget * memory + ingate * jnp.tanh(gates[3 * units :])
    return outgate * jnp.tanh(memory), memory


def early_kernel(
    gates_hbm, rows_ref, forcing_ref, forcing_strip_ref, in_weight_ref, bias_ref,
    sums_ref, hidden_ref, memory_ref, gates, f_three, f_patches, sems,
):
    units = hidden_ref.shape[1]
    count = rows_ref.shape[0]
    bias = bias_ref[...]
    fetches = pieces(gates_hbm, gates, sems)
    for fetch in fetches:
        fetch.start()
    store_patches(forcing_strip_ref[...], f_patches, PAD, count + PAD)
    for y in range(count):
        store_three(f_three, y + PAD, forcing_ref[y], f_patches[y + PAD])
    for i in range(count - 2):
        if i % PIECE == 0:
            fetches[i // PIECE].wait()
        sums = matmul(in_weight_ref[...], row_taps(f_three, i + 1 + PAD)) + bias
        hidden, memory = update(gates[i] + sums, rows_ref[i + 1, units:].astype(F32))
        sums_ref[i] = sums
        hidden_ref[i] = hidden.astype(BF)
        memory_ref[i] = memory


def edge_rows(count, depth, many):
    top = [PAD + depth + i for i in range(many)]
    return top + [PAD + count - 1 - depth - (many - 1) + i for i in range(many)]


def late_kernel(
    flag_ref, rows_ref, strip_ref, forcing_ref, forcing_strip_ref,
    outer_ref, inner_ref, f_outer_ref, f_inner_ref, in_weight_ref, weight_ref, bias_ref,
    inner_sums_ref, inner_hidden_ref, inner_memory_ref,
    hidden_hbm, cell_hbm,
    f_three, three, first, second, sums, memory, patches, h_rows, c_rows, h_out, c_out, sems,
):
    units = rows_ref.shape[1] // 2
    count = rows_ref.shape[0]
    channels = forcing_ref.shape[1]
    has_above = flag_ref[0].astype(F32)
    has_below = flag_ref[1].astype(F32)
    bf_above, bf_below = has_above.astype(BF), has_below.astype(BF)
    bias = bias_ref[...]

    above, below = for_partners(flag_ref[2], outer_ref[...], inner_ref[...])
    f_above, f_below = for_partners(flag_ref[2], f_outer_ref[...], f_inner_ref[...])

    def strips_in(message, present):
        packed = message[3 * channels :] * present
        return jnp.concatenate([packed[:, :LANES], packed[channels:, LANES:]], axis=0)

    joined = jnp.concatenate([forcing_strip_ref[...], strip_ref[...]], axis=0)
    joined = full_strip(joined, strips_in(f_above, bf_above), strips_in(f_below, bf_below))
    strip_forcing = matmul(in_weight_ref[...], strip_taps(joined[:channels]))
    strip_forcing = strip_forcing + jnp.concatenate([bias] * 3, axis=1)
    state_strip = joined[channels : channels + units]
    strip_gates = strip_forcing + matmul(weight_ref[...], strip_taps(state_strip))
    found = patches_of(joined[: channels + units], range(STRIP // LANES), 1, PAD + 2)
    found.update(patches_of(joined[: channels + units], range(STRIP // LANES), count + PAD - 2, count + PAD + 3))

    def place(r, forcing, hidden):
        store_three(f_three, r, forcing, found[r][:channels])
        store_three(three, r, hidden, found[r][channels:])

    for i in range(3):
        line = slice(i * channels, (i + 1) * channels)
        place(1 + i, f_above[line] * bf_above, above[i] * bf_above)
        place(count + PAD + i, f_below[line] * bf_below, below[i] * bf_below)
    for r in edge_rows(count, 0, 2):
        place(r, forcing_ref[r - PAD], rows_ref[r - PAD, :units])

    lane = lane_of((units, 2 * STRIP))
    row_of_lane = lane % STRIP // 8
    keep = jnp.where(row_of_lane < PAD, has_above, 1.0)
    keep = jnp.where(row_of_lane >= PAD + count, has_below, keep)

    def kept(hidden, r):
        if r < PAD:
            hidden = hidden * has_above
        elif r >= PAD + count:
            hidden = hidden * has_below
        return hidden.astype(BF)

    strip_hidden, strip_memory = update(strip_gates, joined[channels + units :].astype(F32))
    strip_hidden = (strip_hidden * keep).astype(BF)
    store_patches(strip_hidden, patches, 2, count + 6)
    olds = [above[3], above[4], rows_ref[0, units:]]
    olds += [rows_ref[count - 1, units:], below[3], below[4]]
    for r, old in zip(edge_rows(count, -2, 3), olds):
        sums[r] = matmul(in_weight_ref[...], row_taps(f_three, r)) + bias
        first_gates = sums[r] + matmul(weight_ref[...], row_taps(three, r))
        hidden, memory[r] = update(first_gates, old.astype(F32))
        store_three(first, r, kept(hidden, r), patches[r])
    inner = range(PAD + 1, PAD + count - 1)
    for i, r in enumerate(inner):
        store_three(first, r, inner_hidden_ref[i], patches[r])

    strip_gates = matmul(weight_ref[...], strip_taps(strip_hidden)) + strip_forcing
    strip_hidden, strip_memory = update(strip_gates, strip_memory)
    strip_hidden = (strip_hidden * keep).astype(BF)
    store_patches(strip_hidden, patches, 3, count + 5)

    def later(source, r, old):
        total = inner_sums_ref[r - PAD - 1] if r in inner else sums[r]
        return update(total + matmul(weight_ref[...], row_taps(source, r)), old)

    for r in range(PAD - 1, PAD + count + 1):
        old = inner_memory_ref[r - PAD - 1] if r in inner else memory[r]
        hidden, memory[r] = later(first, r, old)
        store_three(second, r, kept(hidden, r), patches[r])

    sends = []
    part = count // 2
    for start in (0, part):
        for y in range(start, start + part):
            hidden, new = later(second, y + PAD, memory[y + PAD])
            h_rows[y] = hidden.astype(BF)
            c_rows[y] = new.astype(BF)
        spot = pl.ds(start, part)
        h_out[:, start : start + part, :] = jnp.swapaxes(h_rows[start : start + part], 0, 1)
        c_out[:, start : start + part, :] = jnp.swapaxes(c_rows[start : start + part], 0, 1)
        for source, target in ((h_out, hidden_hbm), (c_out, cell_hbm)):
            sends.append(pltpu.make_async_copy(source.at[:, spot], target.at[:, spot], sems.at[len(sends)]))
            sends[-1].start()
    for send in sends:
        send.wait()


def beside(incoming_ref, mark_ref, row_count, channels):
    sources = incoming_ref.shape[0]
    base = incoming_ref.shape[1] - channels
    lane = lane_of((channels // 2, LANES))
    group_lanes = 8 * ((base // channels) % 16)
    tiles = [[jnp.zeros((channels // 2, LANES), F32) for _ in range(2)] for _ in range(STRIP // LANES)]
    for start in range(0, row_count, 16):
        sums = [jnp.zeros((channels // 2, LANES), F32) for _ in range(16)]
        for p in range(sources):
            edges = incoming_ref[p, base:, :].astype(F32)[: channels // 2]
            mark = jnp.broadcast_to(mark_ref[p : p + 1, :], edges.shape)
            for i in range(16):
                sums[i] = sums[i] + jnp.where(mark == float(start + i), edges, 0.0)
        for i in range(16):
            total = sums[i] + pltpu.roll(sums[i], LANES - 8, axis=1)
            total = total + pltpu.roll(total, LANES - 16, axis=1)
            r = start + i + PAD
            for part in range(2):
                moved = pltpu.roll(total, (8 * (r % 16) - part * group_lanes) % LANES, axis=1)
                tiles[r // 16][part] = jnp.where(lane // 8 == r % 16, moved, tiles[r // 16][part])
    halves = [jnp.concatenate([t[part] for t in tiles], axis=1) for part in range(2)]
    return jnp.concatenate(halves, axis=0).astype(BF)


def scatter_kernel(
    flag_ref, target_ref, count_ref, incoming_ref, mark_ref, state_strip_ref,
    rows_ref, strip_ref, outer_ref, inner_ref, *totals,
):
    cap, sources = target_ref.shape
    row_count, channels, width = rows_ref.shape
    width = width // 2
    spare = 2 * row_count
    for total in totals:
        total[...] = jnp.zeros(total.shape, F32)
    for p in range(sources):
        live = count_ref[0, p]
        for s in range(cap):
            block = jnp.where(s < live, target_ref[s, p], spare)
            total = totals[s % len(totals)]
            total[block] = total[block] + incoming_ref[p, s * channels : (s + 1) * channels, :].astype(F32)
    for y in range(row_count):
        for half in range(2):
            block = sum(total[2 * y + half] for total in totals)
            rows_ref[y, :, half * width : (half + 1) * width] = block.astype(BF)
    own = jnp.concatenate(edge_tiles(lambda y: rows_ref[y], row_count, channels), axis=1)
    others = beside(incoming_ref, mark_ref, row_count, channels)
    left, right = strips_of(own, others, others)
    strip_ref[:, :STRIP] = left
    strip_ref[:, STRIP:] = right
    state = state_strip_ref.shape[0] // 2
    messages = []
    for first, tile in ((0, 0), (row_count - 3, 2)):
        lines = [rows_ref[first + i] for i in range(3)]
        spots = [slice(base + tile * LANES, base + (tile + 1) * LANES) for base in (0, STRIP)]
        packed = pack_strips(*[state_strip_ref[:, spot] for spot in spots])
        own_packed = pack_strips(left[:, spots[0]], right[:, spots[0]])
        halves = [jnp.concatenate([own_packed, part], axis=0) for part in (packed[:state], packed[state:])]
        messages.append(jnp.concatenate([*lines, jnp.concatenate(halves, axis=1)], axis=0))
    outer_ref[...], inner_ref[...] = for_partners(flag_ref[2], *messages)


def around(count):
    return [(i, (i + 1) % count) for i in range(count)]


def back(count):
    return [((i + 1) % count, i) for i in range(count)]


def exchange_columns(edge):
    count = lax.axis_size("lon")
    from_left = lax.ppermute(edge, "lon", around(count))
    from_right = lax.ppermute(edge, "lon", back(count))
    return from_left, from_right


def exchange_rows(outer, inner):
    count = lax.axis_size("lat")

    def swap(x, first):
        partner = list(range(count))
        for i in range(first, count - 1, 2):
            partner[i], partner[i + 1] = i + 1, i
        return lax.ppermute(x, "lat", list(enumerate(partner)))

    got_outer = swap(outer, 0)
    got_inner = swap(inner, 1)
    return got_outer, got_inner


def on_device(
    satellite_blocks,
    slot_source,
    slot_weight,
    slot_target,
    tile_counts,
    gate_input_weight,
    gate_state_weight,
    gate_bias,
    hidden_init,
    cell_init,
):
    _, tiles, cap, band, block = slot_weight.shape
    channels = satellite_blocks.shape[1]
    units, row_count, column_count = hidden_init.shape
    gates = gate_bias.shape[0]
    slots = tiles * cap
    half = jnp.where(jnp.arange(gates) < 3 * units, 0.5, 1.0)
    in_weight = gate_input_weight * half[:, None].astype(BF)
    state_weight = gate_state_weight * half[:, None].astype(BF)
    bias = (gate_bias * half)[:, None]
    lat = lax.axis_index("lat")
    flags = jnp.stack([lat > 0, lat < lax.axis_size("lat") - 1, lat % 2 == 1]).astype(jnp.int32)

    ring = lax.axis_size("lon")
    height = (cap + 1) * channels
    message = jax.ShapeDtypeStruct((tiles, height, block), BF)
    groups = tiles // ring
    outgoing = pl.pallas_call(
        functools.partial(gather_kernel, ring),
        out_shape=pltpu.HBM(message.shape, BF),
        in_specs=[pl.BlockSpec(memory_space=pl.ANY)] * 3,
        out_specs=pl.BlockSpec(memory_space=pl.ANY),
        scratch_shapes=[
            pltpu.VMEM(satellite_blocks.shape, BF),
            pltpu.VMEM((slots, band, block), BF),
            pltpu.VMEM(message.shape, BF),
            pltpu.SMEM((cap, tiles), jnp.int32),
            pltpu.SemaphoreType.DMA,
            pltpu.SemaphoreType.DMA,
            pltpu.SemaphoreType.DMA((groups,)),
            pltpu.SemaphoreType.DMA((groups,)),
        ],
        compiler_params=pltpu.CompilerParams(vmem_limit_bytes=8 * 2**20),
        name="gather_band",
    )(in_hbm(slot_source[0].T), in_hbm(satellite_blocks), in_hbm(slot_weight.reshape(slots, band, block)))
    incoming = lax.all_to_all(outgoing, ("lat", "lon"), split_axis=0, concat_axis=0, tiled=True)

    ends = jax.ShapeDtypeStruct((5, units, column_count), BF)
    rows, edge, outer, inner = pl.pallas_call(
        prepare_kernel,
        out_shape=(
            jax.ShapeDtypeStruct((row_count, 2 * units, column_count), BF),
            jax.ShapeDtypeStruct((2 * units + tiles, STRIP), BF),
            ends,
            ends,
        ),
        in_specs=scalars(1) + [pl.BlockSpec(memory_space=pl.ANY)] * 4,
        out_specs=tuple(whole(4)),
        scratch_shapes=[
            pltpu.VMEM(hidden_init.shape, BF),
            pltpu.VMEM(cell_init.shape, BF),
            pltpu.VMEM((cap, tiles), jnp.int32),
            pltpu.VMEM((1, tiles), jnp.int32),
            pltpu.SemaphoreType.DMA((4,)),
        ],
        compiler_params=pltpu.CompilerParams(vmem_limit_bytes=8 * 2**20),
        name="prepare",
    )(flags, in_hbm(hidden_init), in_hbm(cell_init), in_hbm(slot_target[0].T), in_hbm(tile_counts))
    from_left, from_right = exchange_columns(edge)
    outer, inner = exchange_rows(outer, inner)
    padded = row_count + 8
    inside = (row_count - 2, gates, column_count)
    parts = inside[0] // PIECE
    state_gates, bias, strip, marks = call(
        state_kernel,
        [
            pltpu.HBM(inside, F32),
            jax.ShapeDtypeStruct((gates, column_count), F32),
            jax.ShapeDtypeStruct((2 * units, 2 * STRIP), BF),
            jax.ShapeDtypeStruct((tiles, LANES), F32),
        ],
        6, 0,
        [
            pltpu.VMEM(inside, F32),
            pltpu.VMEM((padded, 3 * units, column_count), BF),
            pltpu.VMEM((padded, units, LANES), BF),
            pltpu.SemaphoreType.DMA((parts,)),
        ],
        "state_gates", 2 * gates * 9 * units * row_count * column_count,
        (rows, edge, from_left, from_right, state_weight, bias), 16,
        out_specs=[pl.BlockSpec(memory_space=pl.ANY)] + whole(3),
    )
    incoming, state_gates, bias, in_weight = lax.optimization_barrier((incoming, state_gates, bias, in_weight))

    ends = jax.ShapeDtypeStruct((4 * channels + units, column_count), BF)
    forcing, forcing_strip, f_outer, f_inner = call(
        scatter_kernel,
        [
            jax.ShapeDtypeStruct((row_count, channels, column_count), BF),
            jax.ShapeDtypeStruct((channels, 2 * STRIP), BF),
            ends,
            ends,
        ],
        3, 3,
        [pltpu.VMEM((2 * row_count + 1, channels, block), F32)] * 4,
        "scatter_add", slots * channels * block,
        (flags, slot_target[0].T, tile_counts, incoming, marks, strip),
    )
    f_outer, f_inner = exchange_rows(f_outer, f_inner)
    sums, hidden, memory = call(
        early_kernel,
        [
            jax.ShapeDtypeStruct(inside, F32),
            jax.ShapeDtypeStruct((inside[0], units, column_count), BF),
            jax.ShapeDtypeStruct((inside[0], units, column_count), F32),
        ],
        6, 0,
        [
            pltpu.VMEM(inside, F32),
            pltpu.VMEM((padded, 3 * channels, column_count), BF),
            pltpu.VMEM((padded, channels, LANES), BF),
            pltpu.SemaphoreType.DMA((parts,)),
        ],
        "first_step", 2 * gates * 9 * channels * row_count * column_count,
        (in_hbm(state_gates), rows, forcing, forcing_strip, in_weight, bias), 16,
        in_specs=[pl.BlockSpec(memory_space=pl.ANY)] + whole(5),
    )
    return call(
        late_kernel,
        [pltpu.HBM(hidden_init.shape, BF)] * 2,
        14, 1,
        [
            pltpu.VMEM((padded, 3 * channels, column_count), BF),
            pltpu.VMEM((padded, 3 * units, column_count), BF),
            pltpu.VMEM((padded, 3 * units, column_count), BF),
            pltpu.VMEM((padded, 3 * units, column_count), BF),
            pltpu.VMEM((padded, gates, column_count), F32),
            pltpu.VMEM((padded, units, column_count), F32),
            pltpu.VMEM((padded, units, LANES), BF),
            pltpu.VMEM((row_count, units, column_count), BF),
            pltpu.VMEM((row_count, units, column_count), BF),
            pltpu.VMEM(hidden_init.shape, BF),
            pltpu.VMEM(hidden_init.shape, BF),
            pltpu.SemaphoreType.DMA((4,)),
        ],
        "later_steps", 2 * gates * 9 * 2 * units * row_count * column_count,
        (flags, rows, strip, forcing, forcing_strip, outer, inner, f_outer, f_inner,
         in_weight, state_weight, bias, sums, hidden, memory), 24,
        out_specs=[pl.BlockSpec(memory_space=pl.ANY)] * 2,
    )


def solution(mesh):
    placed = (
        P(("lat", "lon"), None, None),
        P(("lat", "lon"), None, None),
        P(("lat", "lon"), None, None, None, None),
        P(("lat", "lon"), None, None),
        P(("lat", "lon"), None),
        P(),
        P(),
        P(),
        P(None, "lat", "lon"),
        P(None, "lat", "lon"),
    )
    return jax.shard_map(
        on_device,
        mesh=mesh,
        in_specs=placed,
        out_specs=(P(None, "lat", "lon"), P(None, "lat", "lon")),
        check_vma=False,
    )
```
